32 devices in a mesh: ka: 4 (over z), mode: 2 (over y), row: 4 (over x, core).
Axes of the slice: x: 2, y: 2, z: 4, core: 2. Of those that a mesh axis runs over, the one named last changes fastest.
Arguments:
- vectors: float32 [4, 8, 16, 16, 8, 512], P('ka', None, 'mode', 'row'), may hold values from -6 to 6
- previous: float32 [4, 8, 16, 16, 8, 512], P('ka', None, 'mode', 'row'), may hold values from -6 to 6
- beta: float32 [8, 8], replicated, may hold values from -2 to 2
- potential: float32 [16, 16, 8, 512], P('mode', 'row'), may hold values from 0.1 to 10
- coriolis_fn: float32 [16, 16, 8, 512], P('mode', 'row'), may hold values from 0.5 to 2
- second_fn: float32 [16, 16, 8, 512], P('mode', 'row'), may hold values from 0.5 to 2
- rot_const: float32 [4], replicated, may hold values from 0.02 to 0.06
- coupling: float32 [2, 4], replicated, may hold values from 0.3 to 1.5
- kin_one: float32 [16, 16], replicated, may hold values from -1.5 to 1.5
- kin_two: float32 [16, 16], replicated, may hold values from -1.5 to 1.5
- kin_three: float32 [8, 8], replicated, may hold values from -2 to 2
- kin_four: float32 [8, 8], replicated, may hold values from -2 to 2
- kin_five: float32 [8, 8], replicated, may hold values from -2 to 2
- kin_six: float32 [8, 8], replicated, may hold values from -2 to 2
- coriolis_derivative: float32 [8, 8], replicated, may hold values from -2 to 2
Outputs:
- basis: float32 [4, 8, 16, 16, 8, 512], P('ka', None, 'mode', 'row')
- alpha: float32 [8, 8], replicated
- lower_factor: float32 [8, 8], replicated
The draws below stay inside these ranges and needn't reach their ends.
All inputs are finite; a program needn't handle non-finite values.
Results may differ from the reference program's by a relative error of at most 0.0003.
Values sent between devices are 32-bit elements; how exact they have to be, the bound alone decides.
No kernel may reach another device: no remote copies, remote signals or barrier semaphores. Data moves between devices by JAX's collectives and lax.ppermute only.
A program may use at most 256 MiB of HBM per device.

```python
import math
import jax
import jax.numpy as jnp
from jax import lax

NV = 8
M1 = 16
M2 = 16
M3 = 8
M4 = 8
M5 = 8
M6 = 8
R = 512
KBLOCKS = 4


def block_levels(key, shape, split, least, high):
    def one(axis_at, blocks):
        heights = jax.random.uniform(jax.random.fold_in(jax.random.fold_in(key, 6), axis_at), (blocks,), jnp.float32, least / len(split), high / len(split))
        return jnp.repeat(jnp.exp(heights), shape[axis_at] // blocks).reshape((-1,) + (1,) * (len(shape) - axis_at - 1))

    factor_of = one(*split[0])
    for cut in split[1:]:
        factor_of = factor_of * one(*cut)
    return factor_of


def centred(key, extent, width, reach, shards=(), kind=jnp.bfloat16):
    array = jax.random.normal(key, extent, jnp.float32) * width
    if len(shards) > 0:
        array = block_levels(key, extent, shards, -0.22, 0.18) * array
    return jnp.clip(array, min=-reach, max=reach).astype(kind)


def setup_inputs(seed: int = 0) -> dict:
    splits = jax.random.split(jax.random.key(seed), 16)
    return {
        "vectors": centred(splits[0], (KBLOCKS, NV, M1, M2, M3, R), 1.0, 6.0, ((0, 4), (2, 2), (3, 4)), jnp.float32),
        "previous": centred(splits[1], (KBLOCKS, NV, M1, M2, M3, R), 1.0, 6.0, ((0, 4), (2, 2), (3, 4)), jnp.float32),
        "beta": centred(splits[2], (NV, NV), NV ** -0.5, 2.0, (), jnp.float32),
        "potential": jnp.clip(jnp.exp(math.log(10.0) - 4.6051702 * jax.random.uniform(splits[3], (M1, M2, M3, R), jnp.float32) ** block_levels(splits[3], (M1, M2, M3, R), ((0, 2), (1, 4)), -0.2, 0.2)), 0.1, 10.0),
        "coriolis_fn": jnp.clip(0.5 + 1.5 * jax.random.uniform(splits[4], (M1, M2, M3, R), jnp.float32) ** block_levels(splits[4], (M1, M2, M3, R), ((0, 2), (1, 4)), -0.2, 0.2), 0.5, 2.0),
        "second_fn": jnp.clip(0.5 + 1.5 * jax.random.uniform(splits[5], (M1, M2, M3, R), jnp.float32) ** block_levels(splits[5], (M1, M2, M3, R), ((0, 2), (1, 4)), -0.2, 0.2), 0.5, 2.0),
        "rot_const": jnp.clip(jnp.exp(jax.random.uniform(splits[6], (KBLOCKS,), jnp.float32, math.log(0.02), math.log(0.06))), 0.02, 0.06),
        "coupling": jnp.clip(jnp.exp(jax.random.uniform(splits[7], (2, KBLOCKS), jnp.float32, math.log(0.3), math.log(1.5))), 0.3, 1.5),
        "kin_one": centred(splits[8], (M1, M1), M1 ** -0.5, 1.5, (), jnp.float32),
        "kin_two": centred(splits[9], (M2, M2), M2 ** -0.5, 1.5, (), jnp.float32),
        "kin_three": centred(splits[10], (M3, M3), M3 ** -0.5, 2.0, (), jnp.float32),
        "kin_four": centred(splits[11], (M4, M4), M4 ** -0.5, 2.0, (), jnp.float32),
        "kin_five": centred(splits[12], (M5, M5), M5 ** -0.5, 2.0, (), jnp.float32),
        "kin_six": centred(splits[13], (M6, M6), M6 ** -0.5, 2.0, (), jnp.float32),
        "coriolis_derivative": centred(splits[14], (M6, M6), M6 ** -0.5, 2.0, (), jnp.float32),
    }


precise_mode = lax.Precision.HIGHEST

def symmetric(matrix):
    return 0.5 * (matrix + matrix.T)

def along(matrix, field, axis):
    moved = jnp.tensordot(field, matrix, axes=((axis,), (1,)), precision=precise_mode)
    return jnp.moveaxis(moved, -1, axis)

def reference(vectors, previous, beta, potential, coriolis_fn, second_fn, rot_const, coupling, kin_one, kin_two, kin_three, kin_four, kin_five, kin_six, coriolis_derivative):
    nblocks = vectors.shape[0]
    shape_seven = (NV, M1, M2, M3, M4, M5, M6)
    matrices = [symmetric(kin_one), symmetric(kin_two), symmetric(kin_three), symmetric(kin_four), symmetric(kin_five), symmetric(kin_six)]
    twist = 0.5 * (coriolis_derivative - coriolis_derivative.T)
    grid_six = (M1, M2, M3, M4, M5, M6)
    energy = potential.reshape(grid_six)
    twist_fn = coriolis_fn.reshape(grid_six)
    skip_fn = second_fn.reshape(grid_six)
    near_coef = coupling[0]
    far_coef = coupling[1]

    def pick(index):
        inside = (index >= 0) & (index < nblocks)
        safe = jnp.clip(index, 0, nblocks - 1).astype(jnp.int32)
        piece = lax.dynamic_index_in_dim(vectors, safe, 0, keepdims=False).reshape(shape_seven)
        return jnp.where(inside, piece, jnp.zeros_like(piece))

    def block(index):
        current = lax.dynamic_index_in_dim(vectors, index, 0, keepdims=False).reshape(shape_seven)
        result = along(matrices[0], current, 1)
        for number in range(1, 6):
            result = result + along(matrices[number], current, number + 1)
        level = (index - nblocks // 2).astype(rot_const.dtype)
        result = result + (energy + rot_const[index] * level * level) * current
        below_one = jnp.maximum(index - 1, 0)
        below_two = jnp.maximum(index - 2, 0)
        result = result + near_coef[index] * twist_fn * along(twist, pick(index + 1), 6)
        result = result + near_coef[below_one] * along(twist.T, twist_fn * pick(index - 1), 6)
        result = result + skip_fn * (far_coef[index] * pick(index + 2) + far_coef[below_two] * pick(index - 2))
        older = lax.dynamic_index_in_dim(previous, index, 0, keepdims=False).reshape(shape_seven)
        result = result - jnp.einsum('ij,jabcdef->iabcdef', beta, older, precision=precise_mode)
        return result.reshape(NV, -1)
    work = lax.map(block, jnp.arange(nblocks, dtype=jnp.int32))
    count = float(nblocks * work.shape[2])
    flat = vectors.reshape(nblocks, NV, -1)

    def inner(left, right):
        return jnp.einsum('kjc,kic->ji', left, right, precision=precise_mode) / count
    first = inner(flat, work)
    work = work - jnp.einsum('kjc,ji->kic', flat, first, precision=precise_mode)
    second = inner(flat, work)
    work = work - jnp.einsum('kjc,ji->kic', flat, second, precision=precise_mode)
    gram = inner(work, work)
    lower = jnp.linalg.cholesky(gram)
    inverse = jax.scipy.linalg.solve_triangular(lower, jnp.eye(NV, dtype=gram.dtype), lower=True)
    basis = jnp.einsum('ij,kjc->kic', inverse, work, precision=precise_mode)
    return (basis.reshape(vectors.shape), first + second, lower)
```

```python
import functools

import jax
import jax.numpy as jnp
from jax import lax
from jax.experimental import pallas as pl
from jax.experimental.pallas import tpu as pltpu
from jax.sharding import PartitionSpec as P

precise_mode = lax.Precision.HIGHEST
ALL_AXES = ("ka", "mode", "row")
VMEM_BYTES = 48 * 1024 * 1024
LANES = 128
SUBLANES = 8


def precise_dot(left, right):
    return jnp.dot(left, right, precision=precise_mode, preferred_element_type=jnp.float32)


def symmetric(matrix):
    return 0.5 * (matrix + matrix.T)


def whole_spec(shape):
    return pl.BlockSpec(shape, lambda *_: (0,) * len(shape))


def hop(value, axis, by):
    peers = lax.axis_size(axis)
    pairs = [(i, i + by) for i in range(peers) if 0 <= i + by < peers]
    return lax.ppermute(value, axis, pairs)


def ring_blocks(value, axis, stride):
    peers = lax.axis_size(axis)
    members = peers // stride
    found = []
    for sign in (1, -1):
        count = (members - 1 + (sign == 1)) // 2
        travelling = value
        for step in range(1, count + 1):
            travelling = lax.ppermute(
                travelling, axis, [(i, (i + sign * stride) % peers) for i in range(peers)]
            )
            found.append((-sign * step * stride, travelling))
    return found


def gathered_blocks(value, axis, paired):
    peers = lax.axis_size(axis)
    me = lax.axis_index(axis)
    if not paired or peers % 2:
        return [((me + by) % peers, block) for by, block in ring_blocks(value, axis, 1)]
    held = [(me, value)]
    held += [((me + by) % peers, block) for by, block in ring_blocks(value, axis, 2)]
    swap = [(i, i ^ 1) for i in range(peers)]
    swapped = [(owner ^ 1, lax.ppermute(block, axis, swap)) for owner, block in held]
    return held[1:] + swapped


def vector_groups(nvec):
    return [tuple(range(at, min(at + 4, nvec))) for at in range(0, nvec, 4)]


def tiles(rows, width):
    return [
        (slice(r, r + SUBLANES), slice(c, c + LANES))
        for r in range(0, rows, SUBLANES)
        for c in range(0, width, LANES)
    ]


def packed_columns(sums, nvec, offset, lane):
    packed = jnp.zeros((nvec, LANES), jnp.float32)
    for j in range(nvec):
        stacked = jnp.stack([sums(i, j) for i in range(nvec)])
        column = jnp.sum(jnp.sum(stacked, axis=1), axis=1, keepdims=True)
        packed = packed + jnp.where(lane == offset + j, column, 0.0)
    return packed


def vector_products_kernel(nvec, vec_ref, out_ref, sums):
    step = pl.program_id(0)

    @pl.when(step == 0)
    def _():
        sums[...] = jnp.zeros_like(sums)

    groups = vector_groups(nvec)
    for at, left in enumerate(groups):
        for right in groups[at:]:
            pairs = [(i, j) for i in left for j in right if i <= j]
            totals = {pair: sums[pair[0] * nvec + pair[1]] for pair in pairs}
            for place in tiles(*vec_ref.shape[1:]):
                values = {i: vec_ref[(i, *place)] for i in set(left + right)}
                for i, j in pairs:
                    totals[i, j] = totals[i, j] + values[i] * values[j]
            for i, j in pairs:
                sums[i * nvec + j] = totals[i, j]

    @pl.when(step == pl.num_programs(0) - 1)
    def _():
        lane = lax.broadcasted_iota(jnp.int32, (nvec, LANES), 1)
        out_ref[...] = packed_columns(
            lambda i, j: sums[min(i, j) * nvec + max(i, j)], nvec, 2 * nvec, lane
        )


def vector_products(vec, block_rows):
    nvec, rows, width = vec.shape
    return pl.pallas_call(
        functools.partial(vector_products_kernel, nvec),
        grid=(rows // block_rows,),
        in_specs=[pl.BlockSpec((nvec, block_rows, width), lambda s: (0, s, 0))],
        out_specs=whole_spec((nvec, LANES)),
        out_shape=jax.ShapeDtypeStruct((nvec, LANES), jnp.float32),
        scratch_shapes=[pltpu.VMEM((nvec * nvec, SUBLANES, LANES), jnp.float32)],
        compiler_params=pltpu.CompilerParams(vmem_limit_bytes=VMEM_BYTES),
        cost_estimate=pl.CostEstimate(
            flops=nvec * (nvec + 1) * rows * width, bytes_accessed=4 * vec.size, transcendentals=0
        ),
        name="vector_products",
    )(vec)


def interior_kernel(nvec, far_count, piece_count, *refs):
    refs = list(refs)
    beta_ref, cur_ref, old_ref, pot_ref, cor_ref, left_ref, tail_ref, up_ref, down_ref = refs[:9]
    far_refs = refs[9 : 9 + far_count]
    below_refs = refs[9 + far_count : 9 + far_count + piece_count]
    above_refs = refs[9 + far_count + piece_count : 9 + far_count + 2 * piece_count]
    out_ref = refs[-1]
    me = pl.program_id(0)
    current = cur_ref[0]
    total = pot_ref[...] * current
    for j in range(nvec):
        total = total - beta_ref[me, j] * old_ref[j]
    total = total + precise_dot(current, tail_ref[...])
    total = total + precise_dot(left_ref[0], current)
    for number, far_ref in enumerate(far_refs):
        total = total + precise_dot(left_ref[1 + number], far_ref[0])
    out_ref[0] = total
    piece_rows = below_refs[0].shape[1]
    span = up_ref.shape[0]
    for number in range(piece_count):
        place = slice(number * piece_rows, (number + 1) * piece_rows)
        for at in range(0, cur_ref.shape[2], span):
            part = slice(at, at + span)
            twist_fn = cor_ref[place, part]
            out_ref[0, place, part] += twist_fn * precise_dot(
                above_refs[number][0, :, part], up_ref[...]
            ) + precise_dot(twist_fn * below_refs[number][0, :, part], down_ref[...])


def interior(beta, cur, old, pot, cor, left, tail, up, down, far, below, above):
    nvec, rows, width = cur.shape
    piece_rows = below[0].shape[1]
    one = pl.BlockSpec((1, rows, width), lambda i: (i, 0, 0))
    piece = pl.BlockSpec((1, piece_rows, width), lambda i: (i, 0, 0))
    span = up.shape[0]
    flops = 2 * cur.size * (rows * left.shape[0] + width + 2 * span)
    return pl.pallas_call(
        functools.partial(interior_kernel, nvec, len(far), len(below)),
        grid=(nvec,),
        in_specs=[
            pl.BlockSpec(memory_space=pltpu.SMEM),
            one,
            whole_spec(old.shape),
            whole_spec(pot.shape),
            whole_spec(cor.shape),
            whole_spec(left.shape),
            whole_spec(tail.shape),
            whole_spec(up.shape),
            whole_spec(down.shape),
        ]
        + [one] * len(far)
        + [piece] * (len(below) + len(above)),
        out_specs=one,
        out_shape=jax.ShapeDtypeStruct(cur.shape, jnp.float32),
        compiler_params=pltpu.CompilerParams(vmem_limit_bytes=VMEM_BYTES),
        cost_estimate=pl.CostEstimate(
            flops=6 * flops, bytes_accessed=4 * cur.size * (5 + len(far)), transcendentals=0
        ),
        name="interior",
    )(beta, cur, old, pot, cor, left, tail, up, down, *far, *below, *above)


def far_terms_kernel(
    nvec, coef_ref, work_ref, above_ref, below_ref, fn_ref, vec_ref, before_ref, out_ref, sum_ref, sums
):
    step = pl.program_id(0)

    @pl.when(step == 0)
    def _():
        sums[...] = jnp.zeros_like(sums)

    skip_fn = fn_ref[...]
    for i in range(nvec):
        out_ref[i] = work_ref[i] + skip_fn * (
            coef_ref[0] * above_ref[i] + coef_ref[1] * below_ref[i]
        )
    groups = vector_groups(nvec)
    for ours in groups:
        for other in groups:
            cross = [(j, i) for j in other for i in ours]
            square = [(i, j) for i in ours for j in other if i <= j]
            cross_totals = {p: sums[0, p[0] * nvec + p[1]] for p in cross}
            square_totals = {p: sums[1, p[0] * nvec + p[1]] for p in square}
            for place in tiles(*out_ref.shape[1:]):
                works = {i: out_ref[(i, *place)] for i in ours}
                if square:
                    works.update({j: out_ref[(j, *place)] for j in other if j not in works})
                vecs = {j: vec_ref[(j, *place)] for j in other}
                for j, i in cross:
                    cross_totals[j, i] = cross_totals[j, i] + vecs[j] * works[i]
                for i, j in square:
                    square_totals[i, j] = square_totals[i, j] + works[i] * works[j]
            for j, i in cross:
                sums[0, j * nvec + i] = cross_totals[j, i]
            for i, j in square:
                sums[1, i * nvec + j] = square_totals[i, j]

    @pl.when(step == pl.num_programs(0) - 1)
    def _():
        lane = lax.broadcasted_iota(jnp.int32, (nvec, LANES), 1)
        packed = before_ref[...]
        packed = packed + packed_columns(lambda i, j: sums[0, j * nvec + i], nvec, 0, lane)
        packed = packed + packed_columns(
            lambda i, j: sums[1, min(i, j) * nvec + max(i, j)], nvec, nvec, lane
        )
        sum_ref[...] = jnp.broadcast_to(packed[None], sum_ref.shape)


def far_terms(coef, work, above, below, skip_fn, vec, before, start, block_rows, copies):
    nvec, rows, width = work.shape
    piece_rows = above.shape[1]
    first = start // block_rows
    whole = pl.BlockSpec((nvec, block_rows, width), lambda s: (0, s + first, 0))
    piece = pl.BlockSpec((nvec, block_rows, width), lambda s: (0, s, 0))
    return pl.pallas_call(
        functools.partial(far_terms_kernel, nvec),
        grid=(piece_rows // block_rows,),
        in_specs=[
            pl.BlockSpec(memory_space=pltpu.SMEM),
            whole,
            piece,
            piece,
            pl.BlockSpec((block_rows, width), lambda s: (s + first, 0)),
            whole,
            whole_spec((nvec, LANES)),
        ],
        out_specs=[whole, whole_spec((copies, nvec, LANES))],
        out_shape=[
            jax.ShapeDtypeStruct(work.shape, jnp.float32),
            jax.ShapeDtypeStruct((copies, nvec, LANES), jnp.float32),
        ],
        scratch_shapes=[pltpu.VMEM((2, nvec * nvec, SUBLANES, LANES), jnp.float32)],
        input_output_aliases={1: 0},
        compiler_params=pltpu.CompilerParams(vmem_limit_bytes=VMEM_BYTES),
        cost_estimate=pl.CostEstimate(
            flops=3 * nvec * nvec * piece_rows * width,
            bytes_accessed=20 * above.size,
            transcendentals=0,
        ),
        name="far_terms",
    )(coef, work, above, below, skip_fn, vec, before)


def small_algebra(nvec, count, packed):
    packed = packed * (1.0 / count)
    turned = packed.T
    cross = turned[0:nvec, :]
    cross_turned = packed[:, 0:nvec]
    work_gram = packed[:, nvec : 2 * nvec]
    vec_gram = packed[:, 2 * nvec : 3 * nvec]
    total = 2.0 * cross - precise_dot(vec_gram, cross)
    total_turned = 2.0 * cross_turned - precise_dot(cross_turned, vec_gram)
    gram = work_gram - precise_dot(total_turned, cross) - precise_dot(cross_turned, total)
    gram = gram + precise_dot(total_turned, precise_dot(vec_gram, total))
    gram = 0.5 * (gram + gram.T)
    row = lax.broadcasted_iota(jnp.int32, (nvec, nvec), 0)
    column = lax.broadcasted_iota(jnp.int32, (nvec, nvec), 1)
    inverse = jnp.where(row == column, 1.0, 0.0)
    lower = jnp.zeros((nvec, nvec), jnp.float32)
    for at in range(nvec):
        pivot = gram[at : at + 1, at : at + 1]
        scale = lax.rsqrt(pivot)
        scale = scale * (1.5 - 0.5 * pivot * scale * scale)
        scaled = gram[:, at : at + 1] * scale
        lower = jnp.where((column == at) & (row >= at), scaled, lower)
        pivot_row = inverse[at : at + 1, :] * scale
        factor = jnp.where(row > at, scaled, 0.0)
        inverse = jnp.where(row == at, pivot_row, inverse - factor * pivot_row)
        gram = gram - factor * (gram[at : at + 1, :] * scale)
    return total, lower, inverse, -precise_dot(inverse, total_turned)


def basis_kernel(nvec, count, sum_ref, work_ref, vec_ref, out_ref, alpha_ref, lower_ref, coefs):
    @pl.when(pl.program_id(0) == 0)
    def _():
        packed = sum_ref[0]
        for other in range(1, sum_ref.shape[0]):
            packed = packed + sum_ref[other]
        total, lower, inverse, mixing = small_algebra(nvec, count, packed)
        alpha_ref[...] = total
        lower_ref[...] = lower
        for number, matrix in enumerate((inverse, mixing)):
            for i in range(nvec):
                for j in range(nvec):
                    coefs[number, i * nvec + j] = jnp.broadcast_to(
                        matrix[i : i + 1, j : j + 1], (SUBLANES, LANES)
                    )

    places = tiles(*work_ref.shape[1:])
    for at in range(0, len(places), 2):
        group = places[at : at + 2]
        works = [[work_ref[(j, *place)] for place in group] for j in range(nvec)]
        vecs = [[vec_ref[(j, *place)] for place in group] for j in range(nvec)]
        for i in range(nvec):
            totals = [None] * len(group)
            for j in range(nvec):
                mixing = coefs[1, i * nvec + j]
                for number in range(len(group)):
                    term = mixing * vecs[j][number]
                    totals[number] = term if j == 0 else totals[number] + term
            for j in range(i + 1):
                inverse = coefs[0, i * nvec + j]
                for number in range(len(group)):
                    totals[number] = totals[number] + inverse * works[j][number]
            for number, place in enumerate(group):
                out_ref[(i, *place)] = totals[number]


def basis_of(count, sums, work, vec, block_rows):
    nvec, rows, width = work.shape
    block = pl.BlockSpec((nvec, block_rows, width), lambda s: (0, s, 0))
    small = jax.ShapeDtypeStruct((nvec, nvec), jnp.float32)
    return pl.pallas_call(
        functools.partial(basis_kernel, nvec, count),
        grid=(rows // block_rows,),
        in_specs=[whole_spec(sums.shape), block, block],
        out_specs=[block, whole_spec(small.shape), whole_spec(small.shape)],
        out_shape=[jax.ShapeDtypeStruct(work.shape, jnp.float32), small, small],
        scratch_shapes=[pltpu.VMEM((2, nvec * nvec, SUBLANES, LANES), jnp.float32)],
        compiler_params=pltpu.CompilerParams(vmem_limit_bytes=VMEM_BYTES),
        cost_estimate=pl.CostEstimate(
            flops=4 * nvec * work.size, bytes_accessed=12 * work.size, transcendentals=0
        ),
        name="basis",
    )(sums, work, vec)


def block_of(matrix, rows_at, columns_at, size):
    return lax.dynamic_slice(matrix, (rows_at * size, columns_at * size), (size, size))


def shards(
    vectors,
    previous,
    beta,
    potential,
    coriolis_fn,
    second_fn,
    rot_const,
    coupling,
    kin_one,
    kin_two,
    kin_three,
    kin_four,
    kin_five,
    kin_six,
    coriolis_derivative,
):
    _, nvec, points_one, points_two, points_three, width = vectors.shape
    rows = points_one * points_two * points_three
    devices = lax.axis_size(ALL_AXES)
    block_index = lax.axis_index("ka")
    nblocks = lax.axis_size("ka")
    current = vectors.reshape(nvec, rows, width)
    older = previous.reshape(nvec, rows, width)
    pieces = 4
    piece_rows = rows // pieces
    block_rows = min(32, piece_rows)

    below_one, above_one, below_two, above_two = [], [], [], []
    for number in range(pieces):
        piece = current[:, number * piece_rows : (number + 1) * piece_rows]
        below_one.append(hop(piece, "ka", 1))
        above_one.append(hop(piece, "ka", -1))
    for number in range(pieces):
        below_two.append(hop(below_one[number], "ka", 1))
        above_two.append(hop(above_one[number], "ka", -1))
    mode_blocks = gathered_blocks(current, "mode", False)
    row_blocks = gathered_blocks(current, "row", True)

    first_mat = symmetric(kin_one)
    second_mat = symmetric(kin_two)
    third_mat = symmetric(kin_three)
    mode_at = lax.axis_index("mode")
    row_at = lax.axis_index("row")
    eye_one = jnp.eye(points_one, dtype=jnp.float32)
    eye_two = jnp.eye(points_two, dtype=jnp.float32)
    eye_three = jnp.eye(points_three, dtype=jnp.float32)

    def three(one, two, third):
        return jnp.kron(jnp.kron(one, two), third)

    left = three(block_of(first_mat, mode_at, mode_at, points_one), eye_two, eye_three)
    left = left + three(eye_one, block_of(second_mat, row_at, row_at, points_two), eye_three)
    left = left + three(eye_one, eye_two, third_mat)
    lefts = [left]
    for owner, _ in mode_blocks:
        lefts.append(three(block_of(first_mat, mode_at, owner, points_one), eye_two, eye_three))
    for owner, _ in row_blocks:
        lefts.append(three(eye_one, block_of(second_mat, row_at, owner, points_two), eye_three))
    left = jnp.stack(lefts)

    eye_four = jnp.eye(kin_four.shape[0], dtype=jnp.float32)
    eye_five = jnp.eye(kin_five.shape[0], dtype=jnp.float32)
    eye_six = jnp.eye(kin_six.shape[0], dtype=jnp.float32)
    tail = three(symmetric(kin_four), eye_five, eye_six)
    tail = tail + three(eye_four, symmetric(kin_five), eye_six)
    tail = tail + three(eye_four, eye_five, symmetric(kin_six))
    twist = 0.5 * (coriolis_derivative - coriolis_derivative.T)
    span = next((s for s in (256, 128) if width % s == 0 and s % twist.shape[0] == 0), width)
    eye_span = jnp.eye(span // twist.shape[0], dtype=jnp.float32)
    lower_one = jnp.maximum(block_index - 1, 0)
    lower_two = jnp.maximum(block_index - 2, 0)
    near_coef = coupling[0]
    far_coef = coupling[1]
    from_above = near_coef[block_index] * jnp.kron(eye_span, twist.T)
    from_below = near_coef[lower_one] * jnp.kron(eye_span, twist)
    level = (block_index - nblocks // 2).astype(jnp.float32)
    diagonal = (potential + rot_const[block_index] * level * level).reshape(rows, width)
    far_pair = jnp.stack([far_coef[block_index], far_coef[lower_two]])
    skip_fn = second_fn.reshape(rows, width)

    sums = vector_products(current, block_rows)
    work = interior(
        beta,
        current,
        older,
        diagonal,
        coriolis_fn.reshape(rows, width),
        left,
        tail,
        from_above,
        from_below,
        [block for _, block in mode_blocks + row_blocks],
        below_one,
        above_one,
    )
    for number in range(pieces):
        last = number == pieces - 1
        work, copied = far_terms(
            far_pair,
            work,
            above_two[number],
            below_two[number],
            skip_fn,
            current,
            sums,
            number * piece_rows,
            block_rows,
            devices if last else 1,
        )
        sums = copied[0]
    every_sum = lax.all_to_all(copied, ALL_AXES, split_axis=0, concat_axis=0, tiled=True)
    count = float(devices * rows * width)
    basis, alpha, lower = basis_of(count, every_sum, work, current, block_rows)
    return (basis.reshape(vectors.shape), alpha, lower)


def solution(mesh):
    return jax.shard_map(
        shards,
        mesh=mesh,
        in_specs=(
            P("ka", None, "mode", "row", None, None),
            P("ka", None, "mode", "row", None, None),
            P(),
            P("mode", "row", None, None),
            P("mode", "row", None, None),
            P("mode", "row", None, None),
            P(),
            P(),
            P(),
            P(),
            P(),
            P(),
            P(),
            P(),
            P(),
        ),
        out_specs=(P("ka", None, "mode", "row", None, None), P(), P()),
        check_vma=False,
    )
```

```python
import functools

import jax
import jax.numpy as jnp
from jax import lax
from jax.experimental import pallas as pl
from jax.experimental.pallas import tpu as pltpu
from jax.sharding import PartitionSpec as P

precise_mode = lax.Precision.HIGHEST
ALL_AXES = ("ka", "mode", "row")
VMEM_BYTES = 48 * 1024 * 1024
LANES = 128
SUBLANES = 8


def precise_dot(left, right):
    return jnp.dot(left, right, precision=precise_mode, preferred_element_type=jnp.float32)


def whole_spec(shape):
    return pl.BlockSpec(shape, lambda *_: (0,) * len(shape))


def hop(value, axis, by):
    peers = lax.axis_size(axis)
    pairs = [(i, i + by) for i in range(peers) if 0 <= i + by < peers]
    return lax.ppermute(value, axis, pairs)


def ring_blocks(value, axis):
    peers = lax.axis_size(axis)
    found = []
    for sign in (1, -1):
        travelling = value
        for step in range(1, (peers - 1 + (sign == 1)) // 2 + 1):
            travelling = lax.ppermute(
                travelling, axis, [(i, (i + sign) % peers) for i in range(peers)]
            )
            found.append((-sign * step, travelling))
    return found


def vector_groups(nvec):
    return [tuple(range(at, min(at + 4, nvec))) for at in range(0, nvec, 4)]


def tiles(rows, width):
    return [
        (slice(r, r + SUBLANES), slice(c, c + LANES))
        for r in range(0, rows, SUBLANES)
        for c in range(0, width, LANES)
    ]


def packed_columns(sums, nvec, offset, lane):
    packed = jnp.zeros((nvec, LANES), jnp.float32)
    for j in range(nvec):
        stacked = jnp.stack([sums(i, j) for i in range(nvec)])
        column = jnp.sum(jnp.sum(stacked, axis=1), axis=1, keepdims=True)
        packed = packed + jnp.where(lane == offset + j, column, 0.0)
    return packed


def vector_products_kernel(nvec, vec_ref, out_ref, sums):
    step = pl.program_id(0)

    @pl.when(step == 0)
    def _():
        sums[...] = jnp.zeros_like(sums)

    groups = vector_groups(nvec)
    for at, left in enumerate(groups):
        for right in groups[at:]:
            pairs = [(i, j) for i in left for j in right if i <= j]
            totals = {pair: sums[pair[0] * nvec + pair[1]] for pair in pairs}
            for place in tiles(*vec_ref.shape[1:]):
                values = {i: vec_ref[(i, *place)] for i in set(left + right)}
                for i, j in pairs:
                    totals[i, j] = totals[i, j] + values[i] * values[j]
            for i, j in pairs:
                sums[i * nvec + j] = totals[i, j]

    @pl.when(step == pl.num_programs(0) - 1)
    def _():
        lane = lax.broadcasted_iota(jnp.int32, (nvec, LANES), 1)
        out_ref[...] = packed_columns(
            lambda i, j: sums[min(i, j) * nvec + max(i, j)], nvec, 2 * nvec, lane
        )


def vector_products(vec, block_rows):
    nvec, rows, width = vec.shape
    return pl.pallas_call(
        functools.partial(vector_products_kernel, nvec),
        grid=(rows // block_rows,),
        in_specs=[pl.BlockSpec((nvec, block_rows, width), lambda s: (0, s, 0))],
        out_specs=whole_spec((nvec, LANES)),
        out_shape=jax.ShapeDtypeStruct((nvec, LANES), jnp.float32),
        scratch_shapes=[pltpu.VMEM((nvec * nvec, SUBLANES, LANES), jnp.float32)],
        compiler_params=pltpu.CompilerParams(vmem_limit_bytes=VMEM_BYTES),
        cost_estimate=pl.CostEstimate(
            flops=nvec * (nvec + 1) * rows * width, bytes_accessed=4 * vec.size, transcendentals=0
        ),
        name="vector_products",
    )(vec)


def kron_term(matrix, size, stride, extent, row_offset=0, column_offset=0, sign=1.0):
    points = matrix.shape[0]

    def digits(shape, axis):
        index = lax.broadcasted_iota(jnp.int32, shape, axis)
        return index, lax.rem(lax.div(index, stride), size)

    def picks(offset):
        _, digit = digits((extent, points), 0)
        point = lax.broadcasted_iota(jnp.int32, (extent, points), 1)
        return jnp.where(digit + offset == point, 1.0, 0.0)

    def transposed_dot(one, two):
        return lax.dot_general(
            one, two, (((1,), (1,)), ((), ())), precision=precise_mode,
            preferred_element_type=jnp.float32,
        )

    picked = picks(row_offset)
    picked = 0.5 * (precise_dot(picked, matrix) + sign * transposed_dot(picked, matrix))
    spread = transposed_dot(picked, picks(column_offset))
    row, row_digit = digits((extent, extent), 0)
    column, column_digit = digits((extent, extent), 1)
    same = (row - row_digit * stride) == (column - column_digit * stride)
    return jnp.where(same, spread, 0.0)


def operators_kernel(
    points, at_ref, coupling_ref, one_ref, two_ref, three_ref, four_ref, five_ref, six_ref, der_ref,
    left_ref, row_ref, tail_ref, up_ref, down_ref,
):
    points_one, points_two, points_three = points
    rows = points_one * points_two * points_three
    stride = points_two * points_three
    mine = at_ref[1] * points_one
    left_ref[0] = kron_term(one_ref[...], points_one, stride, rows, mine, mine) + kron_term(
        three_ref[...], points_three, 1, rows
    )
    for number in range(1, left_ref.shape[0]):
        owner = at_ref[1 + number] * points_one
        left_ref[number] = kron_term(one_ref[...], points_one, stride, rows, mine, owner)
    row_ref[...] = kron_term(two_ref[...], two_ref.shape[0], points_three, row_ref.shape[0])
    width = tail_ref.shape[0]
    fives, sixes = five_ref.shape[0], six_ref.shape[0]
    tail_ref[...] = (
        kron_term(four_ref[...], four_ref.shape[0], fives * sixes, width)
        + kron_term(five_ref[...], fives, sixes, width)
        + kron_term(six_ref[...], sixes, 1, width)
    )
    twist = kron_term(der_ref[...], sixes, 1, down_ref.shape[0], sign=-1.0)
    block = at_ref[0]
    up_ref[...] = -coupling_ref[0, block] * twist
    down_ref[...] = coupling_ref[0, jnp.maximum(block - 1, 0)] * twist


def operators(points, mode_count, row_extent, width, span, at, coupling, matrices):
    rows = points[0] * points[1] * points[2]
    shapes = [(mode_count, rows, rows), (row_extent, row_extent), (width, width), (span, span), (span, span)]
    smem = pl.BlockSpec(memory_space=pltpu.SMEM)
    return pl.pallas_call(
        functools.partial(operators_kernel, points),
        in_specs=[smem, smem] + [pl.BlockSpec(memory_space=pltpu.VMEM)] * len(matrices),
        out_specs=[pl.BlockSpec(memory_space=pltpu.VMEM)] * len(shapes),
        out_shape=[jax.ShapeDtypeStruct(shape, jnp.float32) for shape in shapes],
        compiler_params=pltpu.CompilerParams(vmem_limit_bytes=VMEM_BYTES),
        cost_estimate=pl.CostEstimate(
            flops=500_000_000, bytes_accessed=4_000_000, transcendentals=0
        ),
        name="operators",
    )(at, coupling, *matrices)


def local_kernel(nvec, nblocks, at_ref, rot_ref, beta_ref, cur_ref, old_ref, pot_ref, left_ref, tail_ref, out_ref):
    me = pl.program_id(0)
    block = at_ref[0]
    level = (block - nblocks // 2).astype(jnp.float32)
    current = cur_ref[0]
    total = (pot_ref[...] + rot_ref[block] * level * level) * current
    for j in range(nvec):
        total = total - beta_ref[me, j] * old_ref[j]
    total = total + precise_dot(current, tail_ref[...])
    out_ref[0] = total + precise_dot(left_ref[0], current)


def local_terms(nblocks, at, rot_const, beta, cur, old, pot, left, tail):
    nvec, rows, width = cur.shape
    one = pl.BlockSpec((1, rows, width), lambda i: (i, 0, 0))
    smem = pl.BlockSpec(memory_space=pltpu.SMEM)
    return pl.pallas_call(
        functools.partial(local_kernel, nvec, nblocks),
        grid=(nvec,),
        in_specs=[
            smem,
            smem,
            smem,
            one,
            whole_spec(old.shape),
            whole_spec(pot.shape),
            pl.BlockSpec((1, rows, rows), lambda i: (0, 0, 0)),
            whole_spec(tail.shape),
        ],
        out_specs=one,
        out_shape=jax.ShapeDtypeStruct(cur.shape, jnp.float32),
        compiler_params=pltpu.CompilerParams(vmem_limit_bytes=VMEM_BYTES),
        cost_estimate=pl.CostEstimate(
            flops=12 * cur.size * (rows + width), bytes_accessed=12 * cur.size, transcendentals=0
        ),
        name="local_terms",
    )(at, rot_const, beta, cur, old, pot, left, tail)


def row_kinetic_kernel(peers, held, span, in_ref, mat_ref, out_ref):
    for start in range(0, in_ref.shape[2], span):
        place = slice(start, start + span)
        field = jnp.concatenate([in_ref[peer, 0, place] for peer in range(peers)], axis=0)
        field = precise_dot(mat_ref[...], field)
        for peer in range(peers):
            out_ref[peer, 0, place] = field[peer * span : (peer + 1) * span]


def row_kinetic(field, matrix, peers, span):
    nvec, rows, width = field.shape
    held = nvec // peers
    block = pl.BlockSpec((peers, 1, rows, width), lambda q: (0, q, 0, 0))
    out = pl.pallas_call(
        functools.partial(row_kinetic_kernel, peers, held, span),
        grid=(held,),
        in_specs=[block, whole_spec(matrix.shape)],
        out_specs=block,
        out_shape=jax.ShapeDtypeStruct((peers, held, rows, width), jnp.float32),
        compiler_params=pltpu.CompilerParams(vmem_limit_bytes=VMEM_BYTES),
        cost_estimate=pl.CostEstimate(
            flops=12 * field.size * matrix.shape[0], bytes_accessed=8 * field.size, transcendentals=0
        ),
        name="row_kinetic",
    )(field.reshape(peers, held, rows, width), matrix)
    return out.reshape(field.shape)


def join_kernel(mode_count, starts, *refs):
    work_ref, row_ref, cor_ref, left_ref, up_ref, down_ref = refs[:6]
    mode_refs = refs[6 : 6 + mode_count]
    below_refs = refs[6 + mode_count : 6 + mode_count + len(starts)]
    above_refs = refs[6 + mode_count + len(starts) : 6 + mode_count + 2 * len(starts)]
    out_ref = refs[-1]
    total = work_ref[0] + row_ref[0]
    for number, mode_ref in enumerate(mode_refs):
        total = total + precise_dot(left_ref[1 + number], mode_ref[0])
    out_ref[0] = total
    span = up_ref.shape[0]
    for start, below_ref, above_ref in zip(starts, below_refs, above_refs):
        place = slice(start, start + below_ref.shape[1])
        for at in range(0, work_ref.shape[2], span):
            part = slice(at, at + span)
            twist_fn = cor_ref[place, part]
            out_ref[0, place, part] += twist_fn * precise_dot(
                above_ref[0, :, part], up_ref[...]
            ) + precise_dot(twist_fn * below_ref[0, :, part], down_ref[...])


def join_terms(work, row_sum, cor, left, up, down, mode_blocks, starts, below, above):
    nvec, rows, width = work.shape
    one = pl.BlockSpec((1, rows, width), lambda i: (i, 0, 0))
    pieces = [pl.BlockSpec((1, b.shape[1], width), lambda i: (i, 0, 0)) for b in below]
    flops = 2 * work.size * (rows * len(mode_blocks) + 2 * up.shape[0])
    return pl.pallas_call(
        functools.partial(join_kernel, len(mode_blocks), tuple(starts)),
        grid=(nvec,),
        in_specs=[
            one,
            one,
            whole_spec(cor.shape),
            whole_spec(left.shape),
            whole_spec(up.shape),
            whole_spec(down.shape),
        ]
        + [one] * len(mode_blocks)
        + pieces
        + pieces,
        out_specs=one,
        out_shape=jax.ShapeDtypeStruct(work.shape, jnp.float32),
        compiler_params=pltpu.CompilerParams(vmem_limit_bytes=VMEM_BYTES),
        cost_estimate=pl.CostEstimate(
            flops=6 * flops, bytes_accessed=24 * work.size, transcendentals=0
        ),
        name="join_terms",
    )(work, row_sum, cor, left, up, down, *mode_blocks, *below, *above)


def far_terms_kernel(
    nvec, coef_ref, work_ref, above_ref, below_ref, fn_ref, vec_ref, before_ref, out_ref, sum_ref, sums
):
    step = pl.program_id(0)

    @pl.when(step == 0)
    def _():
        sums[...] = jnp.zeros_like(sums)

    skip_fn = fn_ref[...]
    for i in range(nvec):
        out_ref[i] = work_ref[i] + skip_fn * (
            coef_ref[0] * above_ref[i] + coef_ref[1] * below_ref[i]
        )
    groups = vector_groups(nvec)
    for ours in groups:
        for other in groups:
            cross = [(j, i) for j in other for i in ours]
            square = [(i, j) for i in ours for j in other if i <= j]
            cross_totals = {p: sums[0, p[0] * nvec + p[1]] for p in cross}
            square_totals = {p: sums[1, p[0] * nvec + p[1]] for p in square}
            for place in tiles(*out_ref.shape[1:]):
                works = {i: out_ref[(i, *place)] for i in ours}
                if square:
                    works.update({j: out_ref[(j, *place)] for j in other if j not in works})
                vecs = {j: vec_ref[(j, *place)] for j in other}
                for j, i in cross:
                    cross_totals[j, i] = cross_totals[j, i] + vecs[j] * works[i]
                for i, j in square:
                    square_totals[i, j] = square_totals[i, j] + works[i] * works[j]
            for j, i in cross:
                sums[0, j * nvec + i] = cross_totals[j, i]
            for i, j in square:
                sums[1, i * nvec + j] = square_totals[i, j]

    @pl.when(step == pl.num_programs(0) - 1)
    def _():
        lane = lax.broadcasted_iota(jnp.int32, (nvec, LANES), 1)
        packed = before_ref[...]
        packed = packed + packed_columns(lambda i, j: sums[0, j * nvec + i], nvec, 0, lane)
        packed = packed + packed_columns(
            lambda i, j: sums[1, min(i, j) * nvec + max(i, j)], nvec, nvec, lane
        )
        sum_ref[...] = jnp.broadcast_to(packed[None], sum_ref.shape)


def far_terms(coef, work, above, below, skip_fn, vec, before, start, block_rows, copies):
    nvec, rows, width = work.shape
    piece_rows = above.shape[1]
    first = start // block_rows
    whole = pl.BlockSpec((nvec, block_rows, width), lambda s: (0, s + first, 0))
    piece = pl.BlockSpec((nvec, block_rows, width), lambda s: (0, s, 0))
    return pl.pallas_call(
        functools.partial(far_terms_kernel, nvec),
        grid=(piece_rows // block_rows,),
        in_specs=[
            pl.BlockSpec(memory_space=pltpu.SMEM),
            whole,
            piece,
            piece,
            pl.BlockSpec((block_rows, width), lambda s: (s + first, 0)),
            whole,
            whole_spec((nvec, LANES)),
        ],
        out_specs=[whole, whole_spec((copies, nvec, LANES))],
        out_shape=[
            jax.ShapeDtypeStruct(work.shape, jnp.float32),
            jax.ShapeDtypeStruct((copies, nvec, LANES), jnp.float32),
        ],
        scratch_shapes=[pltpu.VMEM((2, nvec * nvec, SUBLANES, LANES), jnp.float32)],
        input_output_aliases={1: 0},
        compiler_params=pltpu.CompilerParams(vmem_limit_bytes=VMEM_BYTES),
        cost_estimate=pl.CostEstimate(
            flops=3 * nvec * nvec * piece_rows * width,
            bytes_accessed=20 * above.size,
            transcendentals=0,
        ),
        name="far_terms",
    )(coef, work, above, below, skip_fn, vec, before)


def small_algebra(nvec, count, packed):
    packed = packed * (1.0 / count)
    turned = packed.T
    cross = turned[0:nvec, :]
    cross_turned = packed[:, 0:nvec]
    work_gram = packed[:, nvec : 2 * nvec]
    vec_gram = packed[:, 2 * nvec : 3 * nvec]
    total = 2.0 * cross - precise_dot(vec_gram, cross)
    total_turned = 2.0 * cross_turned - precise_dot(cross_turned, vec_gram)
    gram = work_gram - precise_dot(total_turned, cross) - precise_dot(cross_turned, total)
    gram = gram + precise_dot(total_turned, precise_dot(vec_gram, total))
    gram = 0.5 * (gram + gram.T)
    row = lax.broadcasted_iota(jnp.int32, (nvec, nvec), 0)
    column = lax.broadcasted_iota(jnp.int32, (nvec, nvec), 1)
    inverse = jnp.where(row == column, 1.0, 0.0)
    lower = jnp.zeros((nvec, nvec), jnp.float32)
    for at in range(nvec):
        pivot = gram[at : at + 1, at : at + 1]
        scale = lax.rsqrt(pivot)
        scale = scale * (1.5 - 0.5 * pivot * scale * scale)
        scaled = gram[:, at : at + 1] * scale
        lower = jnp.where((column == at) & (row >= at), scaled, lower)
        pivot_row = inverse[at : at + 1, :] * scale
        factor = jnp.where(row > at, scaled, 0.0)
        inverse = jnp.where(row == at, pivot_row, inverse - factor * pivot_row)
        gram = gram - factor * (gram[at : at + 1, :] * scale)
    return total, lower, inverse, -precise_dot(inverse, total_turned)


def basis_kernel(nvec, count, sum_ref, work_ref, vec_ref, out_ref, alpha_ref, lower_ref, coefs):
    @pl.when(pl.program_id(0) == 0)
    def _():
        packed = sum_ref[0]
        for other in range(1, sum_ref.shape[0]):
            packed = packed + sum_ref[other]
        total, lower, inverse, mixing = small_algebra(nvec, count, packed)
        alpha_ref[...] = total
        lower_ref[...] = lower
        for number, matrix in enumerate((inverse, mixing)):
            for i in range(nvec):
                for j in range(nvec):
                    coefs[number, i * nvec + j] = jnp.broadcast_to(
                        matrix[i : i + 1, j : j + 1], (SUBLANES, LANES)
                    )

    places = tiles(*work_ref.shape[1:])
    for at in range(0, len(places), 2):
        group = places[at : at + 2]
        works = [[work_ref[(j, *place)] for place in group] for j in range(nvec)]
        vecs = [[vec_ref[(j, *place)] for place in group] for j in range(nvec)]
        for i in range(nvec):
            totals = [None] * len(group)
            for j in range(nvec):
                mixing = coefs[1, i * nvec + j]
                for number in range(len(group)):
                    term = mixing * vecs[j][number]
                    totals[number] = term if j == 0 else totals[number] + term
            for j in range(i + 1):
                inverse = coefs[0, i * nvec + j]
                for number in range(len(group)):
                    totals[number] = totals[number] + inverse * works[j][number]
            for number, place in enumerate(group):
                out_ref[(i, *place)] = totals[number]


def basis_of(count, sums, work, vec, block_rows):
    nvec, rows, width = work.shape
    block = pl.BlockSpec((nvec, block_rows, width), lambda s: (0, s, 0))
    small = jax.ShapeDtypeStruct((nvec, nvec), jnp.float32)
    return pl.pallas_call(
        functools.partial(basis_kernel, nvec, count),
        grid=(rows // block_rows,),
        in_specs=[whole_spec(sums.shape), block, block],
        out_specs=[block, whole_spec(small.shape), whole_spec(small.shape)],
        out_shape=[jax.ShapeDtypeStruct(work.shape, jnp.float32), small, small],
        scratch_shapes=[pltpu.VMEM((2, nvec * nvec, SUBLANES, LANES), jnp.float32)],
        compiler_params=pltpu.CompilerParams(vmem_limit_bytes=VMEM_BYTES),
        cost_estimate=pl.CostEstimate(
            flops=4 * nvec * work.size, bytes_accessed=12 * work.size, transcendentals=0
        ),
        name="basis",
    )(sums, work, vec)


def shards(
    vectors,
    previous,
    beta,
    potential,
    coriolis_fn,
    second_fn,
    rot_const,
    coupling,
    kin_one,
    kin_two,
    kin_three,
    kin_four,
    kin_five,
    kin_six,
    coriolis_derivative,
):
    _, nvec, *points, width = vectors.shape
    rows = points[0] * points[1] * points[2]
    devices = lax.axis_size(ALL_AXES)
    block_index = lax.axis_index("ka")
    nblocks = lax.axis_size("ka")
    row_peers = lax.axis_size("row")
    current = vectors.reshape(nvec, rows, width)
    older = previous.reshape(nvec, rows, width)
    block_rows = min(32, rows // 2)
    starts = [0, rows - block_rows]
    stops = [rows - block_rows, rows]

    below_one, above_one = [], []
    for start, stop in zip(starts, stops):
        piece = current[:, start:stop]
        below_one.append(hop(piece, "ka", 1))
        above_one.append(hop(piece, "ka", -1))
    below_two = [hop(piece, "ka", 1) for piece in below_one]
    above_two = [hop(piece, "ka", -1) for piece in above_one]
    mode_at = lax.axis_index("mode")
    mode_peers = lax.axis_size("mode")
    moved = ring_blocks(current, "mode")
    owners = [(mode_at + by) % mode_peers for by, _ in moved]
    mode_blocks = [block for _, block in moved]
    at = jnp.stack([block_index, mode_at, *owners]).astype(jnp.int32)
    span = next((s for s in (256, 128) if width % s == 0 and s % kin_six.shape[0] == 0), width)
    left, row_mat, tail, up, down = operators(
        tuple(points),
        1 + len(mode_blocks),
        row_peers * points[1] * points[2],
        width,
        span,
        at,
        coupling,
        (kin_one, kin_two, kin_three, kin_four, kin_five, kin_six, coriolis_derivative),
    )
    row_shares = lax.all_to_all(current, "row", split_axis=0, concat_axis=0, tiled=True)
    row_shares = row_kinetic(row_shares, row_mat, row_peers, points[1] * points[2])
    row_sum = lax.all_to_all(row_shares, "row", split_axis=0, concat_axis=0, tiled=True)
    lower_two = jnp.maximum(block_index - 2, 0)
    far_pair = jnp.stack([coupling[1, block_index], coupling[1, lower_two]])
    skip_fn = second_fn.reshape(rows, width)

    sums = vector_products(current, block_rows)
    work = local_terms(
        nblocks, at, rot_const, beta, current, older, potential.reshape(rows, width), left, tail
    )
    work = join_terms(
        work,
        row_sum,
        coriolis_fn.reshape(rows, width),
        left,
        up,
        down,
        mode_blocks,
        starts,
        below_one,
        above_one,
    )
    for number, start in enumerate(starts):
        last = number == len(starts) - 1
        work, copied = far_terms(
            far_pair,
            work,
            above_two[number],
            below_two[number],
            skip_fn,
            current,
            sums,
            start,
            block_rows,
            devices if last else 1,
        )
        sums = copied[0]
    every_sum = lax.all_to_all(copied, ALL_AXES, split_axis=0, concat_axis=0, tiled=True)
    count = float(devices * rows * width)
    basis, alpha, lower = basis_of(count, every_sum, work, current, block_rows)
    return (basis.reshape(vectors.shape), alpha, lower)


def solution(mesh):
    return jax.shard_map(
        shards,
        mesh=mesh,
        in_specs=(
            P("ka", None, "mode", "row", None, None),
            P("ka", None, "mode", "row", None, None),
            P(),
            P("mode", "row", None, None),
            P("mode", "row", None, None),
            P("mode", "row", None, None),
            P(),
            P(),
            P(),
            P(),
            P(),
            P(),
            P(),
            P(),
            P(),
        ),
        out_specs=(P("ka", None, "mode", "row", None, None), P(), P()),
        check_vma=False,
    )
```

```python
import functools

import jax
import jax.numpy as jnp
from jax import lax
from jax.experimental import pallas as pl
from jax.experimental.pallas import tpu as pltpu
from jax.sharding import PartitionSpec as P

precise_mode = lax.Precision.HIGHEST
ALL_AXES = ("ka", "mode", "row")
VMEM_BYTES = 32 * 1024 * 1024
SMALL_VMEM_BYTES = 16 * 1024 * 1024
LANES = 128
SUBLANES = 8


def precise_dot(left, right):
    return jnp.dot(left, right, precision=precise_mode, preferred_element_type=jnp.float32)


def whole_spec(shape):
    return pl.BlockSpec(shape, lambda *_: (0,) * len(shape))


def hop(value, axis, by):
    peers = lax.axis_size(axis)
    pairs = [(i, i + by) for i in range(peers) if 0 <= i + by < peers]
    return lax.ppermute(value, axis, pairs)


def ring_blocks(value, axis):
    peers = lax.axis_size(axis)
    found = []
    for sign in (1, -1):
        travelling = value
        for step in range(1, (peers - 1 + (sign == 1)) // 2 + 1):
            travelling = lax.ppermute(
                travelling, axis, [(i, (i + sign) % peers) for i in range(peers)]
            )
            found.append((-sign * step, travelling))
    return found


def vector_groups(nvec):
    return [tuple(range(at, min(at + 4, nvec))) for at in range(0, nvec, 4)]


def tiles(rows, width):
    return [
        (slice(r, r + SUBLANES), slice(c, c + LANES))
        for r in range(0, rows, SUBLANES)
        for c in range(0, width, LANES)
    ]


def packed_columns(sums, nvec, offset, lane):
    packed = jnp.zeros((nvec, LANES), jnp.float32)
    for j in range(nvec):
        stacked = jnp.stack([sums(i, j) for i in range(nvec)])
        column = jnp.sum(jnp.sum(stacked, axis=1), axis=1, keepdims=True)
        packed = packed + jnp.where(lane == offset + j, column, 0.0)
    return packed


def add_products(nvec, left_ref, right_ref, sums, number, places, symmetric):
    groups = vector_groups(nvec)
    for ours in groups:
        for other in groups:
            pairs = [(i, j) for i in ours for j in other if i <= j or not symmetric]
            if not pairs:
                continue
            totals = {pair: sums[number, pair[0] * nvec + pair[1]] for pair in pairs}
            for place in places:
                lefts = {i: left_ref[(i, *place)] for i in {p[0] for p in pairs}}
                rights = {j: right_ref[(j, *place)] for j in {p[1] for p in pairs}}
                for i, j in pairs:
                    totals[i, j] = totals[i, j] + lefts[i] * rights[j]
            for i, j in pairs:
                sums[number, i * nvec + j] = totals[i, j]


def resident_kernel(nvec, vec_ref, fn_ref, out_ref, copy_ref, fn_copy_ref, sums):
    step = pl.program_id(0)

    @pl.when(step == 0)
    def _():
        sums[...] = jnp.zeros_like(sums)

    copy_ref[...] = vec_ref[...]
    fn_copy_ref[...] = fn_ref[...]
    add_products(nvec, vec_ref, vec_ref, sums, 0, tiles(*vec_ref.shape[1:]), True)

    @pl.when(step == pl.num_programs(0) - 1)
    def _():
        lane = lax.broadcasted_iota(jnp.int32, (nvec, LANES), 1)
        out_ref[...] = packed_columns(
            lambda i, j: sums[0, min(i, j) * nvec + max(i, j)], nvec, 2 * nvec, lane
        )


def resident(vec, skip_fn, block_rows):
    nvec, rows, width = vec.shape
    block = pl.BlockSpec((nvec, block_rows, width), lambda s: (0, s, 0))
    fn_block = pl.BlockSpec((block_rows, width), lambda s: (s, 0))
    return pl.pallas_call(
        functools.partial(resident_kernel, nvec),
        grid=(rows // block_rows,),
        in_specs=[block, fn_block],
        out_specs=[whole_spec((nvec, LANES)), block, fn_block],
        out_shape=[
            jax.ShapeDtypeStruct((nvec, LANES), jnp.float32),
            jax.ShapeDtypeStruct(vec.shape, jnp.float32),
            jax.ShapeDtypeStruct(skip_fn.shape, jnp.float32),
        ],
        scratch_shapes=[pltpu.VMEM((1, nvec * nvec, SUBLANES, LANES), jnp.float32)],
        compiler_params=pltpu.CompilerParams(vmem_limit_bytes=VMEM_BYTES),
        cost_estimate=pl.CostEstimate(
            flops=nvec * (nvec + 1) * rows * width, bytes_accessed=8 * vec.size, transcendentals=0
        ),
        name="resident",
    )(vec, skip_fn)


def kron_term(matrix, size, stride, extent, row_offset=0, column_offset=0, sign=1.0):
    points = matrix.shape[0]

    def digits(shape, axis):
        index = lax.broadcasted_iota(jnp.int32, shape, axis)
        return index, lax.rem(lax.div(index, stride), size)

    def picks(offset):
        _, digit = digits((extent, points), 0)
        point = lax.broadcasted_iota(jnp.int32, (extent, points), 1)
        return jnp.where(digit + offset == point, 1.0, 0.0)

    def transposed_dot(one, two):
        return lax.dot_general(
            one, two, (((1,), (1,)), ((), ())), precision=precise_mode,
            preferred_element_type=jnp.float32,
        )

    picked = picks(row_offset)
    picked = 0.5 * (precise_dot(picked, matrix) + sign * transposed_dot(picked, matrix))
    spread = transposed_dot(picked, picks(column_offset))
    row, row_digit = digits((extent, extent), 0)
    column, column_digit = digits((extent, extent), 1)
    same = (row - row_digit * stride) == (column - column_digit * stride)
    return jnp.where(same, spread, 0.0)


def operators_kernel(
    points, mode_count, group, at_ref, coupling_ref, one_ref, two_ref, three_ref, four_ref, five_ref,
    six_ref, der_ref, left_ref, tail_ref, up_ref, down_ref,
):
    points_one, points_two, points_three = points
    rows = points_one * points_two * points_three
    stride = points_two * points_three
    mine = at_ref[1] * points_one
    row_mine = at_ref[2] * points_two
    left_ref[0] = (
        kron_term(one_ref[...], points_one, stride, rows, mine, mine)
        + kron_term(two_ref[...], points_two, points_three, rows, row_mine, row_mine)
        + kron_term(three_ref[...], points_three, 1, rows)
    )
    if group > 1:
        sibling = at_ref[3] * points_two
        left_ref[1] = kron_term(two_ref[...], points_two, points_three, rows, row_mine, sibling)
    for number in range(mode_count):
        owner = at_ref[4 + number] * points_one
        left_ref[group + number] = kron_term(one_ref[...], points_one, stride, rows, mine, owner)
    width = tail_ref.shape[0]
    fives, sixes = five_ref.shape[0], six_ref.shape[0]
    tail_ref[...] = (
        kron_term(four_ref[...], four_ref.shape[0], fives * sixes, width)
        + kron_term(five_ref[...], fives, sixes, width)
        + kron_term(six_ref[...], sixes, 1, width)
    )
    twist = kron_term(der_ref[...], sixes, 1, down_ref.shape[0], sign=-1.0)
    block = at_ref[0]
    up_ref[...] = -coupling_ref[0, block] * twist
    down_ref[...] = coupling_ref[0, jnp.maximum(block - 1, 0)] * twist


def operators(points, mode_count, group, width, span, at, coupling, matrices):
    rows = points[0] * points[1] * points[2]
    shapes = [(group + mode_count, rows, rows), (width, width), (span, span), (span, span)]
    smem = pl.BlockSpec(memory_space=pltpu.SMEM)
    return pl.pallas_call(
        functools.partial(operators_kernel, points, mode_count, group),
        in_specs=[smem, smem] + [pl.BlockSpec(memory_space=pltpu.VMEM)] * len(matrices),
        out_specs=[pl.BlockSpec(memory_space=pltpu.VMEM)] * len(shapes),
        out_shape=[jax.ShapeDtypeStruct(shape, jnp.float32) for shape in shapes],
        compiler_params=pltpu.CompilerParams(vmem_limit_bytes=VMEM_BYTES),
        cost_estimate=pl.CostEstimate(
            flops=500_000_000, bytes_accessed=4_000_000, transcendentals=0
        ),
        name="operators",
    )(at, coupling, *matrices)


def crossing_kernel(points, group, at_ref, two_ref, *refs):
    points_one, points_two, points_three = points
    held_refs, out_refs = refs[:group], refs[group:]
    owners = [at_ref[2], at_ref[3]][:group]
    peers = two_ref.shape[0] // points_two
    stride = points_two * points_three
    for number, out_ref in enumerate(out_refs):
        target = lax.rem(at_ref[2] + group * (number + 1), peers) * points_two
        coefs = {
            (a, k, b): 0.5
            * (
                two_ref[target + a, owners[k] * points_two + b]
                + two_ref[owners[k] * points_two + b, target + a]
            )
            for a in range(points_two)
            for k in range(group)
            for b in range(points_two)
        }
        for start in range(0, points_one * stride, stride):
            for _, lanes in tiles(SUBLANES, out_ref.shape[2]):
                for inner in range(0, points_three, SUBLANES):
                    values = {
                        (k, b): held_refs[k][0, pl.ds(start + b * points_three + inner, SUBLANES), lanes]
                        for k in range(group)
                        for b in range(points_two)
                    }
                    for a in range(points_two):
                        total = None
                        for (k, b), value in values.items():
                            term = coefs[a, k, b] * value
                            total = term if total is None else total + term
                        out_ref[0, pl.ds(start + a * points_three + inner, SUBLANES), lanes] = total


def crossing(points, at, two, held, count):
    nvec, rows, width = held[0].shape
    one = pl.BlockSpec((1, rows, width), lambda i: (i, 0, 0))
    smem = pl.BlockSpec(memory_space=pltpu.SMEM)
    return pl.pallas_call(
        functools.partial(crossing_kernel, points, len(held)),
        grid=(nvec,),
        in_specs=[smem, smem] + [one] * len(held),
        out_specs=[one] * count,
        out_shape=[jax.ShapeDtypeStruct(held[0].shape, jnp.float32)] * count,
        compiler_params=pltpu.CompilerParams(vmem_limit_bytes=VMEM_BYTES),
        cost_estimate=pl.CostEstimate(
            flops=2 * held[0].size * points[1] * len(held) * count,
            bytes_accessed=4 * held[0].size * (len(held) + count),
            transcendentals=0,
        ),
        name="crossing",
    )(at, two, *held)


def local_kernel(nvec, nblocks, group, at_ref, rot_ref, beta_ref, *refs):
    held_refs = refs[:group]
    old_ref, pot_ref, left_ref, tail_ref, out_ref = refs[group:]
    me = pl.program_id(0)
    block = at_ref[0]
    level = (block - nblocks // 2).astype(jnp.float32)
    current = held_refs[0][0]
    total = (pot_ref[...] + rot_ref[block] * level * level) * current
    for j in range(nvec):
        total = total - beta_ref[me, j] * old_ref[j]
    total = total + precise_dot(current, tail_ref[...])
    for number, held_ref in enumerate(held_refs):
        total = total + precise_dot(left_ref[number], held_ref[0])
    out_ref[0] = total


def local_terms(nblocks, at, rot_const, beta, held, old, pot, left, tail):
    nvec, rows, width = old.shape
    one = pl.BlockSpec((1, rows, width), lambda i: (i, 0, 0))
    smem = pl.BlockSpec(memory_space=pltpu.SMEM)
    return pl.pallas_call(
        functools.partial(local_kernel, nvec, nblocks, len(held)),
        grid=(nvec,),
        in_specs=[smem, smem, smem]
        + [one] * len(held)
        + [
            whole_spec(old.shape),
            whole_spec(pot.shape),
            pl.BlockSpec((len(held), rows, rows), lambda i: (0, 0, 0)),
            whole_spec(tail.shape),
        ],
        out_specs=one,
        out_shape=jax.ShapeDtypeStruct(old.shape, jnp.float32),
        compiler_params=pltpu.CompilerParams(vmem_limit_bytes=VMEM_BYTES),
        cost_estimate=pl.CostEstimate(
            flops=12 * old.size * (rows * len(held) + width),
            bytes_accessed=4 * old.size * (2 + len(held)),
            transcendentals=0,
        ),
        name="local_terms",
    )(at, rot_const, beta, *held, old, pot, left, tail)


def join_kernel(mode_count, sum_count, group, *refs):
    work_ref, cor_ref, left_ref, up_ref, down_ref, below_ref, above_ref = refs[:7]
    mode_refs = refs[7 : 7 + mode_count]
    sum_refs = refs[7 + mode_count : 7 + mode_count + sum_count]
    out_ref = refs[-1]
    total = work_ref[0]
    for sum_ref in sum_refs:
        total = total + sum_ref[0]
    for number, mode_ref in enumerate(mode_refs):
        total = total + precise_dot(left_ref[group + number], mode_ref[0])
    out_ref[0] = total
    span = up_ref.shape[0]
    for at in range(0, work_ref.shape[2], span):
        part = slice(at, at + span)
        twist_fn = cor_ref[:, part]
        out_ref[0, :, part] += twist_fn * precise_dot(
            above_ref[0, :, part], up_ref[...]
        ) + precise_dot(twist_fn * below_ref[0, :, part], down_ref[...])


def join_terms(work, cor, left, up, down, below, above, mode_blocks, row_sums):
    nvec, rows, width = work.shape
    one = pl.BlockSpec((1, rows, width), lambda i: (i, 0, 0))
    flops = 2 * work.size * (rows * len(mode_blocks) + 2 * up.shape[0])
    return pl.pallas_call(
        functools.partial(
            join_kernel, len(mode_blocks), len(row_sums), left.shape[0] - len(mode_blocks)
        ),
        grid=(nvec,),
        in_specs=[
            one,
            whole_spec(cor.shape),
            whole_spec(left.shape),
            whole_spec(up.shape),
            whole_spec(down.shape),
            one,
            one,
        ]
        + [one] * (len(mode_blocks) + len(row_sums)),
        out_specs=one,
        out_shape=jax.ShapeDtypeStruct(work.shape, jnp.float32),
        compiler_params=pltpu.CompilerParams(vmem_limit_bytes=VMEM_BYTES),
        cost_estimate=pl.CostEstimate(
            flops=6 * flops, bytes_accessed=24 * work.size, transcendentals=0
        ),
        name="join_terms",
    )(work, cor, left, up, down, below, above, *mode_blocks, *row_sums)


def far_terms_kernel(
    nvec, block_rows, coef_ref, work_ref, above_ref, below_ref, fn_ref, vec_ref, before_ref,
    out_ref, sum_ref, sums,
):
    del work_ref
    sums[...] = jnp.zeros_like(sums)
    rows, width = out_ref.shape[1:]

    def some_rows(step, _):
        at = pl.multiple_of(step * block_rows, block_rows)
        places = [
            (pl.ds(at + place.start, SUBLANES), lanes) for place, lanes in tiles(block_rows, width)
        ]
        for place in places:
            skip_fn = fn_ref[place]
            above_fn = coef_ref[0] * skip_fn
            below_fn = coef_ref[1] * skip_fn
            for i in range(nvec):
                here = (i, *place)
                out_ref[here] = out_ref[here] + above_fn * above_ref[here] + below_fn * below_ref[here]
        add_products(nvec, vec_ref, out_ref, sums, 0, places, False)
        add_products(nvec, out_ref, out_ref, sums, 1, places, True)
        return 0

    lax.fori_loop(0, rows // block_rows, some_rows, 0)
    lane = lax.broadcasted_iota(jnp.int32, (nvec, LANES), 1)
    packed = before_ref[...]
    packed = packed + packed_columns(lambda i, j: sums[0, j * nvec + i], nvec, 0, lane)
    packed = packed + packed_columns(
        lambda i, j: sums[1, min(i, j) * nvec + max(i, j)], nvec, nvec, lane
    )
    sum_ref[...] = jnp.broadcast_to(packed[None], sum_ref.shape)


def far_terms(coef, work, above, below, skip_fn, vec, before, block_rows, copies):
    nvec, rows, width = work.shape
    whole = pl.BlockSpec(memory_space=pltpu.VMEM)
    work, above, below, skip_fn, vec = (
        pltpu.with_memory_space_constraint(array, pltpu.VMEM)
        for array in (work, above, below, skip_fn, vec)
    )
    return pl.pallas_call(
        functools.partial(far_terms_kernel, nvec, block_rows),
        in_specs=[pl.BlockSpec(memory_space=pltpu.SMEM)] + [whole] * 6,
        out_specs=[whole, whole],
        out_shape=[
            jax.ShapeDtypeStruct(work.shape, jnp.float32),
            jax.ShapeDtypeStruct((copies, nvec, LANES), jnp.float32),
        ],
        scratch_shapes=[pltpu.VMEM((2, nvec * nvec, SUBLANES, LANES), jnp.float32)],
        input_output_aliases={1: 0},
        compiler_params=pltpu.CompilerParams(vmem_limit_bytes=SMALL_VMEM_BYTES),
        cost_estimate=pl.CostEstimate(
            flops=3 * nvec * nvec * rows * width,
            bytes_accessed=20 * above.size,
            transcendentals=0,
        ),
        name="far_terms",
    )(coef, work, above, below, skip_fn, vec, before)


def small_algebra(nvec, count, packed):
    packed = packed * (1.0 / count)
    turned = packed.T
    cross = turned[0:nvec, :]
    cross_turned = packed[:, 0:nvec]
    work_gram = packed[:, nvec : 2 * nvec]
    vec_gram = packed[:, 2 * nvec : 3 * nvec]
    total = 2.0 * cross - precise_dot(vec_gram, cross)
    total_turned = 2.0 * cross_turned - precise_dot(cross_turned, vec_gram)
    gram = work_gram - precise_dot(total_turned, cross) - precise_dot(cross_turned, total)
    gram = gram + precise_dot(total_turned, precise_dot(vec_gram, total))
    gram = 0.5 * (gram + gram.T)
    row = lax.broadcasted_iota(jnp.int32, (nvec, nvec), 0)
    column = lax.broadcasted_iota(jnp.int32, (nvec, nvec), 1)
    inverse = jnp.where(row == column, 1.0, 0.0)
    lower = jnp.zeros((nvec, nvec), jnp.float32)
    for at in range(nvec):
        pivot = gram[at : at + 1, at : at + 1]
        scale = lax.rsqrt(pivot)
        scale = scale * (1.5 - 0.5 * pivot * scale * scale)
        scaled = gram[:, at : at + 1] * scale
        lower = jnp.where((column == at) & (row >= at), scaled, lower)
        pivot_row = inverse[at : at + 1, :] * scale
        factor = jnp.where(row > at, scaled, 0.0)
        inverse = jnp.where(row == at, pivot_row, inverse - factor * pivot_row)
        gram = gram - factor * (gram[at : at + 1, :] * scale)
    return total, lower, inverse, -precise_dot(inverse, total_turned)


def basis_kernel(nvec, count, sum_ref, work_ref, vec_ref, out_ref, alpha_ref, lower_ref, coefs):
    @pl.when(pl.program_id(0) == 0)
    def _():
        packed = sum_ref[0]
        for other in range(1, sum_ref.shape[0]):
            packed = packed + sum_ref[other]
        total, lower, inverse, mixing = small_algebra(nvec, count, packed)
        alpha_ref[...] = total
        lower_ref[...] = lower
        for number, matrix in enumerate((inverse, mixing)):
            for i in range(nvec):
                for j in range(nvec):
                    coefs[number, i * nvec + j] = jnp.broadcast_to(
                        matrix[i : i + 1, j : j + 1], (SUBLANES, LANES)
                    )

    start = pl.multiple_of(pl.program_id(0) * out_ref.shape[1], out_ref.shape[1])
    places = tiles(*out_ref.shape[1:])
    for at in range(0, len(places), 4):
        group = places[at : at + 4]
        held = [(pl.ds(start + place.start, SUBLANES), lanes) for place, lanes in group]
        for ours in vector_groups(nvec):
            totals = {}
            for number, ref in ((1, vec_ref), (0, work_ref)):
                for j in range(nvec):
                    outs = [i for i in ours if number == 1 or j <= i]
                    if not outs:
                        continue
                    values = [ref[(j, *place)] for place in held]
                    for i in outs:
                        coef = coefs[number, i * nvec + j]
                        for spot, value in enumerate(values):
                            term = coef * value
                            here = (i, spot)
                            totals[here] = totals[here] + term if here in totals else term
            for i in ours:
                for spot, place in enumerate(group):
                    out_ref[(i, *place)] = totals[i, spot]


def basis_of(count, sums, work, vec, block_rows):
    nvec, rows, width = work.shape
    block = pl.BlockSpec((nvec, block_rows, width), lambda s: (0, s, 0))
    small = jax.ShapeDtypeStruct((nvec, nvec), jnp.float32)
    whole = pl.BlockSpec(memory_space=pltpu.VMEM)
    work, vec = (pltpu.with_memory_space_constraint(array, pltpu.VMEM) for array in (work, vec))
    return pl.pallas_call(
        functools.partial(basis_kernel, nvec, count),
        grid=(rows // block_rows,),
        in_specs=[whole, whole, whole],
        out_specs=[block, whole_spec(small.shape), whole_spec(small.shape)],
        out_shape=[jax.ShapeDtypeStruct(work.shape, jnp.float32), small, small],
        scratch_shapes=[pltpu.VMEM((2, nvec * nvec, SUBLANES, LANES), jnp.float32)],
        compiler_params=pltpu.CompilerParams(vmem_limit_bytes=SMALL_VMEM_BYTES),
        cost_estimate=pl.CostEstimate(
            flops=4 * nvec * work.size, bytes_accessed=12 * work.size, transcendentals=0
        ),
        name="basis",
    )(sums, work, vec)


def shards(
    vectors,
    previous,
    beta,
    potential,
    coriolis_fn,
    second_fn,
    rot_const,
    coupling,
    kin_one,
    kin_two,
    kin_three,
    kin_four,
    kin_five,
    kin_six,
    coriolis_derivative,
):
    _, nvec, *points, width = vectors.shape
    rows = points[0] * points[1] * points[2]
    devices = lax.axis_size(ALL_AXES)
    block_index = lax.axis_index("ka")
    nblocks = lax.axis_size("ka")
    row_peers = lax.axis_size("row")
    mode_peers = lax.axis_size("mode")
    row_at = lax.axis_index("row")
    mode_at = lax.axis_index("mode")
    current = vectors.reshape(nvec, rows, width)
    older = previous.reshape(nvec, rows, width)
    block_rows = min(32, rows)

    below_one = hop(current, "ka", 1)
    above_one = hop(current, "ka", -1)
    below_two = hop(below_one, "ka", 1)
    above_two = hop(above_one, "ka", -1)
    moved = ring_blocks(current, "mode")
    owners = [(mode_at + by) % mode_peers for by, _ in moved]
    mode_blocks = [block for _, block in moved]
    at = jnp.stack([block_index, mode_at, row_at, row_at ^ 1, *owners]).astype(jnp.int32)
    group = 2 - row_peers % 2
    held = [current]
    if group == 2:
        held.append(lax.ppermute(current, "row", [(i, i ^ 1) for i in range(row_peers)]))
    away = row_peers // group - 1
    row_sums = crossing(tuple(points), at, kin_two, held, away) if away else []
    row_sums = [
        lax.ppermute(
            part, "row", [(i, (i + group * (number + 1)) % row_peers) for i in range(row_peers)]
        )
        for number, part in enumerate(row_sums)
    ]

    span = next((s for s in (256, 128) if width % s == 0 and s % kin_six.shape[0] == 0), width)
    left, tail, up, down = operators(
        tuple(points),
        len(mode_blocks),
        group,
        width,
        span,
        at,
        coupling,
        (kin_one, kin_two, kin_three, kin_four, kin_five, kin_six, coriolis_derivative),
    )
    lower_two = jnp.maximum(block_index - 2, 0)
    far_pair = jnp.stack([coupling[1, block_index], coupling[1, lower_two]])
    sums, vec, skip_fn = resident(current, second_fn.reshape(rows, width), block_rows)
    work = local_terms(
        nblocks, at, rot_const, beta, held, older, potential.reshape(rows, width), left, tail
    )
    work = join_terms(
        work,
        coriolis_fn.reshape(rows, width),
        left,
        up,
        down,
        below_one,
        above_one,
        mode_blocks,
        row_sums,
    )
    work, copied = far_terms(
        far_pair, work, above_two, below_two, skip_fn, vec, sums, block_rows, devices
    )
    every_sum = lax.all_to_all(copied, ALL_AXES, split_axis=0, concat_axis=0, tiled=True)
    count = float(devices * rows * width)
    basis, alpha, lower = basis_of(count, every_sum, work, vec, block_rows)
    return (basis.reshape(vectors.shape), alpha, lower)


def solution(mesh):
    return jax.shard_map(
        shards,
        mesh=mesh,
        in_specs=(
            P("ka", None, "mode", "row", None, None),
            P("ka", None, "mode", "row", None, None),
            P(),
            P("mode", "row", None, None),
            P("mode", "row", None, None),
            P("mode", "row", None, None),
            P(),
            P(),
            P(),
            P(),
            P(),
            P(),
            P(),
            P(),
            P(),
        ),
        out_specs=(P("ka", None, "mode", "row", None, None), P(), P()),
        check_vma=False,
    )
```

```python
import functools

import jax
import jax.numpy as jnp
from jax import lax
from jax.experimental import pallas as pl
from jax.experimental.pallas import tpu as pltpu
from jax.sharding import PartitionSpec as P

precise_mode = lax.Precision.HIGHEST
ALL_AXES = ("ka", "mode", "row")
VMEM_BYTES = 32 * 1024 * 1024
SMALL_VMEM_BYTES = 16 * 1024 * 1024
LANES = 128
HOP_WEIGHT = 25_000_000_000
SUBLANES = 8


def precise_dot(left, right):
    return jnp.dot(left, right, precision=precise_mode, preferred_element_type=jnp.float32)


def whole_spec(shape):
    return pl.BlockSpec(shape, lambda *_: (0,) * len(shape))


def hop(value, axis, by):
    peers = lax.axis_size(axis)
    pairs = [(i, i + by) for i in range(peers) if 0 <= i + by < peers]
    return lax.ppermute(value, axis, pairs)


def vector_groups(nvec):
    return [tuple(range(at, min(at + 4, nvec))) for at in range(0, nvec, 4)]


def tiles(rows, width):
    return [
        (slice(r, r + SUBLANES), slice(c, c + LANES))
        for r in range(0, rows, SUBLANES)
        for c in range(0, width, LANES)
    ]


def packed_columns(sums, nvec, offset, lane):
    packed = jnp.zeros((nvec, LANES), jnp.float32)
    for j in range(nvec):
        stacked = jnp.stack([sums(i, j) for i in range(nvec)])
        column = jnp.sum(jnp.sum(stacked, axis=1), axis=1, keepdims=True)
        packed = packed + jnp.where(lane == offset + j, column, 0.0)
    return packed


def add_products(nvec, left_ref, right_ref, sums, number, places, symmetric):
    groups = vector_groups(nvec)
    for ours in groups:
        for other in groups:
            pairs = [(i, j) for i in ours for j in other if i <= j or not symmetric]
            if not pairs:
                continue
            totals = {pair: sums[number, pair[0] * nvec + pair[1]] for pair in pairs}
            for place in places:
                lefts = {i: left_ref[(i, *place)] for i in {p[0] for p in pairs}}
                rights = {j: right_ref[(j, *place)] for j in {p[1] for p in pairs}}
                for i, j in pairs:
                    totals[i, j] = totals[i, j] + lefts[i] * rights[j]
            for i, j in pairs:
                sums[number, i * nvec + j] = totals[i, j]


def resident_kernel(nvec, vec_ref, fn_ref, out_ref, copy_ref, fn_copy_ref, sums):
    step = pl.program_id(0)

    @pl.when(step == 0)
    def _():
        sums[...] = jnp.zeros_like(sums)

    copy_ref[...] = vec_ref[...]
    fn_copy_ref[...] = fn_ref[...]
    add_products(nvec, vec_ref, vec_ref, sums, 0, tiles(*vec_ref.shape[1:]), True)

    @pl.when(step == pl.num_programs(0) - 1)
    def _():
        lane = lax.broadcasted_iota(jnp.int32, (nvec, LANES), 1)
        out_ref[...] = packed_columns(
            lambda i, j: sums[0, min(i, j) * nvec + max(i, j)], nvec, 2 * nvec, lane
        )


def resident(vec, skip_fn, block_rows):
    nvec, rows, width = vec.shape
    block = pl.BlockSpec((nvec, block_rows, width), lambda s: (0, s, 0))
    fn_block = pl.BlockSpec((block_rows, width), lambda s: (s, 0))
    return pl.pallas_call(
        functools.partial(resident_kernel, nvec),
        grid=(rows // block_rows,),
        in_specs=[block, fn_block],
        out_specs=[whole_spec((nvec, LANES)), block, fn_block],
        out_shape=[
            jax.ShapeDtypeStruct((nvec, LANES), jnp.float32),
            jax.ShapeDtypeStruct(vec.shape, jnp.float32),
            jax.ShapeDtypeStruct(skip_fn.shape, jnp.float32),
        ],
        scratch_shapes=[pltpu.VMEM((1, nvec * nvec, SUBLANES, LANES), jnp.float32)],
        compiler_params=pltpu.CompilerParams(vmem_limit_bytes=VMEM_BYTES),
        cost_estimate=pl.CostEstimate(
            flops=nvec * (nvec + 1) * rows * width, bytes_accessed=8 * vec.size, transcendentals=0
        ),
        name="resident",
    )(vec, skip_fn)


def split_kernel(start, vec_ref, out_ref, sems):
    copies = [
        pltpu.make_async_copy(
            vec_ref.at[i, pl.ds(start, out_ref.shape[1])], out_ref.at[i], sems.at[i]
        )
        for i in range(out_ref.shape[0])
    ]
    for copy in copies:
        copy.start()
    for copy in copies:
        copy.wait()


def split_rows(vec, start, stop):
    nvec, _, width = vec.shape
    shape = (nvec, stop - start, width)
    return pl.pallas_call(
        functools.partial(split_kernel, start),
        in_specs=[pl.BlockSpec(memory_space=pl.ANY)],
        out_specs=pl.BlockSpec(memory_space=pl.ANY),
        out_shape=jax.ShapeDtypeStruct(shape, jnp.float32),
        scratch_shapes=[pltpu.SemaphoreType.DMA((nvec,))],
        compiler_params=pltpu.CompilerParams(vmem_limit_bytes=SMALL_VMEM_BYTES),
        cost_estimate=pl.CostEstimate(
            flops=0, bytes_accessed=8 * nvec * (stop - start) * width, transcendentals=0
        ),
        name="split_rows",
    )(vec)


def handed_on(array, weight):
    return pl.pallas_call(
        lambda in_ref, out_ref: None,
        in_specs=[pl.BlockSpec(memory_space=pl.ANY)],
        out_specs=pl.BlockSpec(memory_space=pl.ANY),
        out_shape=jax.ShapeDtypeStruct(array.shape, array.dtype),
        input_output_aliases={0: 0},
        cost_estimate=pl.CostEstimate(flops=weight, bytes_accessed=0, transcendentals=0),
        name="handed_on",
    )(array)


def kron_term(matrix, size, stride, extent, row_offset=0, column_offset=0, sign=1.0):
    points = matrix.shape[0]

    def digits(shape, axis):
        index = lax.broadcasted_iota(jnp.int32, shape, axis)
        return index, lax.rem(lax.div(index, stride), size)

    def picks(offset):
        _, digit = digits((extent, points), 0)
        point = lax.broadcasted_iota(jnp.int32, (extent, points), 1)
        return jnp.where(digit + offset == point, 1.0, 0.0)

    def transposed_dot(one, two):
        return lax.dot_general(
            one, two, (((1,), (1,)), ((), ())), precision=precise_mode,
            preferred_element_type=jnp.float32,
        )

    picked = picks(row_offset)
    picked = 0.5 * (precise_dot(picked, matrix) + sign * transposed_dot(picked, matrix))
    spread = transposed_dot(picked, picks(column_offset))
    row, row_digit = digits((extent, extent), 0)
    column, column_digit = digits((extent, extent), 1)
    same = (row - row_digit * stride) == (column - column_digit * stride)
    return jnp.where(same, spread, 0.0)


def operators_kernel(
    points, mode_count, group, at_ref, coupling_ref, one_ref, two_ref, three_ref, four_ref, five_ref,
    six_ref, der_ref, left_ref, tail_ref, up_ref, down_ref,
):
    points_one, points_two, points_three = points
    rows = points_one * points_two * points_three
    stride = points_two * points_three
    mine = at_ref[1] * points_one
    row_mine = at_ref[2] * points_two
    left_ref[0] = (
        kron_term(two_ref[...], points_two, points_three, rows, row_mine, row_mine)
        + kron_term(three_ref[...], points_three, 1, rows)
    )
    if group > 1:
        sibling = at_ref[3] * points_two
        left_ref[1] = kron_term(two_ref[...], points_two, points_three, rows, row_mine, sibling)
    for number in range(mode_count):
        left_ref[group + number] = kron_term(
            one_ref[...], points_one, stride, rows, mine, number * points_one
        )
    width = tail_ref.shape[0]
    fives, sixes = five_ref.shape[0], six_ref.shape[0]
    tail_ref[...] = (
        kron_term(four_ref[...], four_ref.shape[0], fives * sixes, width)
        + kron_term(five_ref[...], fives, sixes, width)
        + kron_term(six_ref[...], sixes, 1, width)
    )
    twist = kron_term(der_ref[...], sixes, 1, down_ref.shape[0], sign=-1.0)
    block = at_ref[0]
    up_ref[...] = -coupling_ref[0, block] * twist
    down_ref[...] = coupling_ref[0, jnp.maximum(block - 1, 0)] * twist


def operators(points, mode_count, group, width, span, at, coupling, matrices):
    rows = points[0] * points[1] * points[2]
    shapes = [(group + mode_count, rows, rows), (width, width), (span, span), (span, span)]
    smem = pl.BlockSpec(memory_space=pltpu.SMEM)
    return pl.pallas_call(
        functools.partial(operators_kernel, points, mode_count, group),
        in_specs=[smem, smem] + [pl.BlockSpec(memory_space=pltpu.VMEM)] * len(matrices),
        out_specs=[pl.BlockSpec(memory_space=pltpu.VMEM)] * len(shapes),
        out_shape=[jax.ShapeDtypeStruct(shape, jnp.float32) for shape in shapes],
        compiler_params=pltpu.CompilerParams(vmem_limit_bytes=VMEM_BYTES),
        cost_estimate=pl.CostEstimate(
            flops=500_000_000, bytes_accessed=4_000_000, transcendentals=0
        ),
        name="operators",
    )(at, coupling, *matrices)


def crossing_kernel(points, group, at_ref, two_ref, *refs):
    points_one, points_two, points_three = points
    held_refs, out_refs = refs[:group], refs[group:]
    owners = [at_ref[2], at_ref[3]][:group]
    peers = two_ref.shape[0] // points_two
    stride = points_two * points_three
    for number, out_ref in enumerate(out_refs):
        target = lax.rem(at_ref[2] + group * (number + 1), peers) * points_two
        coefs = {
            (a, k, b): 0.5
            * (
                two_ref[target + a, owners[k] * points_two + b]
                + two_ref[owners[k] * points_two + b, target + a]
            )
            for a in range(points_two)
            for k in range(group)
            for b in range(points_two)
        }
        for start in range(0, points_one * stride, stride):
            for _, lanes in tiles(SUBLANES, out_ref.shape[2]):
                for inner in range(0, points_three, SUBLANES):
                    values = {
                        (k, b): held_refs[k][0, pl.ds(start + b * points_three + inner, SUBLANES), lanes]
                        for k in range(group)
                        for b in range(points_two)
                    }
                    for a in range(points_two):
                        total = None
                        for (k, b), value in values.items():
                            term = coefs[a, k, b] * value
                            total = term if total is None else total + term
                        out_ref[0, pl.ds(start + a * points_three + inner, SUBLANES), lanes] = total


def crossing(points, at, two, held, count):
    nvec, rows, width = held[0].shape
    one = pl.BlockSpec((1, rows, width), lambda i: (i, 0, 0))
    smem = pl.BlockSpec(memory_space=pltpu.SMEM)
    return pl.pallas_call(
        functools.partial(crossing_kernel, points, len(held)),
        grid=(nvec,),
        in_specs=[smem, smem] + [one] * len(held),
        out_specs=[one] * count,
        out_shape=[jax.ShapeDtypeStruct(held[0].shape, jnp.float32)] * count,
        compiler_params=pltpu.CompilerParams(vmem_limit_bytes=VMEM_BYTES),
        cost_estimate=pl.CostEstimate(
            flops=2 * held[0].size * points[1] * len(held) * count,
            bytes_accessed=4 * held[0].size * (len(held) + count),
            transcendentals=0,
        ),
        name="crossing",
    )(at, two, *held)


def local_kernel(nvec, nblocks, group, at_ref, rot_ref, beta_ref, *refs):
    held_refs = refs[:group]
    old_ref, pot_ref, left_ref, tail_ref, out_ref = refs[group:]
    me = pl.program_id(0)
    block = at_ref[0]
    level = (block - nblocks // 2).astype(jnp.float32)
    current = held_refs[0][0]
    total = (pot_ref[...] + rot_ref[block] * level * level) * current
    for j in range(nvec):
        total = total - beta_ref[me, j] * old_ref[j]
    total = total + precise_dot(current, tail_ref[...])
    for number, held_ref in enumerate(held_refs):
        total = total + precise_dot(left_ref[number], held_ref[0])
    out_ref[0] = total


def local_terms(nblocks, at, rot_const, beta, held, old, pot, left, tail):
    nvec, rows, width = old.shape
    one = pl.BlockSpec((1, rows, width), lambda i: (i, 0, 0))
    smem = pl.BlockSpec(memory_space=pltpu.SMEM)
    return pl.pallas_call(
        functools.partial(local_kernel, nvec, nblocks, len(held)),
        grid=(nvec,),
        in_specs=[smem, smem, smem]
        + [one] * len(held)
        + [
            whole_spec(old.shape),
            whole_spec(pot.shape),
            pl.BlockSpec((len(held), rows, rows), lambda i: (0, 0, 0)),
            whole_spec(tail.shape),
        ],
        out_specs=one,
        out_shape=jax.ShapeDtypeStruct(old.shape, jnp.float32),
        compiler_params=pltpu.CompilerParams(vmem_limit_bytes=VMEM_BYTES),
        cost_estimate=pl.CostEstimate(
            flops=12 * old.size * (rows * len(held) + width),
            bytes_accessed=4 * old.size * (2 + len(held)),
            transcendentals=0,
        ),
        name="local_terms",
    )(at, rot_const, beta, *held, old, pot, left, tail)


def join_kernel(starts, sum_count, *refs):
    work_ref, cor_ref, left_ref, up_ref, down_ref, mode_ref = refs[:6]
    pieces = len(starts)
    below_refs = refs[6 : 6 + pieces]
    above_refs = refs[6 + pieces : 6 + 2 * pieces]
    sum_refs = refs[6 + 2 * pieces : 6 + 2 * pieces + sum_count]
    out_ref = refs[-1]
    total = work_ref[0]
    for sum_ref in sum_refs:
        total = total + sum_ref[0]
    modes = mode_ref.shape[0]
    for number in range(modes):
        matrix = left_ref[left_ref.shape[0] - modes + number]
        total = total + precise_dot(matrix, mode_ref[number, 0])
    out_ref[0] = total
    span = up_ref.shape[0]
    for start, below_ref, above_ref in zip(starts, below_refs, above_refs):
        place = slice(start, start + below_ref.shape[1])
        for at in range(0, work_ref.shape[2], span):
            part = slice(at, at + span)
            twist_fn = cor_ref[place, part]
            out_ref[0, place, part] += twist_fn * precise_dot(
                above_ref[0, :, part], up_ref[...]
            ) + precise_dot(twist_fn * below_ref[0, :, part], down_ref[...])


def join_terms(work, cor, left, up, down, mode_blocks, starts, below, above, row_sums):
    nvec, rows, width = work.shape
    modes = mode_blocks.shape[0]
    one = pl.BlockSpec((1, rows, width), lambda i: (i, 0, 0))
    pieces = [pl.BlockSpec((1, b.shape[1], width), lambda i: (i, 0, 0)) for b in below]
    flops = 2 * work.size * (rows * modes + 2 * up.shape[0])
    return pl.pallas_call(
        functools.partial(join_kernel, tuple(starts), len(row_sums)),
        grid=(nvec,),
        in_specs=[
            one,
            whole_spec(cor.shape),
            whole_spec(left.shape),
            whole_spec(up.shape),
            whole_spec(down.shape),
            pl.BlockSpec((modes, 1, rows, width), lambda i: (0, i, 0, 0)),
        ]
        + pieces
        + pieces
        + [one] * len(row_sums),
        out_specs=one,
        out_shape=jax.ShapeDtypeStruct(work.shape, jnp.float32),
        compiler_params=pltpu.CompilerParams(vmem_limit_bytes=VMEM_BYTES),
        cost_estimate=pl.CostEstimate(
            flops=6 * flops, bytes_accessed=28 * work.size, transcendentals=0
        ),
        name="join_terms",
    )(work, cor, left, up, down, mode_blocks, *below, *above, *row_sums)


def far_terms_kernel(
    nvec, start, coef_ref, work_ref, above_ref, below_ref, fn_ref, vec_ref, before_ref, out_ref,
    sum_ref, sums,
):
    del work_ref
    step = pl.program_id(0)
    _, block_rows, width = above_ref.shape

    @pl.when(step == 0)
    def _():
        sums[...] = jnp.zeros_like(sums)

    at = pl.multiple_of(start + step * block_rows, SUBLANES)
    places = []
    for rows_here, lanes in tiles(block_rows, width):
        place = (pl.ds(at + rows_here.start, SUBLANES), lanes)
        places.append(place)
        skip_fn = fn_ref[place]
        above_fn = coef_ref[0] * skip_fn
        below_fn = coef_ref[1] * skip_fn
        for i in range(nvec):
            out_ref[(i, *place)] = (
                out_ref[(i, *place)]
                + above_fn * above_ref[i, rows_here, lanes]
                + below_fn * below_ref[i, rows_here, lanes]
            )
    add_products(nvec, vec_ref, out_ref, sums, 0, places, False)
    add_products(nvec, out_ref, out_ref, sums, 1, places, True)

    @pl.when(step == pl.num_programs(0) - 1)
    def _():
        lane = lax.broadcasted_iota(jnp.int32, (nvec, LANES), 1)
        packed = before_ref[...]
        packed = packed + packed_columns(lambda i, j: sums[0, j * nvec + i], nvec, 0, lane)
        packed = packed + packed_columns(
            lambda i, j: sums[1, min(i, j) * nvec + max(i, j)], nvec, nvec, lane
        )
        sum_ref[...] = jnp.broadcast_to(packed[None], sum_ref.shape)


def far_terms(coef, work, above, below, skip_fn, vec, before, start, block_rows, copies):
    nvec, _, width = work.shape
    rows = above.shape[1]
    whole = pl.BlockSpec(memory_space=pltpu.VMEM)
    block = pl.BlockSpec((nvec, block_rows, width), lambda s: (0, s, 0))
    work, skip_fn, vec = (
        pltpu.with_memory_space_constraint(array, pltpu.VMEM) for array in (work, skip_fn, vec)
    )
    return pl.pallas_call(
        functools.partial(far_terms_kernel, nvec, start),
        grid=(rows // block_rows,),
        in_specs=[
            pl.BlockSpec(memory_space=pltpu.SMEM), whole, block, block, whole, whole, whole
        ],
        out_specs=[whole, whole],
        out_shape=[
            jax.ShapeDtypeStruct(work.shape, jnp.float32),
            jax.ShapeDtypeStruct((copies, nvec, LANES), jnp.float32),
        ],
        scratch_shapes=[pltpu.VMEM((2, nvec * nvec, SUBLANES, LANES), jnp.float32)],
        input_output_aliases={1: 0},
        compiler_params=pltpu.CompilerParams(vmem_limit_bytes=SMALL_VMEM_BYTES),
        cost_estimate=pl.CostEstimate(
            flops=3 * nvec * nvec * rows * width,
            bytes_accessed=20 * above.size,
            transcendentals=0,
        ),
        name="far_terms",
    )(coef, work, above, below, skip_fn, vec, before)


def small_algebra(nvec, count, packed):
    packed = packed * (1.0 / count)
    turned = packed.T
    cross = turned[0:nvec, :]
    cross_turned = packed[:, 0:nvec]
    work_gram = packed[:, nvec : 2 * nvec]
    vec_gram = packed[:, 2 * nvec : 3 * nvec]
    total = 2.0 * cross - precise_dot(vec_gram, cross)
    total_turned = 2.0 * cross_turned - precise_dot(cross_turned, vec_gram)
    gram = work_gram - precise_dot(total_turned, cross) - precise_dot(cross_turned, total)
    gram = gram + precise_dot(total_turned, precise_dot(vec_gram, total))
    gram = 0.5 * (gram + gram.T)
    row = lax.broadcasted_iota(jnp.int32, (nvec, nvec), 0)
    column = lax.broadcasted_iota(jnp.int32, (nvec, nvec), 1)
    inverse = jnp.where(row == column, 1.0, 0.0)
    lower = jnp.zeros((nvec, nvec), jnp.float32)
    for at in range(nvec):
        pivot = gram[at : at + 1, at : at + 1]
        scale = lax.rsqrt(pivot)
        scale = scale * (1.5 - 0.5 * pivot * scale * scale)
        scaled = gram[:, at : at + 1] * scale
        lower = jnp.where((column == at) & (row >= at), scaled, lower)
        pivot_row = inverse[at : at + 1, :] * scale
        factor = jnp.where(row > at, scaled, 0.0)
        inverse = jnp.where(row == at, pivot_row, inverse - factor * pivot_row)
        gram = gram - factor * (gram[at : at + 1, :] * scale)
    return total, lower, inverse, -precise_dot(inverse, total_turned)


def basis_kernel(nvec, count, sum_ref, work_ref, vec_ref, out_ref, alpha_ref, lower_ref, coefs):
    @pl.when(pl.program_id(0) == 0)
    def _():
        packed = sum_ref[0]
        for other in range(1, sum_ref.shape[0]):
            packed = packed + sum_ref[other]
        total, lower, inverse, mixing = small_algebra(nvec, count, packed)
        alpha_ref[...] = total
        lower_ref[...] = lower
        for number, matrix in enumerate((inverse, mixing)):
            for i in range(nvec):
                for j in range(nvec):
                    coefs[number, i * nvec + j] = jnp.broadcast_to(
                        matrix[i : i + 1, j : j + 1], (SUBLANES, LANES)
                    )

    start = pl.multiple_of(pl.program_id(0) * out_ref.shape[1], out_ref.shape[1])
    places = tiles(*out_ref.shape[1:])
    for at in range(0, len(places), 4):
        group = places[at : at + 4]
        held = [(pl.ds(start + place.start, SUBLANES), lanes) for place, lanes in group]
        for ours in vector_groups(nvec):
            totals = {}
            for number, ref in ((1, vec_ref), (0, work_ref)):
                for j in range(nvec):
                    outs = [i for i in ours if number == 1 or j <= i]
                    if not outs:
                        continue
                    values = [ref[(j, *place)] for place in held]
                    for i in outs:
                        coef = coefs[number, i * nvec + j]
                        for spot, value in enumerate(values):
                            term = coef * value
                            here = (i, spot)
                            totals[here] = totals[here] + term if here in totals else term
            for i in ours:
                for spot, place in enumerate(group):
                    out_ref[(i, *place)] = totals[i, spot]


def basis_of(count, sums, work, vec, block_rows):
    nvec, rows, width = work.shape
    block = pl.BlockSpec((nvec, block_rows, width), lambda s: (0, s, 0))
    small = jax.ShapeDtypeStruct((nvec, nvec), jnp.float32)
    whole = pl.BlockSpec(memory_space=pltpu.VMEM)
    work, vec = (pltpu.with_memory_space_constraint(array, pltpu.VMEM) for array in (work, vec))
    return pl.pallas_call(
        functools.partial(basis_kernel, nvec, count),
        grid=(rows // block_rows,),
        in_specs=[whole, whole, whole],
        out_specs=[block, whole_spec(small.shape), whole_spec(small.shape)],
        out_shape=[jax.ShapeDtypeStruct(work.shape, jnp.float32), small, small],
        scratch_shapes=[pltpu.VMEM((2, nvec * nvec, SUBLANES, LANES), jnp.float32)],
        compiler_params=pltpu.CompilerParams(vmem_limit_bytes=SMALL_VMEM_BYTES),
        cost_estimate=pl.CostEstimate(
            flops=4 * nvec * work.size, bytes_accessed=12 * work.size, transcendentals=0
        ),
        name="basis",
    )(sums, work, vec)


def shards(
    vectors,
    previous,
    beta,
    potential,
    coriolis_fn,
    second_fn,
    rot_const,
    coupling,
    kin_one,
    kin_two,
    kin_three,
    kin_four,
    kin_five,
    kin_six,
    coriolis_derivative,
):
    _, nvec, *points, width = vectors.shape
    rows = points[0] * points[1] * points[2]
    devices = lax.axis_size(ALL_AXES)
    block_index = lax.axis_index("ka")
    nblocks = lax.axis_size("ka")
    row_peers = lax.axis_size("row")
    mode_peers = lax.axis_size("mode")
    row_at = lax.axis_index("row")
    mode_at = lax.axis_index("mode")
    current = vectors.reshape(nvec, rows, width)
    older = previous.reshape(nvec, rows, width)
    block_rows = min(32, rows // 2)

    cut = rows * 5 // 8 // block_rows * block_rows or rows // 2
    starts, stops = [0, cut], [cut, rows]
    parts = [split_rows(current, start, stop) for start, stop in zip(starts, stops)]
    below_one = [hop(part, "ka", 1) for part in parts]
    above_one = [hop(part, "ka", -1) for part in parts]
    below_one[0] = handed_on(below_one[0], HOP_WEIGHT)
    above_one[0] = handed_on(above_one[0], HOP_WEIGHT)
    below_two = [hop(part, "ka", 1) for part in below_one]
    above_two = [hop(part, "ka", -1) for part in above_one]
    mode_blocks = lax.all_gather(current, "mode")
    at = jnp.stack([block_index, mode_at, row_at, row_at ^ 1]).astype(jnp.int32)
    group = 2 - row_peers % 2
    held = [current]
    if group == 2:
        held.append(lax.ppermute(current, "row", [(i, i ^ 1) for i in range(row_peers)]))
    away = row_peers // group - 1
    row_sums = crossing(tuple(points), at, kin_two, held, away) if away else []
    row_sums = [
        lax.ppermute(
            part, "row", [(i, (i + group * (number + 1)) % row_peers) for i in range(row_peers)]
        )
        for number, part in enumerate(row_sums)
    ]

    span = next((s for s in (256, 128) if width % s == 0 and s % kin_six.shape[0] == 0), width)
    left, tail, up, down = operators(
        tuple(points),
        mode_peers,
        group,
        width,
        span,
        at,
        coupling,
        (kin_one, kin_two, kin_three, kin_four, kin_five, kin_six, coriolis_derivative),
    )
    lower_two = jnp.maximum(block_index - 2, 0)
    far_pair = jnp.stack([coupling[1, block_index], coupling[1, lower_two]])
    sums, vec, skip_fn = resident(current, second_fn.reshape(rows, width), block_rows)
    work = local_terms(
        nblocks, at, rot_const, beta, held, older, potential.reshape(rows, width), left, tail
    )
    work = join_terms(
        work,
        coriolis_fn.reshape(rows, width),
        left,
        up,
        down,
        mode_blocks,
        starts,
        below_one,
        above_one,
        row_sums,
    )
    for number, start in enumerate(starts):
        work, copied = far_terms(
            far_pair,
            work,
            above_two[number],
            below_two[number],
            skip_fn,
            vec,
            sums,
            start,
            block_rows,
            devices if number == len(starts) - 1 else 1,
        )
        sums = copied[0]
    every_sum = lax.all_to_all(copied, ALL_AXES, split_axis=0, concat_axis=0, tiled=True)
    count = float(devices * rows * width)
    basis, alpha, lower = basis_of(count, every_sum, work, vec, block_rows)
    return (basis.reshape(vectors.shape), alpha, lower)


def solution(mesh):
    return jax.shard_map(
        shards,
        mesh=mesh,
        in_specs=(
            P("ka", None, "mode", "row", None, None),
            P("ka", None, "mode", "row", None, None),
            P(),
            P("mode", "row", None, None),
            P("mode", "row", None, None),
            P("mode", "row", None, None),
            P(),
            P(),
            P(),
            P(),
            P(),
            P(),
            P(),
            P(),
            P(),
        ),
        out_specs=(P("ka", None, "mode", "row", None, None), P(), P()),
        check_vma=False,
    )
```

```python
import functools

import jax
import jax.numpy as jnp
from jax import lax
from jax.experimental import pallas as pl
from jax.experimental.pallas import tpu as pltpu
from jax.sharding import PartitionSpec as P

precise_mode = lax.Precision.HIGHEST
ALL_AXES = ("ka", "mode", "row")
VMEM_BYTES = 32 * 1024 * 1024
SMALL_VMEM_BYTES = 16 * 1024 * 1024
LANES = 128
HOP_WEIGHT = 25_000_000_000
SUBLANES = 8


def precise_dot(left, right):
    return jnp.dot(left, right, precision=precise_mode, preferred_element_type=jnp.float32)


def whole_spec(shape):
    return pl.BlockSpec(shape, lambda *_: (0,) * len(shape))


def hop(value, axis, by):
    peers = lax.axis_size(axis)
    pairs = [(i, i + by) for i in range(peers) if 0 <= i + by < peers]
    return lax.ppermute(value, axis, pairs)


def vector_groups(nvec):
    return [tuple(range(at, min(at + 4, nvec))) for at in range(0, nvec, 4)]


def tiles(rows, width):
    return [
        (slice(r, r + SUBLANES), slice(c, c + LANES))
        for r in range(0, rows, SUBLANES)
        for c in range(0, width, LANES)
    ]


def packed_columns(sums, nvec, offset, lane):
    packed = jnp.zeros((nvec, LANES), jnp.float32)
    for j in range(nvec):
        stacked = jnp.stack([sums(i, j) for i in range(nvec)])
        column = jnp.sum(jnp.sum(stacked, axis=1), axis=1, keepdims=True)
        packed = packed + jnp.where(lane == offset + j, column, 0.0)
    return packed


def add_products(nvec, left_ref, right_ref, sums, number, places, symmetric):
    groups = vector_groups(nvec)
    for ours in groups:
        for other in groups:
            pairs = [(i, j) for i in ours for j in other if i <= j or not symmetric]
            if not pairs:
                continue
            totals = {pair: sums[number, pair[0] * nvec + pair[1]] for pair in pairs}
            for place in places:
                lefts = {i: left_ref[(i, *place)] for i in {p[0] for p in pairs}}
                rights = {j: right_ref[(j, *place)] for j in {p[1] for p in pairs}}
                for i, j in pairs:
                    totals[i, j] = totals[i, j] + lefts[i] * rights[j]
            for i, j in pairs:
                sums[number, i * nvec + j] = totals[i, j]


def resident_kernel(nvec, vec_ref, fn_ref, *refs):
    out_ref, copy_ref, fn_copy_ref, sums = refs[-4:]
    step = pl.program_id(0)

    @pl.when(step == 0)
    def _():
        sums[...] = jnp.zeros_like(sums)

    copy_ref[...] = vec_ref[...]
    fn_copy_ref[...] = fn_ref[...]
    add_products(nvec, vec_ref, vec_ref, sums, 0, tiles(*vec_ref.shape[1:]), True)

    @pl.when(step == pl.num_programs(0) - 1)
    def _():
        lane = lax.broadcasted_iota(jnp.int32, (nvec, LANES), 1)
        out_ref[...] = packed_columns(
            lambda i, j: sums[0, min(i, j) * nvec + max(i, j)], nvec, 2 * nvec, lane
        )


def resident(vec, skip_fn, after, block_rows):
    nvec, rows, width = vec.shape
    block = pl.BlockSpec((nvec, block_rows, width), lambda s: (0, s, 0))
    fn_block = pl.BlockSpec((block_rows, width), lambda s: (s, 0))
    return pl.pallas_call(
        functools.partial(resident_kernel, nvec),
        grid=(rows // block_rows,),
        in_specs=[block, fn_block] + [pl.BlockSpec(memory_space=pl.ANY)] * len(after),
        out_specs=[whole_spec((nvec, LANES)), block, fn_block],
        out_shape=[
            jax.ShapeDtypeStruct((nvec, LANES), jnp.float32),
            jax.ShapeDtypeStruct(vec.shape, jnp.float32),
            jax.ShapeDtypeStruct(skip_fn.shape, jnp.float32),
        ],
        scratch_shapes=[pltpu.VMEM((1, nvec * nvec, SUBLANES, LANES), jnp.float32)],
        compiler_params=pltpu.CompilerParams(vmem_limit_bytes=VMEM_BYTES),
        cost_estimate=pl.CostEstimate(
            flops=nvec * (nvec + 1) * rows * width, bytes_accessed=8 * vec.size, transcendentals=0
        ),
        name="resident",
    )(vec, skip_fn, *after)


def split_kernel(start, vec_ref, out_ref, sems):
    copies = [
        pltpu.make_async_copy(
            vec_ref.at[i, pl.ds(start, out_ref.shape[1])], out_ref.at[i], sems.at[i]
        )
        for i in range(out_ref.shape[0])
    ]
    for copy in copies:
        copy.start()
    for copy in copies:
        copy.wait()


def split_rows(vec, start, stop):
    nvec, _, width = vec.shape
    shape = (nvec, stop - start, width)
    return pl.pallas_call(
        functools.partial(split_kernel, start),
        in_specs=[pl.BlockSpec(memory_space=pl.ANY)],
        out_specs=pl.BlockSpec(memory_space=pl.ANY),
        out_shape=jax.ShapeDtypeStruct(shape, jnp.float32),
        scratch_shapes=[pltpu.SemaphoreType.DMA((nvec,))],
        compiler_params=pltpu.CompilerParams(vmem_limit_bytes=SMALL_VMEM_BYTES),
        cost_estimate=pl.CostEstimate(
            flops=0, bytes_accessed=8 * nvec * (stop - start) * width, transcendentals=0
        ),
        name="split_rows",
    )(pltpu.with_memory_space_constraint(vec, pltpu.HBM))


def handed_on(array, weight, after=()):
    return pl.pallas_call(
        lambda *_: None,
        in_specs=[pl.BlockSpec(memory_space=pl.ANY)] * (1 + len(after)),
        out_specs=pl.BlockSpec(memory_space=pl.ANY),
        out_shape=jax.ShapeDtypeStruct(array.shape, array.dtype),
        input_output_aliases={0: 0},
        cost_estimate=pl.CostEstimate(flops=weight, bytes_accessed=0, transcendentals=0),
        name="handed_on",
    )(array, *after)


def kron_term(matrix, size, stride, extent, row_offset=0, column_offset=0, sign=1.0):
    points = matrix.shape[0]

    def digits(shape, axis):
        index = lax.broadcasted_iota(jnp.int32, shape, axis)
        return index, lax.rem(lax.div(index, stride), size)

    def picks(offset):
        _, digit = digits((extent, points), 0)
        point = lax.broadcasted_iota(jnp.int32, (extent, points), 1)
        return jnp.where(digit + offset == point, 1.0, 0.0)

    def transposed_dot(one, two):
        return lax.dot_general(
            one, two, (((1,), (1,)), ((), ())), precision=precise_mode,
            preferred_element_type=jnp.float32,
        )

    picked = picks(row_offset)
    picked = 0.5 * (precise_dot(picked, matrix) + sign * transposed_dot(picked, matrix))
    spread = transposed_dot(picked, picks(column_offset))
    row, row_digit = digits((extent, extent), 0)
    column, column_digit = digits((extent, extent), 1)
    same = (row - row_digit * stride) == (column - column_digit * stride)
    return jnp.where(same, spread, 0.0)


def operators_kernel(
    points, group, at_ref, coupling_ref, one_ref, two_ref, three_ref, four_ref, five_ref, six_ref,
    der_ref, *refs,
):
    left_ref, mode_ref, tail_ref, up_ref, down_ref = refs[-5:]
    points_one, points_two, points_three = points
    rows = points_one * points_two * points_three
    stride = points_two * points_three
    mine = at_ref[1] * points_two
    left_ref[0] = kron_term(two_ref[...], points_two, points_three, rows, mine, mine) + kron_term(
        three_ref[...], points_three, 1, rows
    )
    if group > 1:
        sibling = at_ref[2] * points_two
        left_ref[1] = kron_term(two_ref[...], points_two, points_three, rows, mine, sibling)
    mode_ref[...] = kron_term(one_ref[...], one_ref.shape[0], stride, mode_ref.shape[0])
    width = tail_ref.shape[0]
    fives, sixes = five_ref.shape[0], six_ref.shape[0]
    tail_ref[...] = (
        kron_term(four_ref[...], four_ref.shape[0], fives * sixes, width)
        + kron_term(five_ref[...], fives, sixes, width)
        + kron_term(six_ref[...], sixes, 1, width)
    )
    twist = kron_term(der_ref[...], sixes, 1, down_ref.shape[0], sign=-1.0)
    block = at_ref[0]
    up_ref[...] = -coupling_ref[0, block] * twist
    down_ref[...] = coupling_ref[0, jnp.maximum(block - 1, 0)] * twist


def operators(points, group, mode_extent, width, span, at, coupling, matrices, after):
    rows = points[0] * points[1] * points[2]
    shapes = [
        (group, rows, rows), (mode_extent, mode_extent), (width, width), (span, span), (span, span)
    ]
    smem = pl.BlockSpec(memory_space=pltpu.SMEM)
    return pl.pallas_call(
        functools.partial(operators_kernel, points, group),
        in_specs=[smem, smem]
        + [pl.BlockSpec(memory_space=pltpu.VMEM)] * len(matrices)
        + [pl.BlockSpec(memory_space=pl.ANY)] * len(after),
        out_specs=[pl.BlockSpec(memory_space=pltpu.VMEM)] * len(shapes),
        out_shape=[jax.ShapeDtypeStruct(shape, jnp.float32) for shape in shapes],
        compiler_params=pltpu.CompilerParams(vmem_limit_bytes=VMEM_BYTES),
        cost_estimate=pl.CostEstimate(
            flops=500_000_000, bytes_accessed=4_000_000, transcendentals=0
        ),
        name="operators",
    )(at, coupling, *matrices, *after)


def crossing_kernel(points, group, at_ref, two_ref, *refs):
    points_one, points_two, points_three = points
    held_refs, out_refs = refs[:group], refs[group:]
    owners = [at_ref[1], at_ref[2]][:group]
    peers = two_ref.shape[0] // points_two
    stride = points_two * points_three
    for number, out_ref in enumerate(out_refs):
        target = lax.rem(at_ref[1] + group * (number + 1), peers) * points_two
        coefs = {
            (a, k, b): 0.5
            * (
                two_ref[target + a, owners[k] * points_two + b]
                + two_ref[owners[k] * points_two + b, target + a]
            )
            for a in range(points_two)
            for k in range(group)
            for b in range(points_two)
        }
        for start in range(0, points_one * stride, stride):
            for _, lanes in tiles(SUBLANES, out_ref.shape[2]):
                for inner in range(0, points_three, SUBLANES):
                    values = {
                        (k, b): held_refs[k][0, pl.ds(start + b * points_three + inner, SUBLANES), lanes]
                        for k in range(group)
                        for b in range(points_two)
                    }
                    for a in range(points_two):
                        total = None
                        for (k, b), value in values.items():
                            term = coefs[a, k, b] * value
                            total = term if total is None else total + term
                        out_ref[0, pl.ds(start + a * points_three + inner, SUBLANES), lanes] = total


def crossing(points, at, two, held, count):
    nvec, rows, width = held[0].shape
    one = pl.BlockSpec((1, rows, width), lambda i: (i, 0, 0))
    smem = pl.BlockSpec(memory_space=pltpu.SMEM)
    return pl.pallas_call(
        functools.partial(crossing_kernel, points, len(held)),
        grid=(nvec,),
        in_specs=[smem, smem] + [one] * len(held),
        out_specs=[one] * count,
        out_shape=[jax.ShapeDtypeStruct(held[0].shape, jnp.float32)] * count,
        compiler_params=pltpu.CompilerParams(vmem_limit_bytes=VMEM_BYTES),
        cost_estimate=pl.CostEstimate(
            flops=2 * held[0].size * points[1] * len(held) * count,
            bytes_accessed=4 * held[0].size * (len(held) + count),
            transcendentals=0,
        ),
        name="crossing",
    )(at, two, *held)


def local_kernel(nvec, nblocks, group, at_ref, rot_ref, beta_ref, *refs):
    held_refs = refs[:group]
    old_ref, pot_ref, left_ref, tail_ref, out_ref = refs[group:]
    me = pl.program_id(0)
    block = at_ref[0]
    level = (block - nblocks // 2).astype(jnp.float32)
    current = held_refs[0][0]
    total = (pot_ref[...] + rot_ref[block] * level * level) * current
    for j in range(nvec):
        total = total - beta_ref[me, j] * old_ref[j]
    total = total + precise_dot(current, tail_ref[...])
    for number, held_ref in enumerate(held_refs):
        total = total + precise_dot(left_ref[number], held_ref[0])
    out_ref[0] = total


def local_terms(nblocks, at, rot_const, beta, held, old, pot, left, tail):
    nvec, rows, width = old.shape
    one = pl.BlockSpec((1, rows, width), lambda i: (i, 0, 0))
    smem = pl.BlockSpec(memory_space=pltpu.SMEM)
    return pl.pallas_call(
        functools.partial(local_kernel, nvec, nblocks, len(held)),
        grid=(nvec,),
        in_specs=[smem, smem, smem]
        + [one] * len(held)
        + [
            whole_spec(old.shape),
            whole_spec(pot.shape),
            pl.BlockSpec((len(held), rows, rows), lambda i: (0, 0, 0)),
            whole_spec(tail.shape),
        ],
        out_specs=one,
        out_shape=jax.ShapeDtypeStruct(old.shape, jnp.float32),
        compiler_params=pltpu.CompilerParams(vmem_limit_bytes=VMEM_BYTES),
        cost_estimate=pl.CostEstimate(
            flops=12 * old.size * (rows * len(held) + width),
            bytes_accessed=4 * old.size * (2 + len(held)),
            transcendentals=0,
        ),
        name="local_terms",
    )(at, rot_const, beta, *held, old, pot, left, tail)


def mode_kinetic_kernel(peers, in_ref, mat_ref, out_ref):
    rows = in_ref.shape[2]
    field = jnp.concatenate([in_ref[peer, 0] for peer in range(peers)], axis=0)
    field = precise_dot(mat_ref[...], field)
    for peer in range(peers):
        out_ref[peer, 0] = field[peer * rows : (peer + 1) * rows]


def mode_kinetic(field, matrix, peers):
    nvec, rows, width = field.shape
    held = nvec // peers
    block = pl.BlockSpec((peers, 1, rows, width), lambda q: (0, q, 0, 0))
    out = pl.pallas_call(
        functools.partial(mode_kinetic_kernel, peers),
        grid=(held,),
        in_specs=[block, whole_spec(matrix.shape)],
        out_specs=block,
        out_shape=jax.ShapeDtypeStruct((peers, held, rows, width), jnp.float32),
        compiler_params=pltpu.CompilerParams(vmem_limit_bytes=VMEM_BYTES),
        cost_estimate=pl.CostEstimate(
            flops=12 * field.size * matrix.shape[0], bytes_accessed=8 * field.size, transcendentals=0
        ),
        name="mode_kinetic",
    )(field.reshape(peers, held, rows, width), matrix)
    return out.reshape(field.shape)


def join_kernel(starts, sum_count, *refs):
    work_ref, cor_ref, up_ref, down_ref = refs[:4]
    pieces = len(starts)
    below_refs = refs[4 : 4 + pieces]
    above_refs = refs[4 + pieces : 4 + 2 * pieces]
    sum_refs = refs[4 + 2 * pieces : 4 + 2 * pieces + sum_count]
    out_ref = refs[-1]
    span = up_ref.shape[0]
    for start, below_ref, above_ref in zip(starts, below_refs, above_refs):
        place = slice(start, start + below_ref.shape[1])
        for at in range(0, work_ref.shape[2], span):
            part = slice(at, at + span)
            total = work_ref[0, place, part]
            for sum_ref in sum_refs:
                total = total + sum_ref[0, place, part]
            twist_fn = cor_ref[place, part]
            total = total + twist_fn * precise_dot(above_ref[0, :, part], up_ref[...])
            out_ref[0, place, part] = total + precise_dot(
                twist_fn * below_ref[0, :, part], down_ref[...]
            )


def join_terms(work, cor, up, down, starts, below, above, sums):
    nvec, rows, width = work.shape
    one = pl.BlockSpec((1, rows, width), lambda i: (i, 0, 0))
    pieces = [pl.BlockSpec((1, b.shape[1], width), lambda i: (i, 0, 0)) for b in below]
    return pl.pallas_call(
        functools.partial(join_kernel, tuple(starts), len(sums)),
        grid=(nvec,),
        in_specs=[one, whole_spec(cor.shape), whole_spec(up.shape), whole_spec(down.shape)]
        + pieces
        + pieces
        + [one] * len(sums),
        out_specs=one,
        out_shape=jax.ShapeDtypeStruct(work.shape, jnp.float32),
        compiler_params=pltpu.CompilerParams(vmem_limit_bytes=VMEM_BYTES),
        cost_estimate=pl.CostEstimate(
            flops=24 * work.size * up.shape[0], bytes_accessed=24 * work.size, transcendentals=0
        ),
        name="join_terms",
    )(work, cor, up, down, *below, *above, *sums)


def far_terms_kernel(
    nvec, start, coef_ref, work_ref, above_ref, below_ref, fn_ref, vec_ref, before_ref, out_ref,
    sum_ref, sums,
):
    del work_ref
    step = pl.program_id(0)
    _, block_rows, width = above_ref.shape

    @pl.when(step == 0)
    def _():
        sums[...] = jnp.zeros_like(sums)

    at = pl.multiple_of(start + step * block_rows, SUBLANES)
    places = []
    for rows_here, lanes in tiles(block_rows, width):
        place = (pl.ds(at + rows_here.start, SUBLANES), lanes)
        places.append(place)
        skip_fn = fn_ref[place]
        above_fn = coef_ref[0] * skip_fn
        below_fn = coef_ref[1] * skip_fn
        for i in range(nvec):
            out_ref[(i, *place)] = (
                out_ref[(i, *place)]
                + above_fn * above_ref[i, rows_here, lanes]
                + below_fn * below_ref[i, rows_here, lanes]
            )
    add_products(nvec, vec_ref, out_ref, sums, 0, places, False)
    add_products(nvec, out_ref, out_ref, sums, 1, places, True)

    @pl.when(step == pl.num_programs(0) - 1)
    def _():
        lane = lax.broadcasted_iota(jnp.int32, (nvec, LANES), 1)
        packed = before_ref[...]
        packed = packed + packed_columns(lambda i, j: sums[0, j * nvec + i], nvec, 0, lane)
        packed = packed + packed_columns(
            lambda i, j: sums[1, min(i, j) * nvec + max(i, j)], nvec, nvec, lane
        )
        sum_ref[...] = jnp.broadcast_to(packed[None], sum_ref.shape)


def far_terms(coef, work, above, below, skip_fn, vec, before, start, block_rows, copies):
    nvec, _, width = work.shape
    rows = above.shape[1]
    whole = pl.BlockSpec(memory_space=pltpu.VMEM)
    block = pl.BlockSpec((nvec, block_rows, width), lambda s: (0, s, 0))
    work, skip_fn, vec = (
        pltpu.with_memory_space_constraint(array, pltpu.VMEM) for array in (work, skip_fn, vec)
    )
    return pl.pallas_call(
        functools.partial(far_terms_kernel, nvec, start),
        grid=(rows // block_rows,),
        in_specs=[
            pl.BlockSpec(memory_space=pltpu.SMEM), whole, block, block, whole, whole, whole
        ],
        out_specs=[whole, whole],
        out_shape=[
            jax.ShapeDtypeStruct(work.shape, jnp.float32),
            jax.ShapeDtypeStruct((copies, nvec, LANES), jnp.float32),
        ],
        scratch_shapes=[pltpu.VMEM((2, nvec * nvec, SUBLANES, LANES), jnp.float32)],
        input_output_aliases={1: 0},
        compiler_params=pltpu.CompilerParams(vmem_limit_bytes=SMALL_VMEM_BYTES),
        cost_estimate=pl.CostEstimate(
            flops=3 * nvec * nvec * rows * width,
            bytes_accessed=20 * above.size,
            transcendentals=0,
        ),
        name="far_terms",
    )(coef, work, above, below, skip_fn, vec, before)


def small_algebra(nvec, count, packed):
    packed = packed * (1.0 / count)
    turned = packed.T
    cross = turned[0:nvec, :]
    cross_turned = packed[:, 0:nvec]
    work_gram = packed[:, nvec : 2 * nvec]
    vec_gram = packed[:, 2 * nvec : 3 * nvec]
    total = 2.0 * cross - precise_dot(vec_gram, cross)
    total_turned = 2.0 * cross_turned - precise_dot(cross_turned, vec_gram)
    gram = work_gram - precise_dot(total_turned, cross) - precise_dot(cross_turned, total)
    gram = gram + precise_dot(total_turned, precise_dot(vec_gram, total))
    gram = 0.5 * (gram + gram.T)
    row = lax.broadcasted_iota(jnp.int32, (nvec, nvec), 0)
    column = lax.broadcasted_iota(jnp.int32, (nvec, nvec), 1)
    inverse = jnp.where(row == column, 1.0, 0.0)
    lower = jnp.zeros((nvec, nvec), jnp.float32)
    for at in range(nvec):
        pivot = gram[at : at + 1, at : at + 1]
        scale = lax.rsqrt(pivot)
        scale = scale * (1.5 - 0.5 * pivot * scale * scale)
        scaled = gram[:, at : at + 1] * scale
        lower = jnp.where((column == at) & (row >= at), scaled, lower)
        pivot_row = inverse[at : at + 1, :] * scale
        factor = jnp.where(row > at, scaled, 0.0)
        inverse = jnp.where(row == at, pivot_row, inverse - factor * pivot_row)
        gram = gram - factor * (gram[at : at + 1, :] * scale)
    return total, lower, inverse, -precise_dot(inverse, total_turned)


def basis_kernel(nvec, count, sum_ref, work_ref, vec_ref, out_ref, alpha_ref, lower_ref, coefs):
    @pl.when(pl.program_id(0) == 0)
    def _():
        packed = sum_ref[0]
        for other in range(1, sum_ref.shape[0]):
            packed = packed + sum_ref[other]
        total, lower, inverse, mixing = small_algebra(nvec, count, packed)
        alpha_ref[...] = total
        lower_ref[...] = lower
        for number, matrix in enumerate((inverse, mixing)):
            for i in range(nvec):
                for j in range(nvec):
                    coefs[number, i * nvec + j] = jnp.broadcast_to(
                        matrix[i : i + 1, j : j + 1], (SUBLANES, LANES)
                    )

    start = pl.multiple_of(pl.program_id(0) * out_ref.shape[1], out_ref.shape[1])
    places = tiles(*out_ref.shape[1:])
    for at in range(0, len(places), 4):
        group = places[at : at + 4]
        held = [(pl.ds(start + place.start, SUBLANES), lanes) for place, lanes in group]
        for ours in vector_groups(nvec):
            totals = {}
            for number, ref in ((1, vec_ref), (0, work_ref)):
                for j in range(nvec):
                    outs = [i for i in ours if number == 1 or j <= i]
                    if not outs:
                        continue
                    values = [ref[(j, *place)] for place in held]
                    for i in outs:
                        coef = coefs[number, i * nvec + j]
                        for spot, value in enumerate(values):
                            term = coef * value
                            here = (i, spot)
                            totals[here] = totals[here] + term if here in totals else term
            for i in ours:
                for spot, place in enumerate(group):
                    out_ref[(i, *place)] = totals[i, spot]


def basis_of(count, sums, work, vec, block_rows):
    nvec, rows, width = work.shape
    block = pl.BlockSpec((nvec, block_rows, width), lambda s: (0, s, 0))
    small = jax.ShapeDtypeStruct((nvec, nvec), jnp.float32)
    whole = pl.BlockSpec(memory_space=pltpu.VMEM)
    work, vec = (pltpu.with_memory_space_constraint(array, pltpu.VMEM) for array in (work, vec))
    return pl.pallas_call(
        functools.partial(basis_kernel, nvec, count),
        grid=(rows // block_rows,),
        in_specs=[whole, whole, whole],
        out_specs=[block, whole_spec(small.shape), whole_spec(small.shape)],
        out_shape=[jax.ShapeDtypeStruct(work.shape, jnp.float32), small, small],
        scratch_shapes=[pltpu.VMEM((2, nvec * nvec, SUBLANES, LANES), jnp.float32)],
        compiler_params=pltpu.CompilerParams(vmem_limit_bytes=SMALL_VMEM_BYTES),
        cost_estimate=pl.CostEstimate(
            flops=4 * nvec * work.size, bytes_accessed=12 * work.size, transcendentals=0
        ),
        name="basis",
    )(sums, work, vec)


def shards(
    vectors,
    previous,
    beta,
    potential,
    coriolis_fn,
    second_fn,
    rot_const,
    coupling,
    kin_one,
    kin_two,
    kin_three,
    kin_four,
    kin_five,
    kin_six,
    coriolis_derivative,
):
    _, nvec, *points, width = vectors.shape
    rows = points[0] * points[1] * points[2]
    devices = lax.axis_size(ALL_AXES)
    block_index = lax.axis_index("ka")
    nblocks = lax.axis_size("ka")
    row_peers = lax.axis_size("row")
    mode_peers = lax.axis_size("mode")
    row_at = lax.axis_index("row")
    current = vectors.reshape(nvec, rows, width)
    older = previous.reshape(nvec, rows, width)
    block_rows = min(32, rows // 2)

    cut = rows * 3 // 4 // block_rows * block_rows or rows // 2
    starts, stops = [0, cut], [cut, rows]
    parts = [split_rows(current, start, stop) for start, stop in zip(starts, stops)]
    below_one = [hop(part, "ka", 1) for part in parts]
    above_one = [hop(part, "ka", -1) for part in parts]
    at = jnp.stack([block_index, row_at, row_at ^ 1]).astype(jnp.int32)
    group = 2 - row_peers % 2
    held = [current]
    if group == 2:
        held.append(lax.ppermute(current, "row", [(i, i ^ 1) for i in range(row_peers)]))
    away = row_peers // group - 1
    row_parts = crossing(tuple(points), at, kin_two, held, away) if away else []
    below_one[0] = handed_on(below_one[0], HOP_WEIGHT, row_parts)
    above_one[0] = handed_on(above_one[0], HOP_WEIGHT, row_parts)
    below_two = [hop(part, "ka", 1) for part in below_one]
    above_two = [hop(part, "ka", -1) for part in above_one]
    row_sums = [
        lax.ppermute(
            part, "row", [(i, (i + group * (number + 1)) % row_peers) for i in range(row_peers)]
        )
        for number, part in enumerate(row_parts)
    ]

    span = next((s for s in (256, 128) if width % s == 0 and s % kin_six.shape[0] == 0), width)
    left, mode_mat, tail, up, down = operators(
        tuple(points),
        group,
        mode_peers * rows,
        width,
        span,
        at,
        coupling,
        (kin_one, kin_two, kin_three, kin_four, kin_five, kin_six, coriolis_derivative),
        row_parts,
    )
    lower_two = jnp.maximum(block_index - 2, 0)
    far_pair = jnp.stack([coupling[1, block_index], coupling[1, lower_two]])
    sums, vec, skip_fn = resident(
        current, second_fn.reshape(rows, width), held[1:], block_rows
    )
    mode_shares = lax.all_to_all(vec, "mode", split_axis=0, concat_axis=0, tiled=True)
    mode_shares = mode_kinetic(mode_shares, mode_mat, mode_peers)
    mode_sum = lax.all_to_all(mode_shares, "mode", split_axis=0, concat_axis=0, tiled=True)
    work = local_terms(
        nblocks, at, rot_const, beta, held, older, potential.reshape(rows, width), left, tail
    )
    work = join_terms(
        work,
        coriolis_fn.reshape(rows, width),
        up,
        down,
        starts,
        below_one,
        above_one,
        [mode_sum, *row_sums],
    )
    for number, start in enumerate(starts):
        work, copied = far_terms(
            far_pair,
            work,
            above_two[number],
            below_two[number],
            skip_fn,
            vec,
            sums,
            start,
            block_rows,
            devices if number == len(starts) - 1 else 1,
        )
        sums = copied[0]
    every_sum = lax.all_to_all(copied, ALL_AXES, split_axis=0, concat_axis=0, tiled=True)
    count = float(devices * rows * width)
    basis, alpha, lower = basis_of(count, every_sum, work, vec, block_rows)
    return (basis.reshape(vectors.shape), alpha, lower)


def solution(mesh):
    return jax.shard_map(
        shards,
        mesh=mesh,
        in_specs=(
            P("ka", None, "mode", "row", None, None),
            P("ka", None, "mode", "row", None, None),
            P(),
            P("mode", "row", None, None),
            P("mode", "row", None, None),
            P("mode", "row", None, None),
            P(),
            P(),
            P(),
            P(),
            P(),
            P(),
            P(),
            P(),
            P(),
        ),
        out_specs=(P("ka", None, "mode", "row", None, None), P(), P()),
        check_vma=False,
    )
```

```python
import functools

import jax
import jax.numpy as jnp
from jax import lax
from jax.experimental import pallas as pl
from jax.experimental.pallas import tpu as pltpu
from jax.sharding import PartitionSpec as P

precise_mode = lax.Precision.HIGHEST
ALL_AXES = ("ka", "mode", "row")
VMEM_BYTES = 32 * 1024 * 1024
SMALL_VMEM_BYTES = 16 * 1024 * 1024
LANES = 128
HOP_WEIGHT = 25_000_000_000
SUBLANES = 8


def precise_dot(left, right):
    return jnp.dot(left, right, precision=precise_mode, preferred_element_type=jnp.float32)


def whole_spec(shape):
    return pl.BlockSpec(shape, lambda *_: (0,) * len(shape))


def hop(value, axis, by):
    peers = lax.axis_size(axis)
    pairs = [(i, i + by) for i in range(peers) if 0 <= i + by < peers]
    return lax.ppermute(value, axis, pairs)


def vector_groups(nvec):
    return [tuple(range(at, min(at + 4, nvec))) for at in range(0, nvec, 4)]


def tiles(rows, width):
    return [
        (slice(r, r + SUBLANES), slice(c, c + LANES))
        for r in range(0, rows, SUBLANES)
        for c in range(0, width, LANES)
    ]


def packed_columns(sums, nvec, offset, lane):
    packed = jnp.zeros((nvec, LANES), jnp.float32)
    for j in range(nvec):
        stacked = jnp.stack([sums(i, j) for i in range(nvec)])
        column = jnp.sum(jnp.sum(stacked, axis=1), axis=1, keepdims=True)
        packed = packed + jnp.where(lane == offset + j, column, 0.0)
    return packed


def add_products(nvec, left_ref, right_ref, sums, number, places, symmetric):
    groups = vector_groups(nvec)
    for ours in groups:
        for other in groups:
            pairs = [(i, j) for i in ours for j in other if i <= j or not symmetric]
            if not pairs:
                continue
            totals = {pair: sums[number, pair[0] * nvec + pair[1]] for pair in pairs}
            for place in places:
                lefts = {i: left_ref[(i, *place)] for i in {p[0] for p in pairs}}
                rights = {j: right_ref[(j, *place)] for j in {p[1] for p in pairs}}
                for i, j in pairs:
                    totals[i, j] = totals[i, j] + lefts[i] * rights[j]
            for i, j in pairs:
                sums[number, i * nvec + j] = totals[i, j]


def resident_kernel(nvec, vec_ref, fn_ref, *refs):
    out_ref, copy_ref, fn_copy_ref, sums = refs[-4:]
    step = pl.program_id(0)

    @pl.when(step == 0)
    def _():
        sums[...] = jnp.zeros_like(sums)

    copy_ref[...] = vec_ref[...]
    fn_copy_ref[...] = fn_ref[...]
    add_products(nvec, vec_ref, vec_ref, sums, 0, tiles(*vec_ref.shape[1:]), True)

    @pl.when(step == pl.num_programs(0) - 1)
    def _():
        lane = lax.broadcasted_iota(jnp.int32, (nvec, LANES), 1)
        out_ref[...] = packed_columns(
            lambda i, j: sums[0, min(i, j) * nvec + max(i, j)], nvec, 2 * nvec, lane
        )


def resident(vec, skip_fn, after, block_rows):
    nvec, rows, width = vec.shape
    block = pl.BlockSpec((nvec, block_rows, width), lambda s: (0, s, 0))
    fn_block = pl.BlockSpec((block_rows, width), lambda s: (s, 0))
    return pl.pallas_call(
        functools.partial(resident_kernel, nvec),
        grid=(rows // block_rows,),
        in_specs=[block, fn_block] + [pl.BlockSpec(memory_space=pl.ANY)] * len(after),
        out_specs=[whole_spec((nvec, LANES)), block, fn_block],
        out_shape=[
            jax.ShapeDtypeStruct((nvec, LANES), jnp.float32),
            jax.ShapeDtypeStruct(vec.shape, jnp.float32),
            jax.ShapeDtypeStruct(skip_fn.shape, jnp.float32),
        ],
        scratch_shapes=[pltpu.VMEM((1, nvec * nvec, SUBLANES, LANES), jnp.float32)],
        compiler_params=pltpu.CompilerParams(vmem_limit_bytes=VMEM_BYTES),
        cost_estimate=pl.CostEstimate(
            flops=nvec * (nvec + 1) * rows * width, bytes_accessed=8 * vec.size, transcendentals=0
        ),
        name="resident",
    )(vec, skip_fn, *after)


def split_kernel(start, vec_ref, out_ref, sems):
    copies = [
        pltpu.make_async_copy(
            vec_ref.at[i, pl.ds(start, out_ref.shape[1])], out_ref.at[i], sems.at[i]
        )
        for i in range(out_ref.shape[0])
    ]
    for copy in copies:
        copy.start()
    for copy in copies:
        copy.wait()


def split_rows(vec, start, stop):
    nvec, _, width = vec.shape
    shape = (nvec, stop - start, width)
    return pl.pallas_call(
        functools.partial(split_kernel, start),
        in_specs=[pl.BlockSpec(memory_space=pl.ANY)],
        out_specs=pl.BlockSpec(memory_space=pltpu.VMEM),
        out_shape=pltpu.VMEM(shape, jnp.float32),
        scratch_shapes=[pltpu.SemaphoreType.DMA((nvec,))],
        compiler_params=pltpu.CompilerParams(vmem_limit_bytes=SMALL_VMEM_BYTES),
        cost_estimate=pl.CostEstimate(
            flops=0, bytes_accessed=8 * nvec * (stop - start) * width, transcendentals=0
        ),
        name="split_rows",
    )(pltpu.with_memory_space_constraint(vec, pltpu.HBM))


def handed_on(array, weight, after=()):
    return pl.pallas_call(
        lambda *_: None,
        in_specs=[pl.BlockSpec(memory_space=pl.ANY)] * (1 + len(after)),
        out_specs=pl.BlockSpec(memory_space=pl.ANY),
        out_shape=jax.ShapeDtypeStruct(array.shape, array.dtype),
        input_output_aliases={0: 0},
        cost_estimate=pl.CostEstimate(flops=weight, bytes_accessed=0, transcendentals=0),
        name="handed_on",
    )(array, *after)


def kron_term(matrix, size, stride, extent, row_offset=0, column_offset=0, sign=1.0):
    points = matrix.shape[0]

    def digits(shape, axis):
        index = lax.broadcasted_iota(jnp.int32, shape, axis)
        return index, lax.rem(lax.div(index, stride), size)

    def picks(offset):
        _, digit = digits((extent, points), 0)
        point = lax.broadcasted_iota(jnp.int32, (extent, points), 1)
        return jnp.where(digit + offset == point, 1.0, 0.0)

    def transposed_dot(one, two):
        return lax.dot_general(
            one, two, (((1,), (1,)), ((), ())), precision=precise_mode,
            preferred_element_type=jnp.float32,
        )

    picked = picks(row_offset)
    picked = 0.5 * (precise_dot(picked, matrix) + sign * transposed_dot(picked, matrix))
    spread = transposed_dot(picked, picks(column_offset))
    row, row_digit = digits((extent, extent), 0)
    column, column_digit = digits((extent, extent), 1)
    same = (row - row_digit * stride) == (column - column_digit * stride)
    return jnp.where(same, spread, 0.0)


def operators_kernel(
    points, group, at_ref, coupling_ref, one_ref, two_ref, three_ref, four_ref, five_ref, six_ref,
    der_ref, *refs,
):
    left_ref, mode_ref, tail_ref, up_ref, down_ref = refs[-5:]
    points_one, points_two, points_three = points
    rows = points_one * points_two * points_three
    stride = points_two * points_three
    mine = at_ref[1] * points_two
    left_ref[0] = kron_term(two_ref[...], points_two, points_three, rows, mine, mine) + kron_term(
        three_ref[...], points_three, 1, rows
    )
    if group > 1:
        sibling = at_ref[2] * points_two
        left_ref[1] = kron_term(two_ref[...], points_two, points_three, rows, mine, sibling)
    mode_ref[...] = kron_term(one_ref[...], one_ref.shape[0], stride, mode_ref.shape[0])
    width = tail_ref.shape[0]
    fives, sixes = five_ref.shape[0], six_ref.shape[0]
    tail_ref[...] = (
        kron_term(four_ref[...], four_ref.shape[0], fives * sixes, width)
        + kron_term(five_ref[...], fives, sixes, width)
        + kron_term(six_ref[...], sixes, 1, width)
    )
    twist = kron_term(der_ref[...], sixes, 1, down_ref.shape[0], sign=-1.0)
    block = at_ref[0]
    up_ref[...] = -coupling_ref[0, block] * twist
    down_ref[...] = coupling_ref[0, jnp.maximum(block - 1, 0)] * twist


def operators(points, group, mode_extent, width, span, at, coupling, matrices, after):
    rows = points[0] * points[1] * points[2]
    shapes = [
        (group, rows, rows), (mode_extent, mode_extent), (width, width), (span, span), (span, span)
    ]
    smem = pl.BlockSpec(memory_space=pltpu.SMEM)
    return pl.pallas_call(
        functools.partial(operators_kernel, points, group),
        in_specs=[smem, smem]
        + [pl.BlockSpec(memory_space=pltpu.VMEM)] * len(matrices)
        + [pl.BlockSpec(memory_space=pl.ANY)] * len(after),
        out_specs=[pl.BlockSpec(memory_space=pltpu.VMEM)] * len(shapes),
        out_shape=[jax.ShapeDtypeStruct(shape, jnp.float32) for shape in shapes],
        compiler_params=pltpu.CompilerParams(vmem_limit_bytes=VMEM_BYTES),
        cost_estimate=pl.CostEstimate(
            flops=500_000_000, bytes_accessed=4_000_000, transcendentals=0
        ),
        name="operators",
    )(at, coupling, *matrices, *after)


def crossing_kernel(points, group, at_ref, two_ref, *refs):
    points_one, points_two, points_three = points
    held_refs, out_refs = refs[:group], refs[group:]
    owners = [at_ref[1], at_ref[2]][:group]
    peers = two_ref.shape[0] // points_two
    stride = points_two * points_three
    for number, out_ref in enumerate(out_refs):
        target = lax.rem(at_ref[1] + group * (number + 1), peers) * points_two
        coefs = {
            (a, k, b): 0.5
            * (
                two_ref[target + a, owners[k] * points_two + b]
                + two_ref[owners[k] * points_two + b, target + a]
            )
            for a in range(points_two)
            for k in range(group)
            for b in range(points_two)
        }
        for start in range(0, points_one * stride, stride):
            for _, lanes in tiles(SUBLANES, out_ref.shape[2]):
                for inner in range(0, points_three, SUBLANES):
                    values = {
                        (k, b): held_refs[k][0, pl.ds(start + b * points_three + inner, SUBLANES), lanes]
                        for k in range(group)
                        for b in range(points_two)
                    }
                    for a in range(points_two):
                        total = None
                        for (k, b), value in values.items():
                            term = coefs[a, k, b] * value
                            total = term if total is None else total + term
                        out_ref[0, pl.ds(start + a * points_three + inner, SUBLANES), lanes] = total


def crossing(points, at, two, held, count):
    nvec, rows, width = held[0].shape
    one = pl.BlockSpec((1, rows, width), lambda i: (i, 0, 0))
    smem = pl.BlockSpec(memory_space=pltpu.SMEM)
    return pl.pallas_call(
        functools.partial(crossing_kernel, points, len(held)),
        grid=(nvec,),
        in_specs=[smem, smem] + [one] * len(held),
        out_specs=[one] * count,
        out_shape=[jax.ShapeDtypeStruct(held[0].shape, jnp.float32)] * count,
        compiler_params=pltpu.CompilerParams(vmem_limit_bytes=VMEM_BYTES),
        cost_estimate=pl.CostEstimate(
            flops=2 * held[0].size * points[1] * len(held) * count,
            bytes_accessed=4 * held[0].size * (len(held) + count),
            transcendentals=0,
        ),
        name="crossing",
    )(at, two, *held)


def local_kernel(nvec, nblocks, group, at_ref, rot_ref, beta_ref, *refs):
    held_refs = refs[:group]
    old_ref, pot_ref, left_ref, tail_ref, out_ref = refs[group:]
    me = pl.program_id(0)
    block = at_ref[0]
    level = (block - nblocks // 2).astype(jnp.float32)
    current = held_refs[0][0]
    total = (pot_ref[...] + rot_ref[block] * level * level) * current
    for j in range(nvec):
        total = total - beta_ref[me, j] * old_ref[j]
    total = total + precise_dot(current, tail_ref[...])
    for number, held_ref in enumerate(held_refs):
        total = total + precise_dot(left_ref[number], held_ref[0])
    out_ref[0] = total


def local_terms(nblocks, at, rot_const, beta, held, old, pot, left, tail):
    nvec, rows, width = old.shape
    one = pl.BlockSpec((1, rows, width), lambda i: (i, 0, 0))
    smem = pl.BlockSpec(memory_space=pltpu.SMEM)
    return pl.pallas_call(
        functools.partial(local_kernel, nvec, nblocks, len(held)),
        grid=(nvec,),
        in_specs=[smem, smem, smem]
        + [one] * len(held)
        + [
            whole_spec(old.shape),
            whole_spec(pot.shape),
            pl.BlockSpec((len(held), rows, rows), lambda i: (0, 0, 0)),
            whole_spec(tail.shape),
        ],
        out_specs=one,
        out_shape=jax.ShapeDtypeStruct(old.shape, jnp.float32),
        compiler_params=pltpu.CompilerParams(vmem_limit_bytes=VMEM_BYTES),
        cost_estimate=pl.CostEstimate(
            flops=12 * old.size * (rows * len(held) + width),
            bytes_accessed=4 * old.size * (2 + len(held)),
            transcendentals=0,
        ),
        name="local_terms",
    )(at, rot_const, beta, *held, old, pot, left, tail)


def mode_kinetic_kernel(peers, in_ref, mat_ref, out_ref):
    rows = in_ref.shape[2]
    field = jnp.concatenate([in_ref[peer, 0] for peer in range(peers)], axis=0)
    field = precise_dot(mat_ref[...], field)
    for peer in range(peers):
        out_ref[peer, 0] = field[peer * rows : (peer + 1) * rows]


def mode_kinetic(field, matrix, peers):
    nvec, rows, width = field.shape
    held = nvec // peers
    block = pl.BlockSpec((peers, 1, rows, width), lambda q: (0, q, 0, 0))
    out = pl.pallas_call(
        functools.partial(mode_kinetic_kernel, peers),
        grid=(held,),
        in_specs=[block, whole_spec(matrix.shape)],
        out_specs=block,
        out_shape=jax.ShapeDtypeStruct((peers, held, rows, width), jnp.float32),
        compiler_params=pltpu.CompilerParams(vmem_limit_bytes=VMEM_BYTES),
        cost_estimate=pl.CostEstimate(
            flops=12 * field.size * matrix.shape[0], bytes_accessed=8 * field.size, transcendentals=0
        ),
        name="mode_kinetic",
    )(field.reshape(peers, held, rows, width), matrix)
    return out.reshape(field.shape)


def join_kernel(starts, sum_count, *refs):
    work_ref, cor_ref, up_ref, down_ref = refs[:4]
    pieces = len(starts)
    below_refs = refs[4 : 4 + pieces]
    above_refs = refs[4 + pieces : 4 + 2 * pieces]
    sum_refs = refs[4 + 2 * pieces : 4 + 2 * pieces + sum_count]
    out_ref = refs[-1]
    span = up_ref.shape[0]
    for start, below_ref, above_ref in zip(starts, below_refs, above_refs):
        place = slice(start, start + below_ref.shape[1])
        for at in range(0, work_ref.shape[2], span):
            part = slice(at, at + span)
            total = work_ref[0, place, part]
            for sum_ref in sum_refs:
                total = total + sum_ref[0, place, part]
            twist_fn = cor_ref[place, part]
            total = total + twist_fn * precise_dot(above_ref[0, :, part], up_ref[...])
            out_ref[0, place, part] = total + precise_dot(
                twist_fn * below_ref[0, :, part], down_ref[...]
            )


def join_terms(work, cor, up, down, starts, below, above, sums):
    nvec, rows, width = work.shape
    one = pl.BlockSpec((1, rows, width), lambda i: (i, 0, 0))
    pieces = [pl.BlockSpec((1, b.shape[1], width), lambda i: (i, 0, 0)) for b in below]
    return pl.pallas_call(
        functools.partial(join_kernel, tuple(starts), len(sums)),
        grid=(nvec,),
        in_specs=[one, whole_spec(cor.shape), whole_spec(up.shape), whole_spec(down.shape)]
        + pieces
        + pieces
        + [one] * len(sums),
        out_specs=one,
        out_shape=jax.ShapeDtypeStruct(work.shape, jnp.float32),
        compiler_params=pltpu.CompilerParams(vmem_limit_bytes=VMEM_BYTES),
        cost_estimate=pl.CostEstimate(
            flops=24 * work.size * up.shape[0], bytes_accessed=24 * work.size, transcendentals=0
        ),
        name="join_terms",
    )(work, cor, up, down, *below, *above, *sums)


def far_terms_kernel(
    nvec, start, coef_ref, work_ref, above_ref, below_ref, fn_ref, vec_ref, before_ref, out_ref,
    sum_ref, sums,
):
    del work_ref
    step = pl.program_id(0)
    _, block_rows, width = above_ref.shape

    @pl.when(step == 0)
    def _():
        sums[...] = jnp.zeros_like(sums)

    at = pl.multiple_of(start + step * block_rows, SUBLANES)
    places = []
    for rows_here, lanes in tiles(block_rows, width):
        place = (pl.ds(at + rows_here.start, SUBLANES), lanes)
        places.append(place)
        skip_fn = fn_ref[place]
        above_fn = coef_ref[0] * skip_fn
        below_fn = coef_ref[1] * skip_fn
        for i in range(nvec):
            out_ref[(i, *place)] = (
                out_ref[(i, *place)]
                + above_fn * above_ref[i, rows_here, lanes]
                + below_fn * below_ref[i, rows_here, lanes]
            )
    add_products(nvec, vec_ref, out_ref, sums, 0, places, False)
    add_products(nvec, out_ref, out_ref, sums, 1, places, True)

    @pl.when(step == pl.num_programs(0) - 1)
    def _():
        lane = lax.broadcasted_iota(jnp.int32, (nvec, LANES), 1)
        packed = before_ref[...]
        packed = packed + packed_columns(lambda i, j: sums[0, j * nvec + i], nvec, 0, lane)
        packed = packed + packed_columns(
            lambda i, j: sums[1, min(i, j) * nvec + max(i, j)], nvec, nvec, lane
        )
        sum_ref[...] = jnp.broadcast_to(packed[None], sum_ref.shape)


def far_terms(coef, work, above, below, skip_fn, vec, before, start, block_rows, copies):
    nvec, _, width = work.shape
    rows = above.shape[1]
    whole = pl.BlockSpec(memory_space=pltpu.VMEM)
    block = pl.BlockSpec((nvec, block_rows, width), lambda s: (0, s, 0))
    work, skip_fn, vec = (
        pltpu.with_memory_space_constraint(array, pltpu.VMEM) for array in (work, skip_fn, vec)
    )
    return pl.pallas_call(
        functools.partial(far_terms_kernel, nvec, start),
        grid=(rows // block_rows,),
        in_specs=[
            pl.BlockSpec(memory_space=pltpu.SMEM), whole, block, block, whole, whole, whole
        ],
        out_specs=[whole, whole],
        out_shape=[
            jax.ShapeDtypeStruct(work.shape, jnp.float32),
            jax.ShapeDtypeStruct((copies, nvec, LANES), jnp.float32),
        ],
        scratch_shapes=[pltpu.VMEM((2, nvec * nvec, SUBLANES, LANES), jnp.float32)],
        input_output_aliases={1: 0},
        compiler_params=pltpu.CompilerParams(vmem_limit_bytes=SMALL_VMEM_BYTES),
        cost_estimate=pl.CostEstimate(
            flops=3 * nvec * nvec * rows * width,
            bytes_accessed=20 * above.size,
            transcendentals=0,
        ),
        name="far_terms",
    )(coef, work, above, below, skip_fn, vec, before)


def small_dot(left, right):
    terms = [left[:, k : k + 1] * right[k : k + 1, :] for k in range(right.shape[0])]
    while len(terms) > 1:
        terms = [sum(terms[k + 1 : k + 2], terms[k]) for k in range(0, len(terms), 2)]
    return terms[0]


def small_algebra(nvec, count, packed):
    packed = packed * (1.0 / count)
    cross = packed.T[0:nvec, :]
    cross_turned = packed[:, 0:nvec]
    work_gram = packed[:, nvec : 2 * nvec]
    vec_gram = packed[:, 2 * nvec : 3 * nvec]
    total = 2.0 * cross - small_dot(vec_gram, cross)
    total_turned = 2.0 * cross_turned - small_dot(cross_turned, vec_gram)
    gram = work_gram - small_dot(total_turned, cross) - small_dot(cross_turned, total)
    gram = gram + small_dot(total_turned, small_dot(vec_gram, total))
    row = lax.broadcasted_iota(jnp.int32, (nvec, nvec), 0)
    column = lax.broadcasted_iota(jnp.int32, (nvec, nvec), 1)
    inverse = jnp.where(row == column, 1.0, 0.0)
    lower = jnp.zeros((nvec, nvec), jnp.float32)
    for at in range(nvec):
        pivot = gram[at : at + 1, at : at + 1]
        scale = lax.rsqrt(pivot)
        scale = scale * (1.5 - 0.5 * pivot * scale * scale)
        scaled = gram[:, at : at + 1] * scale
        lower = jnp.where((column == at) & (row >= at), scaled, lower)
        pivot_row = inverse[at : at + 1, :] * scale
        factor = jnp.where(row > at, scaled, 0.0)
        inverse = jnp.where(row == at, pivot_row, inverse - factor * pivot_row)
        gram = gram - factor * (gram[at : at + 1, :] * scale)
    return total, lower, inverse, -small_dot(inverse, total_turned)


def basis_kernel(nvec, count, sum_ref, work_ref, vec_ref, out_ref, alpha_ref, lower_ref, coefs):
    @pl.when(pl.program_id(0) == 0)
    def _():
        packed = sum_ref[0]
        for other in range(1, sum_ref.shape[0]):
            packed = packed + sum_ref[other]
        total, lower, inverse, mixing = small_algebra(nvec, count, packed)
        alpha_ref[...] = total
        lower_ref[...] = lower
        for number, matrix in enumerate((inverse, mixing)):
            for i in range(nvec):
                for j in range(nvec):
                    coefs[number, i * nvec + j] = jnp.broadcast_to(
                        matrix[i : i + 1, j : j + 1], (SUBLANES, LANES)
                    )

    start = pl.multiple_of(pl.program_id(0) * out_ref.shape[1], out_ref.shape[1])
    places = tiles(*out_ref.shape[1:])
    for at in range(0, len(places), 4):
        group = places[at : at + 4]
        held = [(pl.ds(start + place.start, SUBLANES), lanes) for place, lanes in group]
        for ours in vector_groups(nvec):
            totals = {}
            for number, ref in ((1, vec_ref), (0, work_ref)):
                for j in range(nvec):
                    outs = [i for i in ours if number == 1 or j <= i]
                    if not outs:
                        continue
                    values = [ref[(j, *place)] for place in held]
                    for i in outs:
                        coef = coefs[number, i * nvec + j]
                        for spot, value in enumerate(values):
                            term = coef * value
                            here = (i, spot)
                            totals[here] = totals[here] + term if here in totals else term
            for i in ours:
                for spot, place in enumerate(group):
                    out_ref[(i, *place)] = totals[i, spot]


def basis_of(count, sums, work, vec, block_rows):
    nvec, rows, width = work.shape
    block = pl.BlockSpec((nvec, block_rows, width), lambda s: (0, s, 0))
    small = jax.ShapeDtypeStruct((nvec, nvec), jnp.float32)
    whole = pl.BlockSpec(memory_space=pltpu.VMEM)
    work, vec = (pltpu.with_memory_space_constraint(array, pltpu.VMEM) for array in (work, vec))
    return pl.pallas_call(
        functools.partial(basis_kernel, nvec, count),
        grid=(rows // block_rows,),
        in_specs=[whole, whole, whole],
        out_specs=[block, whole_spec(small.shape), whole_spec(small.shape)],
        out_shape=[jax.ShapeDtypeStruct(work.shape, jnp.float32), small, small],
        scratch_shapes=[pltpu.VMEM((2, nvec * nvec, SUBLANES, LANES), jnp.float32)],
        compiler_params=pltpu.CompilerParams(vmem_limit_bytes=SMALL_VMEM_BYTES),
        cost_estimate=pl.CostEstimate(
            flops=4 * nvec * work.size, bytes_accessed=12 * work.size, transcendentals=0
        ),
        name="basis",
    )(sums, work, vec)


def shards(
    vectors,
    previous,
    beta,
    potential,
    coriolis_fn,
    second_fn,
    rot_const,
    coupling,
    kin_one,
    kin_two,
    kin_three,
    kin_four,
    kin_five,
    kin_six,
    coriolis_derivative,
):
    _, nvec, *points, width = vectors.shape
    rows = points[0] * points[1] * points[2]
    devices = lax.axis_size(ALL_AXES)
    block_index = lax.axis_index("ka")
    nblocks = lax.axis_size("ka")
    row_peers = lax.axis_size("row")
    mode_peers = lax.axis_size("mode")
    row_at = lax.axis_index("row")
    current = vectors.reshape(nvec, rows, width)
    older = previous.reshape(nvec, rows, width)
    block_rows = min(32, rows // 2)

    cut = rows * 3 // 4 // block_rows * block_rows or rows // 2
    starts, stops = [0, cut], [cut, rows]
    parts = [split_rows(current, start, stop) for start, stop in zip(starts, stops)]
    below_one = [hop(part, "ka", 1) for part in parts]
    above_one = [hop(part, "ka", -1) for part in parts]
    at = jnp.stack([block_index, row_at, row_at ^ 1]).astype(jnp.int32)
    group = 2 - row_peers % 2
    held = [current]
    if group == 2:
        held.append(lax.ppermute(current, "row", [(i, i ^ 1) for i in range(row_peers)]))
    away = row_peers // group - 1
    row_parts = crossing(tuple(points), at, kin_two, held, away) if away else []
    below_one[0] = handed_on(below_one[0], HOP_WEIGHT, row_parts)
    above_one[0] = handed_on(above_one[0], HOP_WEIGHT, row_parts)
    below_two = [hop(part, "ka", 1) for part in below_one]
    above_two = [hop(part, "ka", -1) for part in above_one]
    row_sums = [
        lax.ppermute(
            part, "row", [(i, (i + group * (number + 1)) % row_peers) for i in range(row_peers)]
        )
        for number, part in enumerate(row_parts)
    ]

    span = next((s for s in (256, 128) if width % s == 0 and s % kin_six.shape[0] == 0), width)
    left, mode_mat, tail, up, down = operators(
        tuple(points),
        group,
        mode_peers * rows,
        width,
        span,
        at,
        coupling,
        (kin_one, kin_two, kin_three, kin_four, kin_five, kin_six, coriolis_derivative),
        row_parts,
    )
    lower_two = jnp.maximum(block_index - 2, 0)
    far_pair = jnp.stack([coupling[1, block_index], coupling[1, lower_two]])
    sums, vec, skip_fn = resident(
        current, second_fn.reshape(rows, width), held[1:], block_rows
    )
    mode_shares = lax.all_to_all(vec, "mode", split_axis=0, concat_axis=0, tiled=True)
    mode_shares = mode_kinetic(mode_shares, mode_mat, mode_peers)
    mode_sum = lax.all_to_all(mode_shares, "mode", split_axis=0, concat_axis=0, tiled=True)
    work = local_terms(
        nblocks, at, rot_const, beta, held, older, potential.reshape(rows, width), left, tail
    )
    work = join_terms(
        work,
        coriolis_fn.reshape(rows, width),
        up,
        down,
        starts,
        below_one,
        above_one,
        [mode_sum, *row_sums],
    )
    for number, start in enumerate(starts):
        work, copied = far_terms(
            far_pair,
            work,
            above_two[number],
            below_two[number],
            skip_fn,
            vec,
            sums,
            start,
            block_rows,
            devices if number == len(starts) - 1 else 1,
        )
        sums = copied[0]
    every_sum = lax.all_to_all(copied, ALL_AXES, split_axis=0, concat_axis=0, tiled=True)
    count = float(devices * rows * width)
    basis, alpha, lower = basis_of(count, every_sum, work, vec, block_rows)
    return (basis.reshape(vectors.shape), alpha, lower)


def solution(mesh):
    return jax.shard_map(
        shards,
        mesh=mesh,
        in_specs=(
            P("ka", None, "mode", "row", None, None),
            P("ka", None, "mode", "row", None, None),
            P(),
            P("mode", "row", None, None),
            P("mode", "row", None, None),
            P("mode", "row", None, None),
            P(),
            P(),
            P(),
            P(),
            P(),
            P(),
            P(),
            P(),
            P(),
        ),
        out_specs=(P("ka", None, "mode", "row", None, None), P(), P()),
        check_vma=False,
    )
```

```python
import functools

import jax
import jax.numpy as jnp
from jax import lax
from jax.experimental import pallas as pl
from jax.experimental.pallas import tpu as pltpu
from jax.sharding import PartitionSpec as P

precise_mode = lax.Precision.HIGHEST
ALL_AXES = ("ka", "mode", "row")
VMEM_BYTES = 32 * 1024 * 1024
SMALL_VMEM_BYTES = 16 * 1024 * 1024
FULL_VMEM_BYTES = 56 * 1024 * 1024
LANES = 128
HOP_WEIGHT = 25_000_000_000
SUBLANES = 8


def precise_dot(left, right):
    return jnp.dot(left, right, precision=precise_mode, preferred_element_type=jnp.float32)


def whole_spec(shape):
    return pl.BlockSpec(shape, lambda *_: (0,) * len(shape))


def pair_exchange(value, axis, first):
    peers = lax.axis_size(axis)
    pairs = []
    for low in range(first, peers - 1, 2):
        pairs += [(low, low + 1), (low + 1, low)]
    return lax.ppermute(value, axis, pairs)


def vector_groups(nvec):
    return [tuple(range(at, min(at + 4, nvec))) for at in range(0, nvec, 4)]


def tiles(rows, width):
    return [
        (slice(r, r + SUBLANES), slice(c, c + LANES))
        for r in range(0, rows, SUBLANES)
        for c in range(0, width, LANES)
    ]


def packed_columns(sums, nvec, offset, lane):
    packed = jnp.zeros((nvec, LANES), jnp.float32)
    for j in range(nvec):
        stacked = jnp.stack([sums(i, j) for i in range(nvec)])
        column = jnp.sum(jnp.sum(stacked, axis=1), axis=1, keepdims=True)
        packed = packed + jnp.where(lane == offset + j, column, 0.0)
    return packed


def add_products(nvec, left_ref, right_ref, sums, number, places, symmetric):
    groups = vector_groups(nvec)
    for ours in groups:
        for other in groups:
            pairs = [(i, j) for i in ours for j in other if i <= j or not symmetric]
            if not pairs:
                continue
            totals = {pair: sums[number, pair[0] * nvec + pair[1]] for pair in pairs}
            for place in places:
                lefts = {i: left_ref[(i, *place)] for i in {p[0] for p in pairs}}
                rights = {j: right_ref[(j, *place)] for j in {p[1] for p in pairs}}
                for i, j in pairs:
                    totals[i, j] = totals[i, j] + lefts[i] * rights[j]
            for i, j in pairs:
                sums[number, i * nvec + j] = totals[i, j]


def resident_kernel(nvec, vec_ref, fn_ref, *refs):
    out_ref, copy_ref, fn_copy_ref, sums = refs[-4:]
    step = pl.program_id(0)

    @pl.when(step == 0)
    def _():
        sums[...] = jnp.zeros_like(sums)

    copy_ref[...] = vec_ref[...]
    fn_copy_ref[...] = fn_ref[...]
    add_products(nvec, vec_ref, vec_ref, sums, 0, tiles(*vec_ref.shape[1:]), True)

    @pl.when(step == pl.num_programs(0) - 1)
    def _():
        lane = lax.broadcasted_iota(jnp.int32, (nvec, LANES), 1)
        out_ref[...] = packed_columns(
            lambda i, j: sums[0, min(i, j) * nvec + max(i, j)], nvec, 2 * nvec, lane
        )


def resident(vec, skip_fn, after, block_rows):
    nvec, rows, width = vec.shape
    block = pl.BlockSpec((nvec, block_rows, width), lambda s: (0, s, 0))
    fn_block = pl.BlockSpec((block_rows, width), lambda s: (s, 0))
    return pl.pallas_call(
        functools.partial(resident_kernel, nvec),
        grid=(rows // block_rows,),
        in_specs=[block, fn_block] + [pl.BlockSpec(memory_space=pl.ANY)] * len(after),
        out_specs=[whole_spec((nvec, LANES)), block, fn_block],
        out_shape=[
            jax.ShapeDtypeStruct((nvec, LANES), jnp.float32),
            jax.ShapeDtypeStruct(vec.shape, jnp.float32),
            jax.ShapeDtypeStruct(skip_fn.shape, jnp.float32),
        ],
        scratch_shapes=[pltpu.VMEM((1, nvec * nvec, SUBLANES, LANES), jnp.float32)],
        compiler_params=pltpu.CompilerParams(vmem_limit_bytes=VMEM_BYTES),
        cost_estimate=pl.CostEstimate(
            flops=nvec * (nvec + 1) * rows * width, bytes_accessed=8 * vec.size, transcendentals=0
        ),
        name="resident",
    )(vec, skip_fn, *after)


def split_kernel(start, vec_ref, out_ref, held, sems):
    count, rows, _ = out_ref.shape
    loads = [
        pltpu.make_async_copy(vec_ref.at[i, pl.ds(start, rows)], held.at[i], sems.at[0, i])
        for i in range(count)
    ]
    stores = [
        pltpu.make_async_copy(held.at[i], out_ref.at[i], sems.at[1, i]) for i in range(count)
    ]
    for load in loads:
        load.start()
    for load, store in zip(loads, stores):
        load.wait()
        store.start()
    for store in stores:
        store.wait()


def split_rows(vec, start, stop):
    nvec, _, width = vec.shape
    shape = (nvec, stop - start, width)
    return pl.pallas_call(
        functools.partial(split_kernel, start),
        in_specs=[pl.BlockSpec(memory_space=pl.ANY)],
        out_specs=pl.BlockSpec(memory_space=pl.ANY),
        out_shape=jax.ShapeDtypeStruct(shape, jnp.float32),
        scratch_shapes=[
            pltpu.VMEM(shape, jnp.float32),
            pltpu.SemaphoreType.DMA((2, nvec)),
        ],
        compiler_params=pltpu.CompilerParams(vmem_limit_bytes=FULL_VMEM_BYTES),
        cost_estimate=pl.CostEstimate(
            flops=0, bytes_accessed=8 * nvec * (stop - start) * width, transcendentals=0
        ),
        name="split_rows",
    )(vec)


def handed_on(array, weight, after=()):
    return pl.pallas_call(
        lambda *_: None,
        in_specs=[pl.BlockSpec(memory_space=pl.ANY)] * (1 + len(after)),
        out_specs=pl.BlockSpec(memory_space=pl.ANY),
        out_shape=jax.ShapeDtypeStruct(array.shape, array.dtype),
        input_output_aliases={0: 0},
        cost_estimate=pl.CostEstimate(flops=weight, bytes_accessed=0, transcendentals=0),
        name="handed_on",
    )(array, *after)


def kron_term(matrix, size, stride, extent, row_offset=0, column_offset=0, sign=1.0):
    points = matrix.shape[0]

    def digits(shape, axis):
        index = lax.broadcasted_iota(jnp.int32, shape, axis)
        return index, lax.rem(lax.div(index, stride), size)

    def picks(offset):
        _, digit = digits((extent, points), 0)
        point = lax.broadcasted_iota(jnp.int32, (extent, points), 1)
        return jnp.where(digit + offset == point, 1.0, 0.0)

    def transposed_dot(one, two):
        return lax.dot_general(
            one, two, (((1,), (1,)), ((), ())), precision=precise_mode,
            preferred_element_type=jnp.float32,
        )

    picked = picks(row_offset)
    picked = 0.5 * (precise_dot(picked, matrix) + sign * transposed_dot(picked, matrix))
    spread = transposed_dot(picked, picks(column_offset))
    row, row_digit = digits((extent, extent), 0)
    column, column_digit = digits((extent, extent), 1)
    same = (row - row_digit * stride) == (column - column_digit * stride)
    return jnp.where(same, spread, 0.0)


def operators_kernel(
    points, group, at_ref, coupling_ref, one_ref, two_ref, three_ref, four_ref, five_ref, six_ref,
    der_ref, *refs,
):
    left_ref, mode_ref, tail_ref, near_ref = refs[-4:]
    points_one, points_two, points_three = points
    rows = points_one * points_two * points_three
    stride = points_two * points_three
    mine = at_ref[1] * points_two
    left_ref[0] = kron_term(two_ref[...], points_two, points_three, rows, mine, mine) + kron_term(
        three_ref[...], points_three, 1, rows
    )
    if group > 1:
        sibling = at_ref[2] * points_two
        left_ref[1] = kron_term(two_ref[...], points_two, points_three, rows, mine, sibling)
    mode_ref[...] = kron_term(one_ref[...], one_ref.shape[0], stride, mode_ref.shape[0])
    width = tail_ref.shape[0]
    fives, sixes = five_ref.shape[0], six_ref.shape[0]
    tail_ref[...] = (
        kron_term(four_ref[...], four_ref.shape[0], fives * sixes, width)
        + kron_term(five_ref[...], fives, sixes, width)
        + kron_term(six_ref[...], sixes, 1, width)
    )
    twist = kron_term(der_ref[...], sixes, 1, near_ref.shape[1], sign=-1.0)
    block = at_ref[0]
    even = lax.rem(block, 2) == 0
    from_above = -coupling_ref[0, block]
    from_below = coupling_ref[0, jnp.maximum(block - 1, 0)]
    near_ref[0] = jnp.where(even, from_above, from_below) * twist
    near_ref[1] = jnp.where(even, from_below, from_above) * twist


def operators(points, group, mode_extent, width, span, at, coupling, matrices, after):
    rows = points[0] * points[1] * points[2]
    shapes = [
        (group, rows, rows), (mode_extent, mode_extent), (width, width), (2, span, span)
    ]
    smem = pl.BlockSpec(memory_space=pltpu.SMEM)
    return pl.pallas_call(
        functools.partial(operators_kernel, points, group),
        in_specs=[smem, smem]
        + [pl.BlockSpec(memory_space=pltpu.VMEM)] * len(matrices)
        + [pl.BlockSpec(memory_space=pl.ANY)] * len(after),
        out_specs=[pl.BlockSpec(memory_space=pltpu.VMEM)] * len(shapes),
        out_shape=[jax.ShapeDtypeStruct(shape, jnp.float32) for shape in shapes],
        compiler_params=pltpu.CompilerParams(vmem_limit_bytes=VMEM_BYTES),
        cost_estimate=pl.CostEstimate(
            flops=500_000_000, bytes_accessed=4_000_000, transcendentals=0
        ),
        name="operators",
    )(at, coupling, *matrices, *after)


def crossing_kernel(points, group, at_ref, two_ref, *refs):
    points_one, points_two, points_three = points
    held_refs, out_refs = refs[:group], refs[group:]
    owners = [at_ref[1], at_ref[2]][:group]
    peers = two_ref.shape[0] // points_two
    stride = points_two * points_three
    for number, out_ref in enumerate(out_refs):
        target = lax.rem(at_ref[1] + group * (number + 1), peers) * points_two
        coefs = {
            (a, k, b): 0.5
            * (
                two_ref[target + a, owners[k] * points_two + b]
                + two_ref[owners[k] * points_two + b, target + a]
            )
            for a in range(points_two)
            for k in range(group)
            for b in range(points_two)
        }
        for start in range(0, points_one * stride, stride):
            for _, lanes in tiles(SUBLANES, out_ref.shape[2]):
                for inner in range(0, points_three, SUBLANES):
                    values = {
                        (k, b): held_refs[k][0, pl.ds(start + b * points_three + inner, SUBLANES), lanes]
                        for k in range(group)
                        for b in range(points_two)
                    }
                    for a in range(points_two):
                        total = None
                        for (k, b), value in values.items():
                            term = coefs[a, k, b] * value
                            total = term if total is None else total + term
                        out_ref[0, pl.ds(start + a * points_three + inner, SUBLANES), lanes] = total


def crossing(points, at, two, held, count):
    nvec, rows, width = held[0].shape
    one = pl.BlockSpec((1, rows, width), lambda i: (i, 0, 0))
    smem = pl.BlockSpec(memory_space=pltpu.SMEM)
    return pl.pallas_call(
        functools.partial(crossing_kernel, points, len(held)),
        grid=(nvec,),
        in_specs=[smem, smem] + [one] * len(held),
        out_specs=[one] * count,
        out_shape=[jax.ShapeDtypeStruct(held[0].shape, jnp.float32)] * count,
        compiler_params=pltpu.CompilerParams(vmem_limit_bytes=VMEM_BYTES),
        cost_estimate=pl.CostEstimate(
            flops=2 * held[0].size * points[1] * len(held) * count,
            bytes_accessed=4 * held[0].size * (len(held) + count),
            transcendentals=0,
        ),
        name="crossing",
    )(at, two, *held)


def local_kernel(nvec, nblocks, group, at_ref, rot_ref, beta_ref, *refs):
    held_refs = refs[:group]
    old_ref, pot_ref, left_ref, tail_ref, out_ref = refs[group:]
    me = pl.program_id(0)
    block = at_ref[0]
    level = (block - nblocks // 2).astype(jnp.float32)
    current = held_refs[0][0]
    total = (pot_ref[...] + rot_ref[block] * level * level) * current
    for j in range(nvec):
        total = total - beta_ref[me, j] * old_ref[j]
    total = total + precise_dot(current, tail_ref[...])
    for number, held_ref in enumerate(held_refs):
        total = total + precise_dot(left_ref[number], held_ref[0])
    out_ref[0] = total


def local_terms(nblocks, at, rot_const, beta, held, old, pot, left, tail):
    nvec, rows, width = old.shape
    one = pl.BlockSpec((1, rows, width), lambda i: (i, 0, 0))
    smem = pl.BlockSpec(memory_space=pltpu.SMEM)
    return pl.pallas_call(
        functools.partial(local_kernel, nvec, nblocks, len(held)),
        grid=(nvec,),
        in_specs=[smem, smem, smem]
        + [one] * len(held)
        + [
            whole_spec(old.shape),
            whole_spec(pot.shape),
            pl.BlockSpec((len(held), rows, rows), lambda i: (0, 0, 0)),
            whole_spec(tail.shape),
        ],
        out_specs=one,
        out_shape=jax.ShapeDtypeStruct(old.shape, jnp.float32),
        compiler_params=pltpu.CompilerParams(vmem_limit_bytes=VMEM_BYTES),
        cost_estimate=pl.CostEstimate(
            flops=12 * old.size * (rows * len(held) + width),
            bytes_accessed=4 * old.size * (2 + len(held)),
            transcendentals=0,
        ),
        name="local_terms",
    )(at, rot_const, beta, *held, old, pot, left, tail)


def mode_kinetic_kernel(peers, in_ref, mat_ref, out_ref):
    rows = in_ref.shape[2]
    field = jnp.concatenate([in_ref[peer, 0] for peer in range(peers)], axis=0)
    field = precise_dot(mat_ref[...], field)
    for peer in range(peers):
        out_ref[peer, 0] = field[peer * rows : (peer + 1) * rows]


def mode_kinetic(field, matrix, peers):
    nvec, rows, width = field.shape
    held = nvec // peers
    block = pl.BlockSpec((peers, 1, rows, width), lambda q: (0, q, 0, 0))
    out = pl.pallas_call(
        functools.partial(mode_kinetic_kernel, peers),
        grid=(held,),
        in_specs=[block, whole_spec(matrix.shape)],
        out_specs=block,
        out_shape=jax.ShapeDtypeStruct((peers, held, rows, width), jnp.float32),
        compiler_params=pltpu.CompilerParams(vmem_limit_bytes=VMEM_BYTES),
        cost_estimate=pl.CostEstimate(
            flops=12 * field.size * matrix.shape[0], bytes_accessed=8 * field.size, transcendentals=0
        ),
        name="mode_kinetic",
    )(field.reshape(peers, held, rows, width), matrix)
    return out.reshape(field.shape)


def join_kernel(starts, sum_count, at_ref, work_ref, cor_ref, near_ref, *refs):
    pieces = len(starts)
    first_refs, second_refs = refs[:pieces], refs[pieces : 2 * pieces]
    sum_refs = refs[2 * pieces : 2 * pieces + sum_count]
    out_ref = refs[-1]
    span = near_ref.shape[1]
    even = lax.rem(at_ref[0], 2) == 0
    for start, first_ref, second_ref in zip(starts, first_refs, second_refs):
        place = slice(start, start + first_ref.shape[1])
        for at in range(0, work_ref.shape[2], span):
            part = slice(at, at + span)
            total = work_ref[0, place, part]
            for sum_ref in sum_refs:
                total = total + sum_ref[0, place, part]
            twist_fn = cor_ref[place, part]
            if_even = jnp.where(even, twist_fn, 1.0)
            if_odd = jnp.where(even, 1.0, twist_fn)
            total = total + if_even * precise_dot(
                if_odd * first_ref[0, :, part], near_ref[0]
            )
            out_ref[0, place, part] = total + if_odd * precise_dot(
                if_even * second_ref[0, :, part], near_ref[1]
            )


def join_terms(at, work, cor, near, starts, first, second, sums):
    nvec, rows, width = work.shape
    one = pl.BlockSpec((1, rows, width), lambda i: (i, 0, 0))
    pieces = [pl.BlockSpec((1, b.shape[1], width), lambda i: (i, 0, 0)) for b in first]
    return pl.pallas_call(
        functools.partial(join_kernel, tuple(starts), len(sums)),
        grid=(nvec,),
        in_specs=[
            pl.BlockSpec(memory_space=pltpu.SMEM), one, whole_spec(cor.shape), whole_spec(near.shape)
        ]
        + pieces
        + pieces
        + [one] * len(sums),
        out_specs=one,
        out_shape=jax.ShapeDtypeStruct(work.shape, jnp.float32),
        compiler_params=pltpu.CompilerParams(vmem_limit_bytes=VMEM_BYTES),
        cost_estimate=pl.CostEstimate(
            flops=24 * work.size * near.shape[1], bytes_accessed=24 * work.size, transcendentals=0
        ),
        name="join_terms",
    )(at, work, cor, near, *first, *second, *sums)


def far_terms_kernel(
    nvec, start, coef_ref, work_ref, first_ref, second_ref, fn_ref, vec_ref, before_ref, out_ref,
    sum_ref, sums,
):
    del work_ref
    step = pl.program_id(0)
    _, block_rows, width = first_ref.shape

    @pl.when(step == 0)
    def _():
        sums[...] = jnp.zeros_like(sums)

    at = pl.multiple_of(start + step * block_rows, SUBLANES)
    places = []
    for rows_here, lanes in tiles(block_rows, width):
        place = (pl.ds(at + rows_here.start, SUBLANES), lanes)
        places.append(place)
        skip_fn = fn_ref[place]
        first_fn = coef_ref[0] * skip_fn
        second_fn = coef_ref[1] * skip_fn
        for i in range(nvec):
            out_ref[(i, *place)] = (
                out_ref[(i, *place)]
                + first_fn * first_ref[i, rows_here, lanes]
                + second_fn * second_ref[i, rows_here, lanes]
            )
    add_products(nvec, vec_ref, out_ref, sums, 0, places, False)
    add_products(nvec, out_ref, out_ref, sums, 1, places, True)

    @pl.when(step == pl.num_programs(0) - 1)
    def _():
        lane = lax.broadcasted_iota(jnp.int32, (nvec, LANES), 1)
        packed = before_ref[...]
        packed = packed + packed_columns(lambda i, j: sums[0, j * nvec + i], nvec, 0, lane)
        packed = packed + packed_columns(
            lambda i, j: sums[1, min(i, j) * nvec + max(i, j)], nvec, nvec, lane
        )
        sum_ref[...] = jnp.broadcast_to(packed[None], sum_ref.shape)


def far_terms(coef, work, first, second, skip_fn, vec, before, start, block_rows, copies):
    nvec, _, width = work.shape
    rows = first.shape[1]
    whole = pl.BlockSpec(memory_space=pltpu.VMEM)
    block = pl.BlockSpec((nvec, block_rows, width), lambda s: (0, s, 0))
    work, skip_fn, vec = (
        pltpu.with_memory_space_constraint(array, pltpu.VMEM) for array in (work, skip_fn, vec)
    )
    return pl.pallas_call(
        functools.partial(far_terms_kernel, nvec, start),
        grid=(rows // block_rows,),
        in_specs=[
            pl.BlockSpec(memory_space=pltpu.SMEM), whole, block, block, whole, whole, whole
        ],
        out_specs=[whole, whole],
        out_shape=[
            jax.ShapeDtypeStruct(work.shape, jnp.float32),
            jax.ShapeDtypeStruct((copies, nvec, LANES), jnp.float32),
        ],
        scratch_shapes=[pltpu.VMEM((2, nvec * nvec, SUBLANES, LANES), jnp.float32)],
        input_output_aliases={1: 0},
        compiler_params=pltpu.CompilerParams(vmem_limit_bytes=SMALL_VMEM_BYTES),
        cost_estimate=pl.CostEstimate(
            flops=3 * nvec * nvec * rows * width,
            bytes_accessed=20 * first.size,
            transcendentals=0,
        ),
        name="far_terms",
    )(coef, work, first, second, skip_fn, vec, before)


def small_dot(left, right):
    terms = [left[:, k : k + 1] * right[k : k + 1, :] for k in range(right.shape[0])]
    while len(terms) > 1:
        terms = [sum(terms[k + 1 : k + 2], terms[k]) for k in range(0, len(terms), 2)]
    return terms[0]


def small_algebra(nvec, count, packed):
    packed = packed * (1.0 / count)
    cross = packed.T[0:nvec, :]
    cross_turned = packed[:, 0:nvec]
    work_gram = packed[:, nvec : 2 * nvec]
    vec_gram = packed[:, 2 * nvec : 3 * nvec]
    total = 2.0 * cross - small_dot(vec_gram, cross)
    total_turned = 2.0 * cross_turned - small_dot(cross_turned, vec_gram)
    gram = work_gram - small_dot(total_turned, cross) - small_dot(cross_turned, total)
    gram = gram + small_dot(total_turned, small_dot(vec_gram, total))
    row = lax.broadcasted_iota(jnp.int32, (nvec, nvec), 0)
    column = lax.broadcasted_iota(jnp.int32, (nvec, nvec), 1)
    inverse = jnp.where(row == column, 1.0, 0.0)
    lower = jnp.zeros((nvec, nvec), jnp.float32)
    for at in range(nvec):
        pivot = gram[at : at + 1, at : at + 1]
        scale = lax.rsqrt(pivot)
        scale = scale * (1.5 - 0.5 * pivot * scale * scale)
        scaled = gram[:, at : at + 1] * scale
        lower = jnp.where((column == at) & (row >= at), scaled, lower)
        pivot_row = inverse[at : at + 1, :] * scale
        factor = jnp.where(row > at, scaled, 0.0)
        inverse = jnp.where(row == at, pivot_row, inverse - factor * pivot_row)
        gram = gram - factor * (gram[at : at + 1, :] * scale)
    return total, lower, inverse, -small_dot(inverse, total_turned)


def basis_kernel(nvec, count, sum_ref, work_ref, vec_ref, out_ref, alpha_ref, lower_ref, coefs):
    @pl.when(pl.program_id(0) == 0)
    def _():
        packed = sum_ref[0]
        for other in range(1, sum_ref.shape[0]):
            packed = packed + sum_ref[other]
        total, lower, inverse, mixing = small_algebra(nvec, count, packed)
        alpha_ref[...] = total
        lower_ref[...] = lower
        for number, matrix in enumerate((inverse, mixing)):
            for i in range(nvec):
                for j in range(nvec):
                    coefs[number, i * nvec + j] = jnp.broadcast_to(
                        matrix[i : i + 1, j : j + 1], (SUBLANES, LANES)
                    )

    start = pl.multiple_of(pl.program_id(0) * out_ref.shape[1], out_ref.shape[1])
    places = tiles(*out_ref.shape[1:])
    for at in range(0, len(places), 4):
        group = places[at : at + 4]
        held = [(pl.ds(start + place.start, SUBLANES), lanes) for place, lanes in group]
        for ours in vector_groups(nvec):
            totals = {}
            for number, ref in ((1, vec_ref), (0, work_ref)):
                for j in range(nvec):
                    outs = [i for i in ours if number == 1 or j <= i]
                    if not outs:
                        continue
                    values = [ref[(j, *place)] for place in held]
                    for i in outs:
                        coef = coefs[number, i * nvec + j]
                        for spot, value in enumerate(values):
                            term = coef * value
                            here = (i, spot)
                            totals[here] = totals[here] + term if here in totals else term
            for i in ours:
                for spot, place in enumerate(group):
                    out_ref[(i, *place)] = totals[i, spot]


def basis_of(count, sums, work, vec, block_rows):
    nvec, rows, width = work.shape
    block = pl.BlockSpec((nvec, block_rows, width), lambda s: (0, s, 0))
    small = jax.ShapeDtypeStruct((nvec, nvec), jnp.float32)
    whole = pl.BlockSpec(memory_space=pltpu.VMEM)
    work, vec = (pltpu.with_memory_space_constraint(array, pltpu.VMEM) for array in (work, vec))
    return pl.pallas_call(
        functools.partial(basis_kernel, nvec, count),
        grid=(rows // block_rows,),
        in_specs=[whole, whole, whole],
        out_specs=[block, whole_spec(small.shape), whole_spec(small.shape)],
        out_shape=[jax.ShapeDtypeStruct(work.shape, jnp.float32), small, small],
        scratch_shapes=[pltpu.VMEM((2, nvec * nvec, SUBLANES, LANES), jnp.float32)],
        compiler_params=pltpu.CompilerParams(vmem_limit_bytes=SMALL_VMEM_BYTES),
        cost_estimate=pl.CostEstimate(
            flops=4 * nvec * work.size, bytes_accessed=12 * work.size, transcendentals=0
        ),
        name="basis",
    )(sums, work, vec)


def shards(
    vectors,
    previous,
    beta,
    potential,
    coriolis_fn,
    second_fn,
    rot_const,
    coupling,
    kin_one,
    kin_two,
    kin_three,
    kin_four,
    kin_five,
    kin_six,
    coriolis_derivative,
):
    _, nvec, *points, width = vectors.shape
    rows = points[0] * points[1] * points[2]
    devices = lax.axis_size(ALL_AXES)
    block_index = lax.axis_index("ka")
    nblocks = lax.axis_size("ka")
    row_peers = lax.axis_size("row")
    mode_peers = lax.axis_size("mode")
    row_at = lax.axis_index("row")
    current = vectors.reshape(nvec, rows, width)
    older = previous.reshape(nvec, rows, width)
    block_rows = min(32, rows // 2)

    cut = rows * 3 // 4 // block_rows * block_rows or rows // 2
    starts, stops = [0, cut], [cut, rows]
    parts = [split_rows(current, start, stop) for start, stop in zip(starts, stops)]
    near_first = [pair_exchange(part, "ka", 0) for part in parts]
    near_second = [pair_exchange(part, "ka", 1) for part in parts]
    at = jnp.stack([block_index, row_at, row_at ^ 1]).astype(jnp.int32)
    group = 2 - row_peers % 2
    held = [current]
    if group == 2:
        held.append(lax.ppermute(current, "row", [(i, i ^ 1) for i in range(row_peers)]))
    away = row_peers // group - 1
    row_parts = crossing(tuple(points), at, kin_two, held, away) if away else []
    row_sums = [
        lax.ppermute(
            part, "row", [(i, (i + group * (number + 1)) % row_peers) for i in range(row_peers)]
        )
        for number, part in enumerate(row_parts)
    ]

    span = next((s for s in (256, 128) if width % s == 0 and s % kin_six.shape[0] == 0), width)
    left, mode_mat, tail, near = operators(
        tuple(points),
        group,
        mode_peers * rows,
        width,
        span,
        at,
        coupling,
        (kin_one, kin_two, kin_three, kin_four, kin_five, kin_six, coriolis_derivative),
        row_parts,
    )
    near_first[0] = handed_on(near_first[0], HOP_WEIGHT, [*row_parts, mode_mat])
    near_second[0] = handed_on(near_second[0], HOP_WEIGHT, [*row_parts, mode_mat])
    far_first = [pair_exchange(part, "ka", 0) for part in near_second]
    far_second = [pair_exchange(part, "ka", 1) for part in near_first]
    lower_two = jnp.maximum(block_index - 2, 0)
    far_above, far_below = coupling[1, block_index], coupling[1, lower_two]
    even = block_index % 2 == 0
    far_pair = jnp.stack(
        [jnp.where(even, far_above, far_below), jnp.where(even, far_below, far_above)]
    )
    sums, vec, skip_fn = resident(
        current, second_fn.reshape(rows, width), held[1:], block_rows
    )
    mode_shares = lax.all_to_all(vec, "mode", split_axis=0, concat_axis=0, tiled=True)
    mode_shares = mode_kinetic(mode_shares, mode_mat, mode_peers)
    mode_sum = lax.all_to_all(mode_shares, "mode", split_axis=0, concat_axis=0, tiled=True)
    work = local_terms(
        nblocks, at, rot_const, beta, held, older, potential.reshape(rows, width), left, tail
    )
    work = join_terms(
        at,
        work,
        coriolis_fn.reshape(rows, width),
        near,
        starts,
        near_first,
        near_second,
        [mode_sum, *row_sums],
    )
    for number, start in enumerate(starts):
        work, copied = far_terms(
            far_pair,
            work,
            far_first[number],
            far_second[number],
            skip_fn,
            vec,
            sums,
            start,
            block_rows,
            devices if number == len(starts) - 1 else 1,
        )
        sums = copied[0]
    every_sum = lax.all_to_all(copied, ALL_AXES, split_axis=0, concat_axis=0, tiled=True)
    count = float(devices * rows * width)
    basis, alpha, lower = basis_of(count, every_sum, work, vec, block_rows)
    return (basis.reshape(vectors.shape), alpha, lower)


def solution(mesh):
    return jax.shard_map(
        shards,
        mesh=mesh,
        in_specs=(
            P("ka", None, "mode", "row", None, None),
            P("ka", None, "mode", "row", None, None),
            P(),
            P("mode", "row", None, None),
            P("mode", "row", None, None),
            P("mode", "row", None, None),
            P(),
            P(),
            P(),
            P(),
            P(),
            P(),
            P(),
            P(),
            P(),
        ),
        out_specs=(P("ka", None, "mode", "row", None, None), P(), P()),
        check_vma=False,
    )
```

```python
import functools

import jax
import jax.numpy as jnp
from jax import lax
from jax.experimental import pallas as pl
from jax.experimental.pallas import tpu as pltpu
from jax.sharding import PartitionSpec as P

precise_mode = lax.Precision.HIGHEST
ALL_AXES = ("ka", "mode", "row")
VMEM_BYTES = 32 * 1024 * 1024
SMALL_VMEM_BYTES = 16 * 1024 * 1024
FULL_VMEM_BYTES = 56 * 1024 * 1024
LANES = 128
HOP_WEIGHT = 25_000_000_000
SUBLANES = 8


def precise_dot(left, right):
    return jnp.dot(left, right, precision=precise_mode, preferred_element_type=jnp.float32)


def whole_spec(shape):
    return pl.BlockSpec(shape, lambda *_: (0,) * len(shape))


def pair_exchange(value, axis, first):
    peers = lax.axis_size(axis)
    pairs = []
    for low in range(first, peers - 1, 2):
        pairs += [(low, low + 1), (low + 1, low)]
    return lax.ppermute(value, axis, pairs)


def parts_of(value):
    parts = []
    for _ in range(3):
        part = value.astype(jnp.bfloat16)
        parts.append(part)
        value = value - part.astype(jnp.float32)
    return parts


PART_PAIRS = ((0, 0), (0, 1), (1, 0), (1, 1), (0, 2), (2, 0))


def vector_groups(nvec):
    return [tuple(range(at, min(at + 4, nvec))) for at in range(0, nvec, 4)]


def tiles(rows, width):
    return [
        (slice(r, r + SUBLANES), slice(c, c + LANES))
        for r in range(0, rows, SUBLANES)
        for c in range(0, width, LANES)
    ]


def packed_columns(sums, nvec, offset, lane):
    packed = jnp.zeros((nvec, LANES), jnp.float32)
    for j in range(nvec):
        stacked = jnp.stack([sums(i, j) for i in range(nvec)])
        column = jnp.sum(jnp.sum(stacked, axis=1), axis=1, keepdims=True)
        packed = packed + jnp.where(lane == offset + j, column, 0.0)
    return packed


def add_products(nvec, left_ref, right_ref, sums, number, places, symmetric):
    groups = vector_groups(nvec)
    for ours in groups:
        for other in groups:
            pairs = [(i, j) for i in ours for j in other if i <= j or not symmetric]
            if not pairs:
                continue
            totals = {pair: sums[number, pair[0] * nvec + pair[1]] for pair in pairs}
            for place in places:
                lefts = {i: left_ref[(i, *place)] for i in {p[0] for p in pairs}}
                rights = {j: right_ref[(j, *place)] for j in {p[1] for p in pairs}}
                for i, j in pairs:
                    totals[i, j] = totals[i, j] + lefts[i] * rights[j]
            for i, j in pairs:
                sums[number, i * nvec + j] = totals[i, j]


def resident_kernel(nvec, vec_ref, fn_ref, *refs):
    out_ref, copy_ref, part_ref, fn_copy_ref, sums = refs[-5:]
    step = pl.program_id(0)

    @pl.when(step == 0)
    def _():
        sums[...] = jnp.zeros_like(sums)

    copy_ref[...] = vec_ref[...]
    for i in range(nvec):
        for number, part in enumerate(parts_of(vec_ref[i])):
            part_ref[number, i] = part
    fn_copy_ref[...] = fn_ref[...]
    add_products(nvec, vec_ref, vec_ref, sums, 0, tiles(*vec_ref.shape[1:]), True)

    @pl.when(step == pl.num_programs(0) - 1)
    def _():
        lane = lax.broadcasted_iota(jnp.int32, (nvec, LANES), 1)
        out_ref[...] = packed_columns(
            lambda i, j: sums[0, min(i, j) * nvec + max(i, j)], nvec, 2 * nvec, lane
        )


def resident(vec, skip_fn, after, block_rows):
    nvec, rows, width = vec.shape
    block = pl.BlockSpec((nvec, block_rows, width), lambda s: (0, s, 0))
    fn_block = pl.BlockSpec((block_rows, width), lambda s: (s, 0))
    return pl.pallas_call(
        functools.partial(resident_kernel, nvec),
        grid=(rows // block_rows,),
        in_specs=[block, fn_block] + [pl.BlockSpec(memory_space=pl.ANY)] * len(after),
        out_specs=[
            whole_spec((nvec, LANES)),
            block,
            pl.BlockSpec((3, nvec, block_rows, width), lambda s: (0, 0, s, 0)),
            fn_block,
        ],
        out_shape=[
            jax.ShapeDtypeStruct((nvec, LANES), jnp.float32),
            jax.ShapeDtypeStruct(vec.shape, jnp.float32),
            jax.ShapeDtypeStruct((3, *vec.shape), jnp.bfloat16),
            jax.ShapeDtypeStruct(skip_fn.shape, jnp.float32),
        ],
        scratch_shapes=[pltpu.VMEM((1, nvec * nvec, SUBLANES, LANES), jnp.float32)],
        compiler_params=pltpu.CompilerParams(vmem_limit_bytes=VMEM_BYTES),
        cost_estimate=pl.CostEstimate(
            flops=nvec * (nvec + 1) * rows * width, bytes_accessed=8 * vec.size, transcendentals=0
        ),
        name="resident",
    )(vec, skip_fn, *after)


def split_kernel(start, vec_ref, out_ref, held, sems):
    count, rows, _ = out_ref.shape
    loads = [
        pltpu.make_async_copy(vec_ref.at[i, pl.ds(start, rows)], held.at[i], sems.at[0, i])
        for i in range(count)
    ]
    stores = [
        pltpu.make_async_copy(held.at[i], out_ref.at[i], sems.at[1, i]) for i in range(count)
    ]
    window = min(3, count)
    for load in loads[:window]:
        load.start()
    for number, store in enumerate(stores):
        loads[number].wait()
        store.start()
        if number + window < count:
            loads[number + window].start()
    for store in stores:
        store.wait()


def split_rows(vec, start, stop):
    nvec, _, width = vec.shape
    shape = (nvec, stop - start, width)
    return pl.pallas_call(
        functools.partial(split_kernel, start),
        in_specs=[pl.BlockSpec(memory_space=pl.ANY)],
        out_specs=pl.BlockSpec(memory_space=pl.ANY),
        out_shape=jax.ShapeDtypeStruct(shape, jnp.float32),
        scratch_shapes=[
            pltpu.VMEM(shape, jnp.float32),
            pltpu.SemaphoreType.DMA((2, nvec)),
        ],
        compiler_params=pltpu.CompilerParams(vmem_limit_bytes=FULL_VMEM_BYTES),
        cost_estimate=pl.CostEstimate(
            flops=0, bytes_accessed=8 * nvec * (stop - start) * width, transcendentals=0
        ),
        name="split_rows",
    )(vec)


def handed_on(array, weight, after=()):
    return pl.pallas_call(
        lambda *_: None,
        in_specs=[pl.BlockSpec(memory_space=pl.ANY)] * (1 + len(after)),
        out_specs=pl.BlockSpec(memory_space=pl.ANY),
        out_shape=jax.ShapeDtypeStruct(array.shape, array.dtype),
        input_output_aliases={0: 0},
        cost_estimate=pl.CostEstimate(flops=weight, bytes_accessed=0, transcendentals=0),
        name="handed_on",
    )(array, *after)


def kron_term(matrix, size, stride, extent, row_offset=0, column_offset=0, sign=1.0):
    points = matrix.shape[0]

    def digits(shape, axis):
        index = lax.broadcasted_iota(jnp.int32, shape, axis)
        return index, lax.rem(lax.div(index, stride), size)

    def picks(offset):
        _, digit = digits((extent, points), 0)
        point = lax.broadcasted_iota(jnp.int32, (extent, points), 1)
        return jnp.where(digit + offset == point, 1.0, 0.0)

    def transposed_dot(one, two):
        return lax.dot_general(
            one, two, (((1,), (1,)), ((), ())), precision=precise_mode,
            preferred_element_type=jnp.float32,
        )

    picked = picks(row_offset)
    picked = 0.5 * (precise_dot(picked, matrix) + sign * transposed_dot(picked, matrix))
    spread = transposed_dot(picked, picks(column_offset))
    row, row_digit = digits((extent, extent), 0)
    column, column_digit = digits((extent, extent), 1)
    same = (row - row_digit * stride) == (column - column_digit * stride)
    return jnp.where(same, spread, 0.0)


def operators_kernel(
    points, group, at_ref, coupling_ref, one_ref, two_ref, three_ref, four_ref, five_ref, six_ref,
    der_ref, *refs,
):
    left_ref, mode_ref, tail_ref, near_ref = refs[-4:]
    points_one, points_two, points_three = points
    rows = points_one * points_two * points_three
    stride = points_two * points_three
    mine = at_ref[1] * points_two
    left_ref[0] = kron_term(two_ref[...], points_two, points_three, rows, mine, mine) + kron_term(
        three_ref[...], points_three, 1, rows
    )
    if group > 1:
        sibling = at_ref[2] * points_two
        left_ref[1] = kron_term(two_ref[...], points_two, points_three, rows, mine, sibling)
    mode_ref[...] = kron_term(one_ref[...], one_ref.shape[0], stride, mode_ref.shape[0])
    width = tail_ref.shape[0]
    fives, sixes = five_ref.shape[0], six_ref.shape[0]
    tail_ref[...] = (
        kron_term(four_ref[...], four_ref.shape[0], fives * sixes, width)
        + kron_term(five_ref[...], fives, sixes, width)
        + kron_term(six_ref[...], sixes, 1, width)
    )
    twist = kron_term(der_ref[...], sixes, 1, near_ref.shape[1], sign=-1.0)
    block = at_ref[0]
    even = lax.rem(block, 2) == 0
    from_above = -coupling_ref[0, block]
    from_below = coupling_ref[0, jnp.maximum(block - 1, 0)]
    near_ref[0] = jnp.where(even, from_above, from_below) * twist
    near_ref[1] = jnp.where(even, from_below, from_above) * twist


def operators(points, group, mode_extent, width, span, at, coupling, matrices, after):
    rows = points[0] * points[1] * points[2]
    shapes = [
        (group, rows, rows), (mode_extent, mode_extent), (width, width), (2, span, span)
    ]
    smem = pl.BlockSpec(memory_space=pltpu.SMEM)
    return pl.pallas_call(
        functools.partial(operators_kernel, points, group),
        in_specs=[smem, smem]
        + [pl.BlockSpec(memory_space=pltpu.VMEM)] * len(matrices)
        + [pl.BlockSpec(memory_space=pl.ANY)] * len(after),
        out_specs=[pl.BlockSpec(memory_space=pltpu.VMEM)] * len(shapes),
        out_shape=[jax.ShapeDtypeStruct(shape, jnp.float32) for shape in shapes],
        compiler_params=pltpu.CompilerParams(vmem_limit_bytes=VMEM_BYTES),
        cost_estimate=pl.CostEstimate(
            flops=500_000_000, bytes_accessed=4_000_000, transcendentals=0
        ),
        name="operators",
    )(at, coupling, *matrices, *after)


def crossing_kernel(points, group, at_ref, two_ref, *refs):
    points_one, points_two, points_three = points
    held_refs, out_refs = refs[:group], refs[group:]
    owners = [at_ref[1], at_ref[2]][:group]
    peers = two_ref.shape[0] // points_two
    stride = points_two * points_three
    for number, out_ref in enumerate(out_refs):
        target = lax.rem(at_ref[1] + group * (number + 1), peers) * points_two
        coefs = {
            (a, k, b): 0.5
            * (
                two_ref[target + a, owners[k] * points_two + b]
                + two_ref[owners[k] * points_two + b, target + a]
            )
            for a in range(points_two)
            for k in range(group)
            for b in range(points_two)
        }
        for start in range(0, points_one * stride, stride):
            for _, lanes in tiles(SUBLANES, out_ref.shape[2]):
                for inner in range(0, points_three, SUBLANES):
                    values = {
                        (k, b): held_refs[k][0, pl.ds(start + b * points_three + inner, SUBLANES), lanes]
                        for k in range(group)
                        for b in range(points_two)
                    }
                    for a in range(points_two):
                        total = None
                        for (k, b), value in values.items():
                            term = coefs[a, k, b] * value
                            total = term if total is None else total + term
                        out_ref[0, pl.ds(start + a * points_three + inner, SUBLANES), lanes] = total


def crossing(points, at, two, held, count):
    nvec, rows, width = held[0].shape
    one = pl.BlockSpec((1, rows, width), lambda i: (i, 0, 0))
    smem = pl.BlockSpec(memory_space=pltpu.SMEM)
    return pl.pallas_call(
        functools.partial(crossing_kernel, points, len(held)),
        grid=(nvec,),
        in_specs=[smem, smem] + [one] * len(held),
        out_specs=[one] * count,
        out_shape=[jax.ShapeDtypeStruct(held[0].shape, jnp.float32)] * count,
        compiler_params=pltpu.CompilerParams(vmem_limit_bytes=VMEM_BYTES),
        cost_estimate=pl.CostEstimate(
            flops=2 * held[0].size * points[1] * len(held) * count,
            bytes_accessed=4 * held[0].size * (len(held) + count),
            transcendentals=0,
        ),
        name="crossing",
    )(at, two, *held)


def local_kernel(nvec, nblocks, group, at_ref, rot_ref, beta_ref, *refs):
    held_refs = refs[:group]
    old_ref, pot_ref, left_ref, tail_ref, out_ref = refs[group:]
    me = pl.program_id(0)
    block = at_ref[0]
    level = (block - nblocks // 2).astype(jnp.float32)
    current = held_refs[0][0]
    total = (pot_ref[...] + rot_ref[block] * level * level) * current
    for j in range(nvec):
        total = total - beta_ref[me, j] * old_ref[j]
    total = total + precise_dot(current, tail_ref[...])
    for number, held_ref in enumerate(held_refs):
        total = total + precise_dot(left_ref[number], held_ref[0])
    out_ref[0] = total


def local_terms(nblocks, at, rot_const, beta, held, old, pot, left, tail):
    nvec, rows, width = old.shape
    one = pl.BlockSpec((1, rows, width), lambda i: (i, 0, 0))
    smem = pl.BlockSpec(memory_space=pltpu.SMEM)
    return pl.pallas_call(
        functools.partial(local_kernel, nvec, nblocks, len(held)),
        grid=(nvec,),
        in_specs=[smem, smem, smem]
        + [one] * len(held)
        + [
            whole_spec(old.shape),
            whole_spec(pot.shape),
            pl.BlockSpec((len(held), rows, rows), lambda i: (0, 0, 0)),
            whole_spec(tail.shape),
        ],
        out_specs=one,
        out_shape=jax.ShapeDtypeStruct(old.shape, jnp.float32),
        compiler_params=pltpu.CompilerParams(vmem_limit_bytes=VMEM_BYTES),
        cost_estimate=pl.CostEstimate(
            flops=12 * old.size * (rows * len(held) + width),
            bytes_accessed=4 * old.size * (2 + len(held)),
            transcendentals=0,
        ),
        name="local_terms",
    )(at, rot_const, beta, *held, old, pot, left, tail)


def mode_kinetic_kernel(peers, in_ref, mat_ref, out_ref):
    rows = in_ref.shape[2]
    field = jnp.concatenate([in_ref[peer, 0] for peer in range(peers)], axis=0)
    field = precise_dot(mat_ref[...], field)
    for peer in range(peers):
        out_ref[peer, 0] = field[peer * rows : (peer + 1) * rows]


def mode_kinetic(field, matrix, peers):
    nvec, rows, width = field.shape
    held = nvec // peers
    block = pl.BlockSpec((peers, 1, rows, width), lambda q: (0, q, 0, 0))
    out = pl.pallas_call(
        functools.partial(mode_kinetic_kernel, peers),
        grid=(held,),
        in_specs=[block, whole_spec(matrix.shape)],
        out_specs=block,
        out_shape=jax.ShapeDtypeStruct((peers, held, rows, width), jnp.float32),
        compiler_params=pltpu.CompilerParams(vmem_limit_bytes=VMEM_BYTES),
        cost_estimate=pl.CostEstimate(
            flops=12 * field.size * matrix.shape[0], bytes_accessed=8 * field.size, transcendentals=0
        ),
        name="mode_kinetic",
    )(field.reshape(peers, held, rows, width), matrix)
    return out.reshape(field.shape)


def join_kernel(starts, sum_count, at_ref, work_ref, cor_ref, near_ref, *refs):
    pieces = len(starts)
    first_refs, second_refs = refs[:pieces], refs[pieces : 2 * pieces]
    sum_refs = refs[2 * pieces : 2 * pieces + sum_count]
    out_ref = refs[-1]
    span = near_ref.shape[1]
    even = lax.rem(at_ref[0], 2) == 0
    for start, first_ref, second_ref in zip(starts, first_refs, second_refs):
        place = slice(start, start + first_ref.shape[1])
        for at in range(0, work_ref.shape[2], span):
            part = slice(at, at + span)
            total = work_ref[0, place, part]
            for sum_ref in sum_refs:
                total = total + sum_ref[0, place, part]
            twist_fn = cor_ref[place, part]
            if_even = jnp.where(even, twist_fn, 1.0)
            if_odd = jnp.where(even, 1.0, twist_fn)
            total = total + if_even * precise_dot(
                if_odd * first_ref[0, :, part], near_ref[0]
            )
            out_ref[0, place, part] = total + if_odd * precise_dot(
                if_even * second_ref[0, :, part], near_ref[1]
            )


def join_terms(at, work, cor, near, starts, first, second, sums):
    nvec, rows, width = work.shape
    one = pl.BlockSpec((1, rows, width), lambda i: (i, 0, 0))
    pieces = [pl.BlockSpec((1, b.shape[1], width), lambda i: (i, 0, 0)) for b in first]
    return pl.pallas_call(
        functools.partial(join_kernel, tuple(starts), len(sums)),
        grid=(nvec,),
        in_specs=[
            pl.BlockSpec(memory_space=pltpu.SMEM), one, whole_spec(cor.shape), whole_spec(near.shape)
        ]
        + pieces
        + pieces
        + [one] * len(sums),
        out_specs=one,
        out_shape=jax.ShapeDtypeStruct(work.shape, jnp.float32),
        compiler_params=pltpu.CompilerParams(vmem_limit_bytes=VMEM_BYTES),
        cost_estimate=pl.CostEstimate(
            flops=24 * work.size * near.shape[1], bytes_accessed=24 * work.size, transcendentals=0
        ),
        name="join_terms",
    )(at, work, cor, near, *first, *second, *sums)


def far_terms_kernel(
    nvec, start, coef_ref, work_ref, first_ref, second_ref, fn_ref, vec_ref, before_ref, out_ref,
    sum_ref, sums,
):
    del work_ref
    step = pl.program_id(0)
    _, block_rows, width = first_ref.shape

    @pl.when(step == 0)
    def _():
        sums[...] = jnp.zeros_like(sums)

    at = pl.multiple_of(start + step * block_rows, SUBLANES)
    places = []
    for rows_here, lanes in tiles(block_rows, width):
        place = (pl.ds(at + rows_here.start, SUBLANES), lanes)
        places.append(place)
        skip_fn = fn_ref[place]
        first_fn = coef_ref[0] * skip_fn
        second_fn = coef_ref[1] * skip_fn
        for i in range(nvec):
            out_ref[(i, *place)] = (
                out_ref[(i, *place)]
                + first_fn * first_ref[i, rows_here, lanes]
                + second_fn * second_ref[i, rows_here, lanes]
            )
    add_products(nvec, vec_ref, out_ref, sums, 0, places, False)
    add_products(nvec, out_ref, out_ref, sums, 1, places, True)

    @pl.when(step == pl.num_programs(0) - 1)
    def _():
        lane = lax.broadcasted_iota(jnp.int32, (nvec, LANES), 1)
        packed = before_ref[...]
        packed = packed + packed_columns(lambda i, j: sums[0, j * nvec + i], nvec, 0, lane)
        packed = packed + packed_columns(
            lambda i, j: sums[1, min(i, j) * nvec + max(i, j)], nvec, nvec, lane
        )
        sum_ref[...] = jnp.broadcast_to(packed[None], sum_ref.shape)


def far_terms(coef, work, first, second, skip_fn, vec, before, start, block_rows, copies):
    nvec, _, width = work.shape
    rows = first.shape[1]
    whole = pl.BlockSpec(memory_space=pltpu.VMEM)
    block = pl.BlockSpec((nvec, block_rows, width), lambda s: (0, s, 0))
    work, skip_fn, vec = (
        pltpu.with_memory_space_constraint(array, pltpu.VMEM) for array in (work, skip_fn, vec)
    )
    return pl.pallas_call(
        functools.partial(far_terms_kernel, nvec, start),
        grid=(rows // block_rows,),
        in_specs=[
            pl.BlockSpec(memory_space=pltpu.SMEM), whole, block, block, whole, whole, whole
        ],
        out_specs=[whole, whole],
        out_shape=[
            jax.ShapeDtypeStruct(work.shape, jnp.float32),
            jax.ShapeDtypeStruct((copies, nvec, LANES), jnp.float32),
        ],
        scratch_shapes=[pltpu.VMEM((2, nvec * nvec, SUBLANES, LANES), jnp.float32)],
        input_output_aliases={1: 0},
        compiler_params=pltpu.CompilerParams(vmem_limit_bytes=SMALL_VMEM_BYTES),
        cost_estimate=pl.CostEstimate(
            flops=3 * nvec * nvec * rows * width,
            bytes_accessed=20 * first.size,
            transcendentals=0,
        ),
        name="far_terms",
    )(coef, work, first, second, skip_fn, vec, before)


def small_dot(left, right):
    terms = [left[:, k : k + 1] * right[k : k + 1, :] for k in range(right.shape[0])]
    while len(terms) > 1:
        terms = [sum(terms[k + 1 : k + 2], terms[k]) for k in range(0, len(terms), 2)]
    return terms[0]


def small_algebra(nvec, count, packed):
    packed = packed * (1.0 / count)
    cross = packed.T[0:nvec, :]
    cross_turned = packed[:, 0:nvec]
    work_gram = packed[:, nvec : 2 * nvec]
    vec_gram = packed[:, 2 * nvec : 3 * nvec]
    total = 2.0 * cross - small_dot(vec_gram, cross)
    total_turned = 2.0 * cross_turned - small_dot(cross_turned, vec_gram)
    gram = work_gram - small_dot(total_turned, cross) - small_dot(cross_turned, total)
    gram = gram + small_dot(total_turned, small_dot(vec_gram, total))
    row = lax.broadcasted_iota(jnp.int32, (nvec, nvec), 0)
    column = lax.broadcasted_iota(jnp.int32, (nvec, nvec), 1)
    inverse = jnp.where(row == column, 1.0, 0.0)
    lower = jnp.zeros((nvec, nvec), jnp.float32)
    for at in range(nvec):
        pivot = gram[at : at + 1, at : at + 1]
        scale = lax.rsqrt(pivot)
        scale = scale * (1.5 - 0.5 * pivot * scale * scale)
        scaled = gram[:, at : at + 1] * scale
        lower = jnp.where((column == at) & (row >= at), scaled, lower)
        pivot_row = inverse[at : at + 1, :] * scale
        factor = jnp.where(row > at, scaled, 0.0)
        inverse = jnp.where(row == at, pivot_row, inverse - factor * pivot_row)
        gram = gram - factor * (gram[at : at + 1, :] * scale)
    return total, lower, inverse, -small_dot(inverse, total_turned)


def basis_kernel(
    nvec, count, sum_ref, work_ref, part_ref, out_ref, alpha_ref, lower_ref, coefs, left
):
    block_rows = out_ref.shape[1]
    held = nvec * block_rows

    @pl.when(pl.program_id(0) == 0)
    def _():
        packed = sum_ref[0]
        for other in range(1, sum_ref.shape[0]):
            packed = packed + sum_ref[other]
        total, lower, inverse, mixing = small_algebra(nvec, count, packed)
        alpha_ref[...] = total
        lower_ref[...] = lower
        column = lax.broadcasted_iota(jnp.int32, (nvec, held), 1)
        row = lax.broadcasted_iota(jnp.int32, (nvec, held), 0)
        spread = precise_dot(mixing, jnp.where(lax.div(column, block_rows) == row, 1.0, 0.0))
        column = lax.broadcasted_iota(jnp.int32, (block_rows, held), 1)
        row = lax.broadcasted_iota(jnp.int32, (block_rows, held), 0)
        same = lax.rem(column, block_rows) == row
        for i in range(nvec):
            piece = parts_of(jnp.where(same, spread[i : i + 1, :], 0.0))
            for number, (ours, _) in enumerate(PART_PAIRS):
                left[
                    i * block_rows : (i + 1) * block_rows, number * held : (number + 1) * held
                ] = piece[ours]
            for j in range(i + 1):
                coefs[i * nvec + j] = jnp.broadcast_to(
                    inverse[i : i + 1, j : j + 1], (SUBLANES, LANES)
                )

    start = pl.multiple_of(pl.program_id(0) * block_rows, block_rows)
    parts = [
        part_ref[number, :, pl.ds(start, block_rows), :].reshape(held, out_ref.shape[2])
        for number in range(3)
    ]
    mixed = jnp.dot(
        left[...],
        jnp.concatenate([parts[theirs] for _, theirs in PART_PAIRS], axis=0),
        preferred_element_type=jnp.float32,
    )
    out_ref[...] = mixed.reshape(out_ref.shape)
    places = tiles(*out_ref.shape[1:])
    for at in range(0, len(places), 4):
        group = places[at : at + 4]
        for ours in vector_groups(nvec):
            totals = {(i, spot): out_ref[(i, *place)] for i in ours for spot, place in enumerate(group)}
            for j in range(ours[-1] + 1):
                values = [
                    work_ref[j, pl.ds(start + place.start, SUBLANES), lanes] for place, lanes in group
                ]
                for i in ours:
                    if j <= i:
                        coef = coefs[i * nvec + j]
                        for spot, value in enumerate(values):
                            totals[i, spot] = totals[i, spot] + coef * value
            for i in ours:
                for spot, place in enumerate(group):
                    out_ref[(i, *place)] = totals[i, spot]


def basis_of(count, sums, work, vec_parts, block_rows):
    nvec, rows, width = work.shape
    block = pl.BlockSpec((nvec, block_rows, width), lambda s: (0, s, 0))
    small = jax.ShapeDtypeStruct((nvec, nvec), jnp.float32)
    whole = pl.BlockSpec(memory_space=pltpu.VMEM)
    work, vec_parts = (
        pltpu.with_memory_space_constraint(array, pltpu.VMEM) for array in (work, vec_parts)
    )
    return pl.pallas_call(
        functools.partial(basis_kernel, nvec, count),
        grid=(rows // block_rows,),
        in_specs=[whole, whole, whole],
        out_specs=[block, whole_spec(small.shape), whole_spec(small.shape)],
        out_shape=[jax.ShapeDtypeStruct(work.shape, jnp.float32), small, small],
        scratch_shapes=[
            pltpu.VMEM((nvec * nvec, SUBLANES, LANES), jnp.float32),
            pltpu.VMEM(
                (nvec * block_rows, len(PART_PAIRS) * nvec * block_rows), jnp.bfloat16
            ),
        ],
        compiler_params=pltpu.CompilerParams(vmem_limit_bytes=SMALL_VMEM_BYTES),
        cost_estimate=pl.CostEstimate(
            flops=4 * nvec * work.size, bytes_accessed=12 * work.size, transcendentals=0
        ),
        name="basis",
    )(sums, work, vec_parts)


def shards(
    vectors,
    previous,
    beta,
    potential,
    coriolis_fn,
    second_fn,
    rot_const,
    coupling,
    kin_one,
    kin_two,
    kin_three,
    kin_four,
    kin_five,
    kin_six,
    coriolis_derivative,
):
    _, nvec, *points, width = vectors.shape
    rows = points[0] * points[1] * points[2]
    devices = lax.axis_size(ALL_AXES)
    block_index = lax.axis_index("ka")
    nblocks = lax.axis_size("ka")
    row_peers = lax.axis_size("row")
    mode_peers = lax.axis_size("mode")
    row_at = lax.axis_index("row")
    current = vectors.reshape(nvec, rows, width)
    older = previous.reshape(nvec, rows, width)
    block_rows = min(32, rows // 2)

    cut = rows * 3 // 4 // block_rows * block_rows or rows // 2
    starts, stops = [0, cut], [cut, rows]
    parts = [split_rows(current, start, stop) for start, stop in zip(starts, stops)]
    near_first = [pair_exchange(part, "ka", 0) for part in parts]
    near_second = [pair_exchange(part, "ka", 1) for part in parts]
    at = jnp.stack([block_index, row_at, row_at ^ 1]).astype(jnp.int32)
    group = 2 - row_peers % 2
    held = [current]
    if group == 2:
        held.append(lax.ppermute(current, "row", [(i, i ^ 1) for i in range(row_peers)]))
    away = row_peers // group - 1
    row_parts = crossing(tuple(points), at, kin_two, held, away) if away else []
    row_sums = [
        lax.ppermute(
            part, "row", [(i, (i + group * (number + 1)) % row_peers) for i in range(row_peers)]
        )
        for number, part in enumerate(row_parts)
    ]

    span = next((s for s in (256, 128) if width % s == 0 and s % kin_six.shape[0] == 0), width)
    left, mode_mat, tail, near = operators(
        tuple(points),
        group,
        mode_peers * rows,
        width,
        span,
        at,
        coupling,
        (kin_one, kin_two, kin_three, kin_four, kin_five, kin_six, coriolis_derivative),
        row_parts,
    )
    near_first[0] = handed_on(near_first[0], HOP_WEIGHT, [*row_parts, mode_mat])
    near_second[0] = handed_on(near_second[0], HOP_WEIGHT, [*row_parts, mode_mat])
    far_first = [pair_exchange(part, "ka", 0) for part in near_second]
    far_second = [pair_exchange(part, "ka", 1) for part in near_first]
    lower_two = jnp.maximum(block_index - 2, 0)
    far_above, far_below = coupling[1, block_index], coupling[1, lower_two]
    even = block_index % 2 == 0
    far_pair = jnp.stack(
        [jnp.where(even, far_above, far_below), jnp.where(even, far_below, far_above)]
    )
    sums, vec, vec_parts, skip_fn = resident(
        current, second_fn.reshape(rows, width), held[1:], block_rows
    )
    mode_shares = lax.all_to_all(vec, "mode", split_axis=0, concat_axis=0, tiled=True)
    mode_shares = mode_kinetic(mode_shares, mode_mat, mode_peers)
    mode_sum = lax.all_to_all(mode_shares, "mode", split_axis=0, concat_axis=0, tiled=True)
    work = local_terms(
        nblocks, at, rot_const, beta, held, older, potential.reshape(rows, width), left, tail
    )
    work = join_terms(
        at,
        work,
        coriolis_fn.reshape(rows, width),
        near,
        starts,
        near_first,
        near_second,
        [mode_sum, *row_sums],
    )
    for number, start in enumerate(starts):
        work, copied = far_terms(
            far_pair,
            work,
            far_first[number],
            far_second[number],
            skip_fn,
            vec,
            sums,
            start,
            block_rows,
            devices if number == len(starts) - 1 else 1,
        )
        sums = copied[0]
    every_sum = lax.all_to_all(copied, ALL_AXES, split_axis=0, concat_axis=0, tiled=True)
    count = float(devices * rows * width)
    basis, alpha, lower = basis_of(count, every_sum, work, vec_parts, block_rows)
    return (basis.reshape(vectors.shape), alpha, lower)


def solution(mesh):
    return jax.shard_map(
        shards,
        mesh=mesh,
        in_specs=(
            P("ka", None, "mode", "row", None, None),
            P("ka", None, "mode", "row", None, None),
            P(),
            P("mode", "row", None, None),
            P("mode", "row", None, None),
            P("mode", "row", None, None),
            P(),
            P(),
            P(),
            P(),
            P(),
            P(),
            P(),
            P(),
            P(),
        ),
        out_specs=(P("ka", None, "mode", "row", None, None), P(), P()),
        check_vma=False,
    )
```

```python
import functools

import jax
import jax.numpy as jnp
from jax import lax
from jax.experimental import pallas as pl
from jax.experimental.pallas import tpu as pltpu
from jax.sharding import PartitionSpec as P

precise_mode = lax.Precision.HIGHEST
ALL_AXES = ("ka", "mode", "row")
VMEM_BYTES = 32 * 1024 * 1024
SMALL_VMEM_BYTES = 16 * 1024 * 1024
FULL_VMEM_BYTES = 56 * 1024 * 1024
LANES = 128
HOP_WEIGHT = 25_000_000_000
SUBLANES = 8


def precise_dot(left, right):
    return jnp.dot(left, right, precision=precise_mode, preferred_element_type=jnp.float32)


def whole_spec(shape):
    return pl.BlockSpec(shape, lambda *_: (0,) * len(shape))


def pair_exchange(value, axis, first):
    peers = lax.axis_size(axis)
    pairs = []
    for low in range(first, peers - 1, 2):
        pairs += [(low, low + 1), (low + 1, low)]
    return lax.ppermute(value, axis, pairs)


def vector_groups(nvec):
    return [tuple(range(at, min(at + 4, nvec))) for at in range(0, nvec, 4)]


def tiles(rows, width):
    return [
        (slice(r, r + SUBLANES), slice(c, c + LANES))
        for r in range(0, rows, SUBLANES)
        for c in range(0, width, LANES)
    ]


def packed_columns(sums, nvec, offset, lane):
    packed = jnp.zeros((nvec, LANES), jnp.float32)
    for j in range(nvec):
        stacked = jnp.stack([sums(i, j) for i in range(nvec)])
        column = jnp.sum(jnp.sum(stacked, axis=1), axis=1, keepdims=True)
        packed = packed + jnp.where(lane == offset + j, column, 0.0)
    return packed


def add_products(nvec, left_ref, right_ref, sums, number, places, symmetric):
    groups = vector_groups(nvec)
    for ours in groups:
        for other in groups:
            pairs = [(i, j) for i in ours for j in other if i <= j or not symmetric]
            if not pairs:
                continue
            totals = {pair: sums[number, pair[0] * nvec + pair[1]] for pair in pairs}
            for place in places:
                lefts = {i: left_ref[(i, *place)] for i in {p[0] for p in pairs}}
                rights = {j: right_ref[(j, *place)] for j in {p[1] for p in pairs}}
                for i, j in pairs:
                    totals[i, j] = totals[i, j] + lefts[i] * rights[j]
            for i, j in pairs:
                sums[number, i * nvec + j] = totals[i, j]


def resident_kernel(nvec, vec_ref, fn_ref, *refs):
    out_ref, copy_ref, fn_copy_ref, sums = refs[-4:]
    step = pl.program_id(0)

    @pl.when(step == 0)
    def _():
        sums[...] = jnp.zeros_like(sums)

    copy_ref[...] = vec_ref[...]
    fn_copy_ref[...] = fn_ref[...]
    add_products(nvec, vec_ref, vec_ref, sums, 0, tiles(*vec_ref.shape[1:]), True)

    @pl.when(step == pl.num_programs(0) - 1)
    def _():
        lane = lax.broadcasted_iota(jnp.int32, (nvec, LANES), 1)
        out_ref[...] = packed_columns(
            lambda i, j: sums[0, min(i, j) * nvec + max(i, j)], nvec, 2 * nvec, lane
        )


def resident(vec, skip_fn, after, block_rows):
    nvec, rows, width = vec.shape
    block = pl.BlockSpec((nvec, block_rows, width), lambda s: (0, s, 0))
    fn_block = pl.BlockSpec((block_rows, width), lambda s: (s, 0))
    return pl.pallas_call(
        functools.partial(resident_kernel, nvec),
        grid=(rows // block_rows,),
        in_specs=[block, fn_block] + [pl.BlockSpec(memory_space=pl.ANY)] * len(after),
        out_specs=[whole_spec((nvec, LANES)), block, fn_block],
        out_shape=[
            jax.ShapeDtypeStruct((nvec, LANES), jnp.float32),
            jax.ShapeDtypeStruct(vec.shape, jnp.float32),
            jax.ShapeDtypeStruct(skip_fn.shape, jnp.float32),
        ],
        scratch_shapes=[pltpu.VMEM((1, nvec * nvec, SUBLANES, LANES), jnp.float32)],
        compiler_params=pltpu.CompilerParams(vmem_limit_bytes=VMEM_BYTES),
        cost_estimate=pl.CostEstimate(
            flops=nvec * (nvec + 1) * rows * width, bytes_accessed=8 * vec.size, transcendentals=0
        ),
        name="resident",
    )(vec, skip_fn, *after)


def split_kernel(start, parts, vec_ref, out_ref, held, sems):
    count, rows, _ = out_ref.shape
    size = rows // parts
    spots = [(i, p, pl.ds(p * size, size)) for i in range(count) for p in range(parts)]
    loads = [
        pltpu.make_async_copy(
            vec_ref.at[i, pl.ds(start + p * size, size)], held.at[i, place], sems.at[0, i, p]
        )
        for i, p, place in spots
    ]
    stores = [
        pltpu.make_async_copy(held.at[i, place], out_ref.at[i, place], sems.at[1, i, p])
        for i, p, place in spots
    ]
    for load in loads:
        load.start()
    for load, store in zip(loads, stores):
        load.wait()
        store.start()
    for store in stores:
        store.wait()


def split_rows(vec, start, stop):
    nvec, _, width = vec.shape
    shape = (nvec, stop - start, width)
    parts = next(p for p in (4, 2, 1) if shape[1] % (SUBLANES * p) == 0)
    return pl.pallas_call(
        functools.partial(split_kernel, start, parts),
        in_specs=[pl.BlockSpec(memory_space=pl.ANY)],
        out_specs=pl.BlockSpec(memory_space=pl.ANY),
        out_shape=jax.ShapeDtypeStruct(shape, jnp.float32),
        scratch_shapes=[
            pltpu.VMEM(shape, jnp.float32),
            pltpu.SemaphoreType.DMA((2, nvec, parts)),
        ],
        compiler_params=pltpu.CompilerParams(vmem_limit_bytes=FULL_VMEM_BYTES),
        cost_estimate=pl.CostEstimate(
            flops=0, bytes_accessed=8 * nvec * (stop - start) * width, transcendentals=0
        ),
        name="split_rows",
    )(vec)


def handed_on(array, weight, after=()):
    return pl.pallas_call(
        lambda *_: None,
        in_specs=[pl.BlockSpec(memory_space=pl.ANY)] * (1 + len(after)),
        out_specs=pl.BlockSpec(memory_space=pl.ANY),
        out_shape=jax.ShapeDtypeStruct(array.shape, array.dtype),
        input_output_aliases={0: 0},
        cost_estimate=pl.CostEstimate(flops=weight, bytes_accessed=0, transcendentals=0),
        name="handed_on",
    )(array, *after)


def kron_term(matrix, size, stride, extent, row_offset=0, column_offset=0, sign=1.0):
    points = matrix.shape[0]

    def digits(shape, axis):
        index = lax.broadcasted_iota(jnp.int32, shape, axis)
        return index, lax.rem(lax.div(index, stride), size)

    def picks(offset):
        _, digit = digits((extent, points), 0)
        point = lax.broadcasted_iota(jnp.int32, (extent, points), 1)
        return jnp.where(digit + offset == point, 1.0, 0.0)

    def transposed_dot(one, two):
        return lax.dot_general(
            one, two, (((1,), (1,)), ((), ())), precision=precise_mode,
            preferred_element_type=jnp.float32,
        )

    picked = picks(row_offset)
    picked = 0.5 * (precise_dot(picked, matrix) + sign * transposed_dot(picked, matrix))
    spread = transposed_dot(picked, picks(column_offset))
    row, row_digit = digits((extent, extent), 0)
    column, column_digit = digits((extent, extent), 1)
    same = (row - row_digit * stride) == (column - column_digit * stride)
    return jnp.where(same, spread, 0.0)


def operators_kernel(
    points, group, at_ref, coupling_ref, one_ref, two_ref, three_ref, four_ref, five_ref, six_ref,
    der_ref, *refs,
):
    left_ref, mode_ref, tail_ref, near_ref = refs[-4:]
    points_one, points_two, points_three = points
    rows = points_one * points_two * points_three
    stride = points_two * points_three
    mine = at_ref[1] * points_two
    left_ref[0] = kron_term(two_ref[...], points_two, points_three, rows, mine, mine) + kron_term(
        three_ref[...], points_three, 1, rows
    )
    if group > 1:
        sibling = at_ref[2] * points_two
        left_ref[1] = kron_term(two_ref[...], points_two, points_three, rows, mine, sibling)
    mode_ref[...] = kron_term(one_ref[...], one_ref.shape[0], stride, mode_ref.shape[0])
    width = tail_ref.shape[0]
    fives, sixes = five_ref.shape[0], six_ref.shape[0]
    tail_ref[...] = (
        kron_term(four_ref[...], four_ref.shape[0], fives * sixes, width)
        + kron_term(five_ref[...], fives, sixes, width)
        + kron_term(six_ref[...], sixes, 1, width)
    )
    twist = kron_term(der_ref[...], sixes, 1, near_ref.shape[1], sign=-1.0)
    block = at_ref[0]
    even = lax.rem(block, 2) == 0
    from_above = -coupling_ref[0, block]
    from_below = coupling_ref[0, jnp.maximum(block - 1, 0)]
    near_ref[0] = jnp.where(even, from_above, from_below) * twist
    near_ref[1] = jnp.where(even, from_below, from_above) * twist


def operators(points, group, mode_extent, width, span, at, coupling, matrices, after):
    rows = points[0] * points[1] * points[2]
    shapes = [
        (group, rows, rows), (mode_extent, mode_extent), (width, width), (2, span, span)
    ]
    smem = pl.BlockSpec(memory_space=pltpu.SMEM)
    return pl.pallas_call(
        functools.partial(operators_kernel, points, group),
        in_specs=[smem, smem]
        + [pl.BlockSpec(memory_space=pltpu.VMEM)] * len(matrices)
        + [pl.BlockSpec(memory_space=pl.ANY)] * len(after),
        out_specs=[pl.BlockSpec(memory_space=pltpu.VMEM)] * len(shapes),
        out_shape=[jax.ShapeDtypeStruct(shape, jnp.float32) for shape in shapes],
        compiler_params=pltpu.CompilerParams(vmem_limit_bytes=VMEM_BYTES),
        cost_estimate=pl.CostEstimate(
            flops=500_000_000, bytes_accessed=4_000_000, transcendentals=0
        ),
        name="operators",
    )(at, coupling, *matrices, *after)


def crossing_kernel(points, group, at_ref, two_ref, *refs):
    points_one, points_two, points_three = points
    held_refs, out_refs = refs[:group], refs[group:]
    owners = [at_ref[1], at_ref[2]][:group]
    peers = two_ref.shape[0] // points_two
    stride = points_two * points_three
    for number, out_ref in enumerate(out_refs):
        target = lax.rem(at_ref[1] + group * (number + 1), peers) * points_two
        coefs = {
            (a, k, b): 0.5
            * (
                two_ref[target + a, owners[k] * points_two + b]
                + two_ref[owners[k] * points_two + b, target + a]
            )
            for a in range(points_two)
            for k in range(group)
            for b in range(points_two)
        }
        for start in range(0, points_one * stride, stride):
            for _, lanes in tiles(SUBLANES, out_ref.shape[2]):
                for inner in range(0, points_three, SUBLANES):
                    values = {
                        (k, b): held_refs[k][0, pl.ds(start + b * points_three + inner, SUBLANES), lanes]
                        for k in range(group)
                        for b in range(points_two)
                    }
                    for a in range(points_two):
                        total = None
                        for (k, b), value in values.items():
                            term = coefs[a, k, b] * value
                            total = term if total is None else total + term
                        out_ref[0, pl.ds(start + a * points_three + inner, SUBLANES), lanes] = total


def crossing(points, at, two, held, count):
    nvec, rows, width = held[0].shape
    one = pl.BlockSpec((1, rows, width), lambda i: (i, 0, 0))
    smem = pl.BlockSpec(memory_space=pltpu.SMEM)
    return pl.pallas_call(
        functools.partial(crossing_kernel, points, len(held)),
        grid=(nvec,),
        in_specs=[smem, smem] + [one] * len(held),
        out_specs=[one] * count,
        out_shape=[jax.ShapeDtypeStruct(held[0].shape, jnp.float32)] * count,
        compiler_params=pltpu.CompilerParams(vmem_limit_bytes=VMEM_BYTES),
        cost_estimate=pl.CostEstimate(
            flops=2 * held[0].size * points[1] * len(held) * count,
            bytes_accessed=4 * held[0].size * (len(held) + count),
            transcendentals=0,
        ),
        name="crossing",
    )(at, two, *held)


def local_kernel(nvec, nblocks, group, at_ref, rot_ref, beta_ref, *refs):
    held_refs = refs[:group]
    old_ref, pot_ref, left_ref, tail_ref, out_ref = refs[group:]
    me = pl.program_id(0)
    block = at_ref[0]
    level = (block - nblocks // 2).astype(jnp.float32)
    current = held_refs[0][0]
    total = (pot_ref[...] + rot_ref[block] * level * level) * current
    for j in range(nvec):
        total = total - beta_ref[me, j] * old_ref[j]
    total = total + precise_dot(current, tail_ref[...])
    for number, held_ref in enumerate(held_refs):
        total = total + precise_dot(left_ref[number], held_ref[0])
    out_ref[0] = total


def local_terms(nblocks, at, rot_const, beta, held, old, pot, left, tail):
    nvec, rows, width = old.shape
    one = pl.BlockSpec((1, rows, width), lambda i: (i, 0, 0))
    smem = pl.BlockSpec(memory_space=pltpu.SMEM)
    return pl.pallas_call(
        functools.partial(local_kernel, nvec, nblocks, len(held)),
        grid=(nvec,),
        in_specs=[smem, smem, smem]
        + [one] * len(held)
        + [
            whole_spec(old.shape),
            whole_spec(pot.shape),
            pl.BlockSpec((len(held), rows, rows), lambda i: (0, 0, 0)),
            whole_spec(tail.shape),
        ],
        out_specs=one,
        out_shape=jax.ShapeDtypeStruct(old.shape, jnp.float32),
        compiler_params=pltpu.CompilerParams(vmem_limit_bytes=VMEM_BYTES),
        cost_estimate=pl.CostEstimate(
            flops=12 * old.size * (rows * len(held) + width),
            bytes_accessed=4 * old.size * (2 + len(held)),
            transcendentals=0,
        ),
        name="local_terms",
    )(at, rot_const, beta, *held, old, pot, left, tail)


def mode_kinetic_kernel(peers, in_ref, mat_ref, out_ref):
    rows = in_ref.shape[2]
    field = jnp.concatenate([in_ref[peer, 0] for peer in range(peers)], axis=0)
    field = precise_dot(mat_ref[...], field)
    for peer in range(peers):
        out_ref[peer, 0] = field[peer * rows : (peer + 1) * rows]


def mode_kinetic(field, matrix, peers):
    nvec, rows, width = field.shape
    held = nvec // peers
    block = pl.BlockSpec((peers, 1, rows, width), lambda q: (0, q, 0, 0))
    out = pl.pallas_call(
        functools.partial(mode_kinetic_kernel, peers),
        grid=(held,),
        in_specs=[block, whole_spec(matrix.shape)],
        out_specs=block,
        out_shape=jax.ShapeDtypeStruct((peers, held, rows, width), jnp.float32),
        compiler_params=pltpu.CompilerParams(vmem_limit_bytes=VMEM_BYTES),
        cost_estimate=pl.CostEstimate(
            flops=12 * field.size * matrix.shape[0], bytes_accessed=8 * field.size, transcendentals=0
        ),
        name="mode_kinetic",
    )(field.reshape(peers, held, rows, width), matrix)
    return out.reshape(field.shape)


def join_kernel(starts, sum_count, at_ref, work_ref, cor_ref, near_ref, *refs):
    pieces = len(starts)
    first_refs, second_refs = refs[:pieces], refs[pieces : 2 * pieces]
    sum_refs = refs[2 * pieces : 2 * pieces + sum_count]
    out_ref = refs[-1]
    span = near_ref.shape[1]
    even = lax.rem(at_ref[0], 2) == 0
    for start, first_ref, second_ref in zip(starts, first_refs, second_refs):
        place = slice(start, start + first_ref.shape[1])
        for at in range(0, work_ref.shape[2], span):
            part = slice(at, at + span)
            total = work_ref[0, place, part]
            for sum_ref in sum_refs:
                total = total + sum_ref[0, place, part]
            twist_fn = cor_ref[place, part]
            if_even = jnp.where(even, twist_fn, 1.0)
            if_odd = jnp.where(even, 1.0, twist_fn)
            total = total + if_even * precise_dot(
                if_odd * first_ref[0, :, part], near_ref[0]
            )
            out_ref[0, place, part] = total + if_odd * precise_dot(
                if_even * second_ref[0, :, part], near_ref[1]
            )


def join_terms(at, work, cor, near, starts, first, second, sums):
    nvec, rows, width = work.shape
    one = pl.BlockSpec((1, rows, width), lambda i: (i, 0, 0))
    pieces = [pl.BlockSpec((1, b.shape[1], width), lambda i: (i, 0, 0)) for b in first]
    return pl.pallas_call(
        functools.partial(join_kernel, tuple(starts), len(sums)),
        grid=(nvec,),
        in_specs=[
            pl.BlockSpec(memory_space=pltpu.SMEM), one, whole_spec(cor.shape), whole_spec(near.shape)
        ]
        + pieces
        + pieces
        + [one] * len(sums),
        out_specs=one,
        out_shape=jax.ShapeDtypeStruct(work.shape, jnp.float32),
        compiler_params=pltpu.CompilerParams(vmem_limit_bytes=VMEM_BYTES),
        cost_estimate=pl.CostEstimate(
            flops=24 * work.size * near.shape[1], bytes_accessed=24 * work.size, transcendentals=0
        ),
        name="join_terms",
    )(at, work, cor, near, *first, *second, *sums)


def far_terms_kernel(
    nvec, start, coef_ref, work_ref, first_ref, second_ref, fn_ref, vec_ref, before_ref, out_ref,
    sum_ref, sums,
):
    del work_ref
    step = pl.program_id(0)
    _, block_rows, width = first_ref.shape

    @pl.when(step == 0)
    def _():
        sums[...] = jnp.zeros_like(sums)

    at = pl.multiple_of(start + step * block_rows, SUBLANES)
    places = []
    for rows_here, lanes in tiles(block_rows, width):
        place = (pl.ds(at + rows_here.start, SUBLANES), lanes)
        places.append(place)
        skip_fn = fn_ref[place]
        first_fn = coef_ref[0] * skip_fn
        second_fn = coef_ref[1] * skip_fn
        for i in range(nvec):
            out_ref[(i, *place)] = (
                out_ref[(i, *place)]
                + first_fn * first_ref[i, rows_here, lanes]
                + second_fn * second_ref[i, rows_here, lanes]
            )
    add_products(nvec, vec_ref, out_ref, sums, 0, places, False)
    add_products(nvec, out_ref, out_ref, sums, 1, places, True)

    @pl.when(step == pl.num_programs(0) - 1)
    def _():
        lane = lax.broadcasted_iota(jnp.int32, (nvec, LANES), 1)
        packed = before_ref[...]
        packed = packed + packed_columns(lambda i, j: sums[0, j * nvec + i], nvec, 0, lane)
        packed = packed + packed_columns(
            lambda i, j: sums[1, min(i, j) * nvec + max(i, j)], nvec, nvec, lane
        )
        sum_ref[...] = jnp.broadcast_to(packed[None], sum_ref.shape)


def far_terms(coef, work, first, second, skip_fn, vec, before, start, block_rows, copies):
    nvec, _, width = work.shape
    rows = first.shape[1]
    whole = pl.BlockSpec(memory_space=pltpu.VMEM)
    block = pl.BlockSpec((nvec, block_rows, width), lambda s: (0, s, 0))
    work, skip_fn, vec = (
        pltpu.with_memory_space_constraint(array, pltpu.VMEM) for array in (work, skip_fn, vec)
    )
    return pl.pallas_call(
        functools.partial(far_terms_kernel, nvec, start),
        grid=(rows // block_rows,),
        in_specs=[
            pl.BlockSpec(memory_space=pltpu.SMEM), whole, block, block, whole, whole, whole
        ],
        out_specs=[whole, whole],
        out_shape=[
            jax.ShapeDtypeStruct(work.shape, jnp.float32),
            jax.ShapeDtypeStruct((copies, nvec, LANES), jnp.float32),
        ],
        scratch_shapes=[pltpu.VMEM((2, nvec * nvec, SUBLANES, LANES), jnp.float32)],
        input_output_aliases={1: 0},
        compiler_params=pltpu.CompilerParams(vmem_limit_bytes=SMALL_VMEM_BYTES),
        cost_estimate=pl.CostEstimate(
            flops=3 * nvec * nvec * rows * width,
            bytes_accessed=20 * first.size,
            transcendentals=0,
        ),
        name="far_terms",
    )(coef, work, first, second, skip_fn, vec, before)


def across(column, row):
    return jnp.broadcast_to(column[row : row + 1, :], (SUBLANES, LANES))


def spread_columns(matrix, start, count):
    return [
        jnp.broadcast_to(matrix[:, k : k + 1], (count, LANES)) for k in range(start, start + count)
    ]


def spread_dot(left, right):
    count = len(left)
    columns = []
    for column in right:
        terms = [left[m] * jnp.broadcast_to(column[m : m + 1, :], left[m].shape) for m in range(count)]
        while len(terms) > 1:
            terms = [sum(terms[k + 1 : k + 2], terms[k]) for k in range(0, len(terms), 2)]
        columns.append(terms[0])
    return columns


def small_algebra(nvec, count, packed):
    packed = packed * (1.0 / count)
    cross = spread_columns(packed.T[0:nvec, :], 0, nvec)
    cross_turned = spread_columns(packed, 0, nvec)
    gram = spread_columns(packed, nvec, nvec)
    vec_gram = spread_columns(packed, 2 * nvec, nvec)
    total = [2.0 * c - d for c, d in zip(cross, spread_dot(vec_gram, cross))]
    total_turned = [2.0 * c - d for c, d in zip(cross_turned, spread_dot(cross_turned, vec_gram))]
    inner = [d - c for c, d in zip(cross, spread_dot(vec_gram, total))]
    gram = [
        g - one + other
        for g, one, other in zip(
            gram, spread_dot(cross_turned, total), spread_dot(total_turned, inner)
        )
    ]
    row = lax.broadcasted_iota(jnp.int32, (nvec, LANES), 0)
    inverse = [jnp.where(row == k, 1.0, 0.0) for k in range(nvec)]
    lower = []
    for at in range(nvec):
        pivot = jnp.broadcast_to(gram[at][at : at + 1, :], (nvec, LANES))
        scale = lax.rsqrt(pivot)
        scale = scale * (1.5 - 0.5 * pivot * scale * scale)
        scaled = gram[at] * scale
        lower.append(jnp.where(row >= at, scaled, 0.0))
        factor = jnp.where(row > at, scaled, 0.0)
        for k in range(at + 1, nvec):
            here = jnp.broadcast_to(gram[k][at : at + 1, :], (nvec, LANES)) * scale
            gram[k] = gram[k] - factor * here
        for k in range(at + 1):
            here = jnp.broadcast_to(inverse[k][at : at + 1, :], (nvec, LANES)) * scale
            inverse[k] = jnp.where(row == at, here, inverse[k] - factor * here)
    mixing = [-column for column in spread_dot(inverse, total_turned)]
    return total, lower, inverse, mixing


def gathered_columns(columns):
    lane = lax.broadcasted_iota(jnp.int32, columns[0].shape, 1)
    matrix = jnp.zeros_like(columns[0])
    for k, column in enumerate(columns):
        matrix = jnp.where(lane == k, column, matrix)
    return matrix[:, : len(columns)]


def basis_kernel(nvec, count, sum_ref, work_ref, vec_ref, out_ref, alpha_ref, lower_ref, coefs):
    @pl.when(pl.program_id(0) == 0)
    def _():
        packed = sum_ref[0]
        for other in range(1, sum_ref.shape[0]):
            packed = packed + sum_ref[other]
        total, lower, inverse, mixing = small_algebra(nvec, count, packed)
        for number, columns in enumerate((inverse, mixing)):
            for j in range(nvec):
                for i in range(nvec):
                    if number == 1 or j <= i:
                        coefs[number, i * nvec + j] = across(columns[j], i)
        alpha_ref[...] = gathered_columns(total)
        lower_ref[...] = gathered_columns(lower)

    start = pl.multiple_of(pl.program_id(0) * out_ref.shape[1], out_ref.shape[1])
    places = tiles(*out_ref.shape[1:])
    for at in range(0, len(places), 4):
        group = places[at : at + 4]
        held = [(pl.ds(start + place.start, SUBLANES), lanes) for place, lanes in group]
        totals = {}
        for number, ref in ((1, vec_ref), (0, work_ref)):
            for j in range(nvec):
                values = [ref[(j, *place)] for place in held]
                for i in range(nvec):
                    if number == 0 and j > i:
                        continue
                    coef = coefs[number, i * nvec + j]
                    for spot, value in enumerate(values):
                        term = coef * value
                        here = (i, spot)
                        totals[here] = totals[here] + term if here in totals else term
        for (i, spot), value in totals.items():
            out_ref[(i, *group[spot])] = value


def basis_of(count, sums, work, vec, block_rows):
    nvec, rows, width = work.shape
    block = pl.BlockSpec((nvec, block_rows, width), lambda s: (0, s, 0))
    small = jax.ShapeDtypeStruct((nvec, nvec), jnp.float32)
    whole = pl.BlockSpec(memory_space=pltpu.VMEM)
    work, vec = (pltpu.with_memory_space_constraint(array, pltpu.VMEM) for array in (work, vec))
    return pl.pallas_call(
        functools.partial(basis_kernel, nvec, count),
        grid=(rows // block_rows,),
        in_specs=[whole, whole, whole],
        out_specs=[block, whole_spec(small.shape), whole_spec(small.shape)],
        out_shape=[jax.ShapeDtypeStruct(work.shape, jnp.float32), small, small],
        scratch_shapes=[pltpu.VMEM((2, nvec * nvec, SUBLANES, LANES), jnp.float32)],
        compiler_params=pltpu.CompilerParams(vmem_limit_bytes=SMALL_VMEM_BYTES),
        cost_estimate=pl.CostEstimate(
            flops=4 * nvec * work.size, bytes_accessed=12 * work.size, transcendentals=0
        ),
        name="basis",
    )(sums, work, vec)


def shards(
    vectors,
    previous,
    beta,
    potential,
    coriolis_fn,
    second_fn,
    rot_const,
    coupling,
    kin_one,
    kin_two,
    kin_three,
    kin_four,
    kin_five,
    kin_six,
    coriolis_derivative,
):
    _, nvec, *points, width = vectors.shape
    rows = points[0] * points[1] * points[2]
    devices = lax.axis_size(ALL_AXES)
    block_index = lax.axis_index("ka")
    nblocks = lax.axis_size("ka")
    row_peers = lax.axis_size("row")
    mode_peers = lax.axis_size("mode")
    row_at = lax.axis_index("row")
    current = vectors.reshape(nvec, rows, width)
    older = previous.reshape(nvec, rows, width)
    block_rows = min(32, rows // 2)

    cut = rows * 3 // 4 // block_rows * block_rows or rows // 2
    starts, stops = [0, cut], [cut, rows]
    parts = [split_rows(current, start, stop) for start, stop in zip(starts, stops)]
    near_first = [pair_exchange(part, "ka", 0) for part in parts]
    near_second = [pair_exchange(part, "ka", 1) for part in parts]
    at = jnp.stack([block_index, row_at, row_at ^ 1]).astype(jnp.int32)
    group = 2 - row_peers % 2
    held = [current]
    if group == 2:
        held.append(lax.ppermute(current, "row", [(i, i ^ 1) for i in range(row_peers)]))
    away = row_peers // group - 1
    row_parts = crossing(tuple(points), at, kin_two, held, away) if away else []
    row_sums = [
        lax.ppermute(
            part, "row", [(i, (i + group * (number + 1)) % row_peers) for i in range(row_peers)]
        )
        for number, part in enumerate(row_parts)
    ]

    span = next((s for s in (256, 128) if width % s == 0 and s % kin_six.shape[0] == 0), width)
    left, mode_mat, tail, near = operators(
        tuple(points),
        group,
        mode_peers * rows,
        width,
        span,
        at,
        coupling,
        (kin_one, kin_two, kin_three, kin_four, kin_five, kin_six, coriolis_derivative),
        row_parts,
    )
    near_first[0] = handed_on(near_first[0], HOP_WEIGHT, [*row_parts, mode_mat])
    near_second[0] = handed_on(near_second[0], HOP_WEIGHT, [*row_parts, mode_mat])
    far_first = [pair_exchange(part, "ka", 0) for part in near_second]
    far_second = [pair_exchange(part, "ka", 1) for part in near_first]
    lower_two = jnp.maximum(block_index - 2, 0)
    far_above, far_below = coupling[1, block_index], coupling[1, lower_two]
    even = block_index % 2 == 0
    far_pair = jnp.stack(
        [jnp.where(even, far_above, far_below), jnp.where(even, far_below, far_above)]
    )
    sums, vec, skip_fn = resident(
        current, second_fn.reshape(rows, width), held[1:], block_rows
    )
    mode_shares = lax.all_to_all(vec, "mode", split_axis=0, concat_axis=0, tiled=True)
    mode_shares = mode_kinetic(mode_shares, mode_mat, mode_peers)
    mode_sum = lax.all_to_all(mode_shares, "mode", split_axis=0, concat_axis=0, tiled=True)
    work = local_terms(
        nblocks, at, rot_const, beta, held, older, potential.reshape(rows, width), left, tail
    )
    work = join_terms(
        at,
        work,
        coriolis_fn.reshape(rows, width),
        near,
        starts,
        near_first,
        near_second,
        [mode_sum, *row_sums],
    )
    for number, start in enumerate(starts):
        work, copied = far_terms(
            far_pair,
            work,
            far_first[number],
            far_second[number],
            skip_fn,
            vec,
            sums,
            start,
            block_rows,
            devices if number == len(starts) - 1 else 1,
        )
        sums = copied[0]
    every_sum = lax.all_to_all(copied, ALL_AXES, split_axis=0, concat_axis=0, tiled=True)
    count = float(devices * rows * width)
    basis, alpha, lower = basis_of(count, every_sum, work, vec, block_rows)
    return (basis.reshape(vectors.shape), alpha, lower)


def solution(mesh):
    return jax.shard_map(
        shards,
        mesh=mesh,
        in_specs=(
            P("ka", None, "mode", "row", None, None),
            P("ka", None, "mode", "row", None, None),
            P(),
            P("mode", "row", None, None),
            P("mode", "row", None, None),
            P("mode", "row", None, None),
            P(),
            P(),
            P(),
            P(),
            P(),
            P(),
            P(),
            P(),
            P(),
        ),
        out_specs=(P("ka", None, "mode", "row", None, None), P(), P()),
        check_vma=False,
    )
```

```python
import functools

import jax
import jax.numpy as jnp
from jax import lax
from jax.experimental import pallas as pl
from jax.experimental.pallas import tpu as pltpu
from jax.sharding import PartitionSpec as P

precise_mode = lax.Precision.HIGHEST
ALL_AXES = ("ka", "mode", "row")
VMEM_BYTES = 32 * 1024 * 1024
SMALL_VMEM_BYTES = 16 * 1024 * 1024
FULL_VMEM_BYTES = 56 * 1024 * 1024
LANES = 128
HOP_WEIGHT = 25_000_000_000
SUBLANES = 8


def precise_dot(left, right):
    return jnp.dot(left, right, precision=precise_mode, preferred_element_type=jnp.float32)


def whole_spec(shape):
    return pl.BlockSpec(shape, lambda *_: (0,) * len(shape))


def pair_exchange(value, axis, first):
    peers = lax.axis_size(axis)
    pairs = []
    for low in range(first, peers - 1, 2):
        pairs += [(low, low + 1), (low + 1, low)]
    return lax.ppermute(value, axis, pairs)


def vector_groups(nvec):
    return [tuple(range(at, min(at + 4, nvec))) for at in range(0, nvec, 4)]


def tiles(rows, width):
    return [
        (slice(r, r + SUBLANES), slice(c, c + LANES))
        for r in range(0, rows, SUBLANES)
        for c in range(0, width, LANES)
    ]


def packed_columns(sums, nvec, offset, lane):
    packed = jnp.zeros((nvec, LANES), jnp.float32)
    for j in range(nvec):
        stacked = jnp.stack([sums(i, j) for i in range(nvec)])
        column = jnp.sum(jnp.sum(stacked, axis=1), axis=1, keepdims=True)
        packed = packed + jnp.where(lane == offset + j, column, 0.0)
    return packed


def add_products(nvec, left_ref, right_ref, sums, number, places, symmetric):
    groups = vector_groups(nvec)
    for ours in groups:
        for other in groups:
            pairs = [(i, j) for i in ours for j in other if i <= j or not symmetric]
            if not pairs:
                continue
            totals = {pair: sums[number, pair[0] * nvec + pair[1]] for pair in pairs}
            for place in places:
                lefts = {i: left_ref[(i, *place)] for i in {p[0] for p in pairs}}
                rights = {j: right_ref[(j, *place)] for j in {p[1] for p in pairs}}
                for i, j in pairs:
                    totals[i, j] = totals[i, j] + lefts[i] * rights[j]
            for i, j in pairs:
                sums[number, i * nvec + j] = totals[i, j]


def resident_kernel(nvec, vec_ref, fn_ref, *refs):
    out_ref, copy_ref, fn_copy_ref, sums = refs[-4:]
    step = pl.program_id(0)

    @pl.when(step == 0)
    def _():
        sums[...] = jnp.zeros_like(sums)

    copy_ref[...] = vec_ref[...]
    fn_copy_ref[...] = fn_ref[...]
    add_products(nvec, vec_ref, vec_ref, sums, 0, tiles(*vec_ref.shape[1:]), True)

    @pl.when(step == pl.num_programs(0) - 1)
    def _():
        lane = lax.broadcasted_iota(jnp.int32, (nvec, LANES), 1)
        out_ref[...] = packed_columns(
            lambda i, j: sums[0, min(i, j) * nvec + max(i, j)], nvec, 2 * nvec, lane
        )


def resident(vec, skip_fn, after, block_rows):
    nvec, rows, width = vec.shape
    block = pl.BlockSpec((nvec, block_rows, width), lambda s: (0, s, 0))
    fn_block = pl.BlockSpec((block_rows, width), lambda s: (s, 0))
    return pl.pallas_call(
        functools.partial(resident_kernel, nvec),
        grid=(rows // block_rows,),
        in_specs=[block, fn_block] + [pl.BlockSpec(memory_space=pl.ANY)] * len(after),
        out_specs=[whole_spec((nvec, LANES)), block, fn_block],
        out_shape=[
            jax.ShapeDtypeStruct((nvec, LANES), jnp.float32),
            jax.ShapeDtypeStruct(vec.shape, jnp.float32),
            jax.ShapeDtypeStruct(skip_fn.shape, jnp.float32),
        ],
        scratch_shapes=[pltpu.VMEM((1, nvec * nvec, SUBLANES, LANES), jnp.float32)],
        compiler_params=pltpu.CompilerParams(vmem_limit_bytes=VMEM_BYTES),
        cost_estimate=pl.CostEstimate(
            flops=nvec * (nvec + 1) * rows * width, bytes_accessed=8 * vec.size, transcendentals=0
        ),
        name="resident",
    )(vec, skip_fn, *after)


def split_kernel(start, vec_ref, out_ref, held, sems):
    count, rows, _ = out_ref.shape
    loads = [
        pltpu.make_async_copy(vec_ref.at[i, pl.ds(start, rows)], held.at[i], sems.at[0, i])
        for i in range(count)
    ]
    stores = [
        pltpu.make_async_copy(held.at[i], out_ref.at[i], sems.at[1, i]) for i in range(count)
    ]
    for load in loads:
        load.start()
    for load, store in zip(loads, stores):
        load.wait()
        store.start()
    for store in stores:
        store.wait()


def split_rows(vec, start, stop):
    nvec, _, width = vec.shape
    shape = (nvec, stop - start, width)
    return pl.pallas_call(
        functools.partial(split_kernel, start),
        in_specs=[pl.BlockSpec(memory_space=pl.ANY)],
        out_specs=pl.BlockSpec(memory_space=pl.ANY),
        out_shape=jax.ShapeDtypeStruct(shape, jnp.float32),
        scratch_shapes=[
            pltpu.VMEM(shape, jnp.float32),
            pltpu.SemaphoreType.DMA((2, nvec)),
        ],
        compiler_params=pltpu.CompilerParams(vmem_limit_bytes=FULL_VMEM_BYTES),
        cost_estimate=pl.CostEstimate(
            flops=0, bytes_accessed=8 * nvec * (stop - start) * width, transcendentals=0
        ),
        name="split_rows",
    )(vec)


def handed_on(array, weight, after=()):
    return pl.pallas_call(
        lambda *_: None,
        in_specs=[pl.BlockSpec(memory_space=pl.ANY)] * (1 + len(after)),
        out_specs=pl.BlockSpec(memory_space=pl.ANY),
        out_shape=jax.ShapeDtypeStruct(array.shape, array.dtype),
        input_output_aliases={0: 0},
        cost_estimate=pl.CostEstimate(flops=weight, bytes_accessed=0, transcendentals=0),
        name="handed_on",
    )(array, *after)


def kron_term(matrix, size, stride, extent, row_offset=0, column_offset=0, sign=1.0):
    points = matrix.shape[0]

    def digits(shape, axis):
        index = lax.broadcasted_iota(jnp.int32, shape, axis)
        return index, lax.rem(lax.div(index, stride), size)

    def picks(offset):
        _, digit = digits((extent, points), 0)
        point = lax.broadcasted_iota(jnp.int32, (extent, points), 1)
        return jnp.where(digit + offset == point, 1.0, 0.0)

    def transposed_dot(one, two):
        return lax.dot_general(
            one, two, (((1,), (1,)), ((), ())), precision=precise_mode,
            preferred_element_type=jnp.float32,
        )

    picked = picks(row_offset)
    picked = 0.5 * (precise_dot(picked, matrix) + sign * transposed_dot(picked, matrix))
    spread = transposed_dot(picked, picks(column_offset))
    row, row_digit = digits((extent, extent), 0)
    column, column_digit = digits((extent, extent), 1)
    same = (row - row_digit * stride) == (column - column_digit * stride)
    return jnp.where(same, spread, 0.0)


def operators_kernel(
    points, group, at_ref, coupling_ref, one_ref, two_ref, three_ref, four_ref, five_ref, six_ref,
    der_ref, *refs,
):
    left_ref, mode_ref, tail_ref, near_ref = refs[-4:]
    points_one, points_two, points_three = points
    rows = points_one * points_two * points_three
    stride = points_two * points_three
    mine = at_ref[1] * points_two
    left_ref[0] = kron_term(two_ref[...], points_two, points_three, rows, mine, mine) + kron_term(
        three_ref[...], points_three, 1, rows
    )
    if group > 1:
        sibling = at_ref[2] * points_two
        left_ref[1] = kron_term(two_ref[...], points_two, points_three, rows, mine, sibling)
    mode_ref[...] = kron_term(one_ref[...], one_ref.shape[0], stride, mode_ref.shape[0])
    width = tail_ref.shape[0]
    fives, sixes = five_ref.shape[0], six_ref.shape[0]
    tail_ref[...] = (
        kron_term(four_ref[...], four_ref.shape[0], fives * sixes, width)
        + kron_term(five_ref[...], fives, sixes, width)
        + kron_term(six_ref[...], sixes, 1, width)
    )
    twist = kron_term(der_ref[...], sixes, 1, near_ref.shape[1], sign=-1.0)
    block = at_ref[0]
    even = lax.rem(block, 2) == 0
    from_above = -coupling_ref[0, block]
    from_below = coupling_ref[0, jnp.maximum(block - 1, 0)]
    near_ref[0] = jnp.where(even, from_above, from_below) * twist
    near_ref[1] = jnp.where(even, from_below, from_above) * twist


def operators(points, group, mode_extent, width, span, at, coupling, matrices, after):
    rows = points[0] * points[1] * points[2]
    shapes = [
        (group, rows, rows), (mode_extent, mode_extent), (width, width), (2, span, span)
    ]
    smem = pl.BlockSpec(memory_space=pltpu.SMEM)
    return pl.pallas_call(
        functools.partial(operators_kernel, points, group),
        in_specs=[smem, smem]
        + [pl.BlockSpec(memory_space=pltpu.VMEM)] * len(matrices)
        + [pl.BlockSpec(memory_space=pl.ANY)] * len(after),
        out_specs=[pl.BlockSpec(memory_space=pltpu.VMEM)] * len(shapes),
        out_shape=[jax.ShapeDtypeStruct(shape, jnp.float32) for shape in shapes],
        compiler_params=pltpu.CompilerParams(vmem_limit_bytes=VMEM_BYTES),
        cost_estimate=pl.CostEstimate(
            flops=500_000_000, bytes_accessed=4_000_000, transcendentals=0
        ),
        name="operators",
    )(at, coupling, *matrices, *after)


def crossing_kernel(points, group, at_ref, two_ref, *refs):
    points_one, points_two, points_three = points
    held_refs, out_refs = refs[:group], refs[group:]
    owners = [at_ref[1], at_ref[2]][:group]
    peers = two_ref.shape[0] // points_two
    stride = points_two * points_three
    for number, out_ref in enumerate(out_refs):
        target = lax.rem(at_ref[1] + group * (number + 1), peers) * points_two
        coefs = {
            (a, k, b): 0.5
            * (
                two_ref[target + a, owners[k] * points_two + b]
                + two_ref[owners[k] * points_two + b, target + a]
            )
            for a in range(points_two)
            for k in range(group)
            for b in range(points_two)
        }
        for start in range(0, points_one * stride, stride):
            for _, lanes in tiles(SUBLANES, out_ref.shape[2]):
                for inner in range(0, points_three, SUBLANES):
                    values = {
                        (k, b): held_refs[k][0, pl.ds(start + b * points_three + inner, SUBLANES), lanes]
                        for k in range(group)
                        for b in range(points_two)
                    }
                    for a in range(points_two):
                        total = None
                        for (k, b), value in values.items():
                            term = coefs[a, k, b] * value
                            total = term if total is None else total + term
                        out_ref[0, pl.ds(start + a * points_three + inner, SUBLANES), lanes] = total


def crossing(points, at, two, held, count):
    nvec, rows, width = held[0].shape
    one = pl.BlockSpec((1, rows, width), lambda i: (i, 0, 0))
    smem = pl.BlockSpec(memory_space=pltpu.SMEM)
    return pl.pallas_call(
        functools.partial(crossing_kernel, points, len(held)),
        grid=(nvec,),
        in_specs=[smem, smem] + [one] * len(held),
        out_specs=[one] * count,
        out_shape=[jax.ShapeDtypeStruct(held[0].shape, jnp.float32)] * count,
        compiler_params=pltpu.CompilerParams(vmem_limit_bytes=VMEM_BYTES),
        cost_estimate=pl.CostEstimate(
            flops=2 * held[0].size * points[1] * len(held) * count,
            bytes_accessed=4 * held[0].size * (len(held) + count),
            transcendentals=0,
        ),
        name="crossing",
    )(at, two, *held)


def local_kernel(nvec, nblocks, group, at_ref, rot_ref, beta_ref, *refs):
    held_refs = refs[:group]
    old_ref, pot_ref, left_ref, tail_ref, out_ref = refs[group:]
    me = pl.program_id(0)
    block = at_ref[0]
    level = (block - nblocks // 2).astype(jnp.float32)
    current = held_refs[0][0]
    total = (pot_ref[...] + rot_ref[block] * level * level) * current
    for j in range(nvec):
        total = total - beta_ref[me, j] * old_ref[j]
    total = total + precise_dot(current, tail_ref[...])
    for number, held_ref in enumerate(held_refs):
        total = total + precise_dot(left_ref[number], held_ref[0])
    out_ref[0] = total


def local_terms(nblocks, at, rot_const, beta, held, old, pot, left, tail):
    nvec, rows, width = old.shape
    one = pl.BlockSpec((1, rows, width), lambda i: (i, 0, 0))
    smem = pl.BlockSpec(memory_space=pltpu.SMEM)
    return pl.pallas_call(
        functools.partial(local_kernel, nvec, nblocks, len(held)),
        grid=(nvec,),
        in_specs=[smem, smem, smem]
        + [one] * len(held)
        + [
            whole_spec(old.shape),
            whole_spec(pot.shape),
            pl.BlockSpec((len(held), rows, rows), lambda i: (0, 0, 0)),
            whole_spec(tail.shape),
        ],
        out_specs=one,
        out_shape=jax.ShapeDtypeStruct(old.shape, jnp.float32),
        compiler_params=pltpu.CompilerParams(vmem_limit_bytes=VMEM_BYTES),
        cost_estimate=pl.CostEstimate(
            flops=12 * old.size * (rows * len(held) + width),
            bytes_accessed=4 * old.size * (2 + len(held)),
            transcendentals=0,
        ),
        name="local_terms",
    )(at, rot_const, beta, *held, old, pot, left, tail)


def mode_kinetic_kernel(peers, in_ref, mat_ref, out_ref):
    rows = in_ref.shape[2]
    field = jnp.concatenate([in_ref[peer, 0] for peer in range(peers)], axis=0)
    field = precise_dot(mat_ref[...], field)
    for peer in range(peers):
        out_ref[peer, 0] = field[peer * rows : (peer + 1) * rows]


def mode_kinetic(field, matrix, peers):
    nvec, rows, width = field.shape
    held = nvec // peers
    block = pl.BlockSpec((peers, 1, rows, width), lambda q: (0, q, 0, 0))
    out = pl.pallas_call(
        functools.partial(mode_kinetic_kernel, peers),
        grid=(held,),
        in_specs=[block, whole_spec(matrix.shape)],
        out_specs=block,
        out_shape=jax.ShapeDtypeStruct((peers, held, rows, width), jnp.float32),
        compiler_params=pltpu.CompilerParams(vmem_limit_bytes=VMEM_BYTES),
        cost_estimate=pl.CostEstimate(
            flops=12 * field.size * matrix.shape[0], bytes_accessed=8 * field.size, transcendentals=0
        ),
        name="mode_kinetic",
    )(field.reshape(peers, held, rows, width), matrix)
    return out.reshape(field.shape)


def join_kernel(starts, sum_count, at_ref, work_ref, cor_ref, near_ref, *refs):
    pieces = len(starts)
    first_refs, second_refs = refs[:pieces], refs[pieces : 2 * pieces]
    sum_refs = refs[2 * pieces : 2 * pieces + sum_count]
    out_ref = refs[-1]
    span = near_ref.shape[1]
    even = lax.rem(at_ref[0], 2) == 0
    for start, first_ref, second_ref in zip(starts, first_refs, second_refs):
        place = slice(start, start + first_ref.shape[1])
        for at in range(0, work_ref.shape[2], span):
            part = slice(at, at + span)
            total = work_ref[0, place, part]
            for sum_ref in sum_refs:
                total = total + sum_ref[0, place, part]
            twist_fn = cor_ref[place, part]
            if_even = jnp.where(even, twist_fn, 1.0)
            if_odd = jnp.where(even, 1.0, twist_fn)
            total = total + if_even * precise_dot(
                if_odd * first_ref[0, :, part], near_ref[0]
            )
            out_ref[0, place, part] = total + if_odd * precise_dot(
                if_even * second_ref[0, :, part], near_ref[1]
            )


def join_terms(at, work, cor, near, starts, first, second, sums):
    nvec, rows, width = work.shape
    one = pl.BlockSpec((1, rows, width), lambda i: (i, 0, 0))
    pieces = [pl.BlockSpec((1, b.shape[1], width), lambda i: (i, 0, 0)) for b in first]
    return pl.pallas_call(
        functools.partial(join_kernel, tuple(starts), len(sums)),
        grid=(nvec,),
        in_specs=[
            pl.BlockSpec(memory_space=pltpu.SMEM), one, whole_spec(cor.shape), whole_spec(near.shape)
        ]
        + pieces
        + pieces
        + [one] * len(sums),
        out_specs=one,
        out_shape=jax.ShapeDtypeStruct(work.shape, jnp.float32),
        compiler_params=pltpu.CompilerParams(vmem_limit_bytes=VMEM_BYTES),
        cost_estimate=pl.CostEstimate(
            flops=24 * work.size * near.shape[1], bytes_accessed=24 * work.size, transcendentals=0
        ),
        name="join_terms",
    )(at, work, cor, near, *first, *second, *sums)


def far_terms_kernel(
    nvec, start, coef_ref, work_ref, first_ref, second_ref, fn_ref, vec_ref, before_ref, out_ref,
    sum_ref, sums,
):
    del work_ref
    step = pl.program_id(0)
    _, block_rows, width = first_ref.shape

    @pl.when(step == 0)
    def _():
        sums[...] = jnp.zeros_like(sums)

    at = pl.multiple_of(start + step * block_rows, SUBLANES)
    places = []
    for rows_here, lanes in tiles(block_rows, width):
        place = (pl.ds(at + rows_here.start, SUBLANES), lanes)
        places.append(place)
        skip_fn = fn_ref[place]
        first_fn = coef_ref[0] * skip_fn
        second_fn = coef_ref[1] * skip_fn
        for i in range(nvec):
            out_ref[(i, *place)] = (
                out_ref[(i, *place)]
                + first_fn * first_ref[i, rows_here, lanes]
                + second_fn * second_ref[i, rows_here, lanes]
            )
    add_products(nvec, vec_ref, out_ref, sums, 0, places, False)
    add_products(nvec, out_ref, out_ref, sums, 1, places, True)

    @pl.when(step == pl.num_programs(0) - 1)
    def _():
        lane = lax.broadcasted_iota(jnp.int32, (nvec, LANES), 1)
        packed = before_ref[...]
        packed = packed + packed_columns(lambda i, j: sums[0, j * nvec + i], nvec, 0, lane)
        packed = packed + packed_columns(
            lambda i, j: sums[1, min(i, j) * nvec + max(i, j)], nvec, nvec, lane
        )
        sum_ref[...] = jnp.broadcast_to(packed[None], sum_ref.shape)


def far_terms(coef, work, first, second, skip_fn, vec, before, start, block_rows, copies):
    nvec, _, width = work.shape
    rows = first.shape[1]
    whole = pl.BlockSpec(memory_space=pltpu.VMEM)
    block = pl.BlockSpec((nvec, block_rows, width), lambda s: (0, s, 0))
    work, skip_fn, vec = (
        pltpu.with_memory_space_constraint(array, pltpu.VMEM) for array in (work, skip_fn, vec)
    )
    return pl.pallas_call(
        functools.partial(far_terms_kernel, nvec, start),
        grid=(rows // block_rows,),
        in_specs=[
            pl.BlockSpec(memory_space=pltpu.SMEM), whole, block, block, whole, whole, whole
        ],
        out_specs=[whole, whole],
        out_shape=[
            jax.ShapeDtypeStruct(work.shape, jnp.float32),
            jax.ShapeDtypeStruct((copies, nvec, LANES), jnp.float32),
        ],
        scratch_shapes=[pltpu.VMEM((2, nvec * nvec, SUBLANES, LANES), jnp.float32)],
        input_output_aliases={1: 0},
        compiler_params=pltpu.CompilerParams(vmem_limit_bytes=SMALL_VMEM_BYTES),
        cost_estimate=pl.CostEstimate(
            flops=3 * nvec * nvec * rows * width,
            bytes_accessed=20 * first.size,
            transcendentals=0,
        ),
        name="far_terms",
    )(coef, work, first, second, skip_fn, vec, before)


def across(column, row):
    return jnp.broadcast_to(column[row : row + 1, :], (SUBLANES, LANES))


def spread_columns(matrix, start, count):
    return [
        jnp.broadcast_to(matrix[:, k : k + 1], (count, LANES)) for k in range(start, start + count)
    ]


def spread_dot(left, right):
    count = len(left)
    columns = []
    for column in right:
        terms = [left[m] * jnp.broadcast_to(column[m : m + 1, :], left[m].shape) for m in range(count)]
        while len(terms) > 1:
            terms = [sum(terms[k + 1 : k + 2], terms[k]) for k in range(0, len(terms), 2)]
        columns.append(terms[0])
    return columns


def small_algebra(nvec, count, packed):
    packed = packed * (1.0 / count)
    cross = spread_columns(packed.T[0:nvec, :], 0, nvec)
    cross_turned = spread_columns(packed, 0, nvec)
    gram = spread_columns(packed, nvec, nvec)
    vec_gram = spread_columns(packed, 2 * nvec, nvec)
    total = [2.0 * c - d for c, d in zip(cross, spread_dot(vec_gram, cross))]
    total_turned = [2.0 * c - d for c, d in zip(cross_turned, spread_dot(cross_turned, vec_gram))]
    inner = [d - c for c, d in zip(cross, spread_dot(vec_gram, total))]
    gram = [
        g - one + other
        for g, one, other in zip(
            gram, spread_dot(cross_turned, total), spread_dot(total_turned, inner)
        )
    ]
    row = lax.broadcasted_iota(jnp.int32, (nvec, LANES), 0)
    inverse = [jnp.where(row == k, 1.0, 0.0) for k in range(nvec)]
    lower = []
    for at in range(nvec):
        pivot = jnp.broadcast_to(gram[at][at : at + 1, :], (nvec, LANES))
        scale = lax.rsqrt(pivot)
        scale = scale * (1.5 - 0.5 * pivot * scale * scale)
        scaled = gram[at] * scale
        lower.append(jnp.where(row >= at, scaled, 0.0))
        factor = jnp.where(row > at, scaled, 0.0)
        for k in range(at + 1, nvec):
            here = jnp.broadcast_to(gram[k][at : at + 1, :], (nvec, LANES)) * scale
            gram[k] = gram[k] - factor * here
        for k in range(at + 1):
            here = jnp.broadcast_to(inverse[k][at : at + 1, :], (nvec, LANES)) * scale
            inverse[k] = jnp.where(row == at, here, inverse[k] - factor * here)
    mixing = [-column for column in spread_dot(inverse, total_turned)]
    return total, lower, inverse, mixing


def gathered_columns(columns):
    lane = lax.broadcasted_iota(jnp.int32, columns[0].shape, 1)
    matrix = jnp.zeros_like(columns[0])
    for k, column in enumerate(columns):
        matrix = jnp.where(lane == k, column, matrix)
    return matrix[:, : len(columns)]


def basis_kernel(nvec, count, sum_ref, work_ref, vec_ref, out_ref, alpha_ref, lower_ref, coefs):
    @pl.when(pl.program_id(0) == 0)
    def _():
        packed = sum_ref[0]
        for other in range(1, sum_ref.shape[0]):
            packed = packed + sum_ref[other]
        total, lower, inverse, mixing = small_algebra(nvec, count, packed)
        for number, columns in enumerate((inverse, mixing)):
            for j in range(nvec):
                for i in range(nvec):
                    if number == 1 or j <= i:
                        coefs[number, i * nvec + j] = across(columns[j], i)
        alpha_ref[...] = gathered_columns(total)
        lower_ref[...] = gathered_columns(lower)

    start = pl.multiple_of(pl.program_id(0) * out_ref.shape[1], out_ref.shape[1])
    places = tiles(*out_ref.shape[1:])
    for at in range(0, len(places), 4):
        group = places[at : at + 4]
        held = [(pl.ds(start + place.start, SUBLANES), lanes) for place, lanes in group]
        totals = {}
        for number, ref in ((1, vec_ref), (0, work_ref)):
            for j in range(nvec):
                values = [ref[(j, *place)] for place in held]
                for i in range(nvec):
                    if number == 0 and j > i:
                        continue
                    coef = coefs[number, i * nvec + j]
                    for spot, value in enumerate(values):
                        term = coef * value
                        here = (i, spot)
                        totals[here] = totals[here] + term if here in totals else term
        for (i, spot), value in totals.items():
            out_ref[(i, *group[spot])] = value


def basis_of(count, sums, work, vec, block_rows):
    nvec, rows, width = work.shape
    block = pl.BlockSpec((nvec, block_rows, width), lambda s: (0, s, 0))
    small = jax.ShapeDtypeStruct((nvec, nvec), jnp.float32)
    whole = pl.BlockSpec(memory_space=pltpu.VMEM)
    work, vec = (pltpu.with_memory_space_constraint(array, pltpu.VMEM) for array in (work, vec))
    return pl.pallas_call(
        functools.partial(basis_kernel, nvec, count),
        grid=(rows // block_rows,),
        in_specs=[whole, whole, whole],
        out_specs=[block, whole_spec(small.shape), whole_spec(small.shape)],
        out_shape=[jax.ShapeDtypeStruct(work.shape, jnp.float32), small, small],
        scratch_shapes=[pltpu.VMEM((2, nvec * nvec, SUBLANES, LANES), jnp.float32)],
        compiler_params=pltpu.CompilerParams(vmem_limit_bytes=SMALL_VMEM_BYTES),
        cost_estimate=pl.CostEstimate(
            flops=4 * nvec * work.size, bytes_accessed=12 * work.size, transcendentals=0
        ),
        name="basis",
    )(sums, work, vec)


def shards(
    vectors,
    previous,
    beta,
    potential,
    coriolis_fn,
    second_fn,
    rot_const,
    coupling,
    kin_one,
    kin_two,
    kin_three,
    kin_four,
    kin_five,
    kin_six,
    coriolis_derivative,
):
    _, nvec, *points, width = vectors.shape
    rows = points[0] * points[1] * points[2]
    devices = lax.axis_size(ALL_AXES)
    block_index = lax.axis_index("ka")
    nblocks = lax.axis_size("ka")
    row_peers = lax.axis_size("row")
    mode_peers = lax.axis_size("mode")
    row_at = lax.axis_index("row")
    current = vectors.reshape(nvec, rows, width)
    older = previous.reshape(nvec, rows, width)
    block_rows = min(32, rows // 2)

    cut = rows * 3 // 4 // block_rows * block_rows or rows // 2
    starts, stops = [0, cut], [cut, rows]
    parts = [split_rows(current, start, stop) for start, stop in zip(starts, stops)]
    near_first = [pair_exchange(part, "ka", 0) for part in parts]
    near_second = [pair_exchange(part, "ka", 1) for part in parts]
    at = jnp.stack([block_index, row_at, row_at ^ 1]).astype(jnp.int32)
    group = 2 - row_peers % 2
    held = [current]
    if group == 2:
        held.append(lax.ppermute(current, "row", [(i, i ^ 1) for i in range(row_peers)]))
    away = row_peers // group - 1
    row_parts = crossing(tuple(points), at, kin_two, held, away) if away else []
    row_sums = [
        lax.ppermute(
            part, "row", [(i, (i + group * (number + 1)) % row_peers) for i in range(row_peers)]
        )
        for number, part in enumerate(row_parts)
    ]

    span = next((s for s in (256, 128) if width % s == 0 and s % kin_six.shape[0] == 0), width)
    left, mode_mat, tail, near = operators(
        tuple(points),
        group,
        mode_peers * rows,
        width,
        span,
        at,
        coupling,
        (kin_one, kin_two, kin_three, kin_four, kin_five, kin_six, coriolis_derivative),
        row_parts,
    )
    near_first[0] = handed_on(near_first[0], HOP_WEIGHT, [*row_parts, mode_mat])
    near_second[0] = handed_on(near_second[0], HOP_WEIGHT, [*row_parts, mode_mat])
    far_first = [pair_exchange(part, "ka", 0) for part in near_second]
    far_second = [pair_exchange(part, "ka", 1) for part in near_first]
    lower_two = jnp.maximum(block_index - 2, 0)
    far_above, far_below = coupling[1, block_index], coupling[1, lower_two]
    even = block_index % 2 == 0
    far_pair = jnp.stack(
        [jnp.where(even, far_above, far_below), jnp.where(even, far_below, far_above)]
    )
    sums, vec, skip_fn = resident(
        current, second_fn.reshape(rows, width), held[1:], block_rows
    )
    mode_shares = lax.all_to_all(vec, "mode", split_axis=0, concat_axis=0, tiled=True)
    mode_shares = mode_kinetic(mode_shares, mode_mat, mode_peers)
    mode_sum = lax.all_to_all(mode_shares, "mode", split_axis=0, concat_axis=0, tiled=True)
    work = local_terms(
        nblocks, at, rot_const, beta, held, older, potential.reshape(rows, width), left, tail
    )
    work = join_terms(
        at,
        work,
        coriolis_fn.reshape(rows, width),
        near,
        starts,
        near_first,
        near_second,
        [mode_sum, *row_sums],
    )
    for number, start in enumerate(starts):
        work, copied = far_terms(
            far_pair,
            work,
            far_first[number],
            far_second[number],
            skip_fn,
            vec,
            sums,
            start,
            block_rows if number < len(starts) - 1 else max(block_rows // 2, SUBLANES),
            devices if number == len(starts) - 1 else 1,
        )
        sums = copied[0]
    every_sum = lax.all_to_all(copied, ALL_AXES, split_axis=0, concat_axis=0, tiled=True)
    count = float(devices * rows * width)
    basis, alpha, lower = basis_of(count, every_sum, work, vec, block_rows)
    return (basis.reshape(vectors.shape), alpha, lower)


def solution(mesh):
    return jax.shard_map(
        shards,
        mesh=mesh,
        in_specs=(
            P("ka", None, "mode", "row", None, None),
            P("ka", None, "mode", "row", None, None),
            P(),
            P("mode", "row", None, None),
            P("mode", "row", None, None),
            P("mode", "row", None, None),
            P(),
            P(),
            P(),
            P(),
            P(),
            P(),
            P(),
            P(),
            P(),
        ),
        out_specs=(P("ka", None, "mode", "row", None, None), P(), P()),
        check_vma=False,
    )
```

```python
import functools

import jax
import jax.numpy as jnp
from jax import lax
from jax.experimental import pallas as pl
from jax.experimental.pallas import tpu as pltpu
from jax.sharding import PartitionSpec as P

precise_mode = lax.Precision.HIGHEST
ALL_AXES = ("ka", "mode", "row")
VMEM_BYTES = 32 * 1024 * 1024
SMALL_VMEM_BYTES = 16 * 1024 * 1024
FULL_VMEM_BYTES = 56 * 1024 * 1024
LANES = 128
HOP_WEIGHT = 25_000_000_000
SUBLANES = 8


def precise_dot(left, right):
    return jnp.dot(left, right, precision=precise_mode, preferred_element_type=jnp.float32)


def whole_spec(shape):
    return pl.BlockSpec(shape, lambda *_: (0,) * len(shape))


def pair_exchange(value, axis, first):
    peers = lax.axis_size(axis)
    pairs = []
    for low in range(first, peers - 1, 2):
        pairs += [(low, low + 1), (low + 1, low)]
    return lax.ppermute(value, axis, pairs)


def vector_groups(nvec):
    return [tuple(range(at, min(at + 4, nvec))) for at in range(0, nvec, 4)]


def tiles(rows, width):
    return [
        (slice(r, r + SUBLANES), slice(c, c + LANES))
        for r in range(0, rows, SUBLANES)
        for c in range(0, width, LANES)
    ]


def packed_columns(sums, nvec, offset, lane):
    packed = jnp.zeros((nvec, LANES), jnp.float32)
    for j in range(nvec):
        stacked = jnp.stack([sums(i, j) for i in range(nvec)])
        column = jnp.sum(jnp.sum(stacked, axis=1), axis=1, keepdims=True)
        packed = packed + jnp.where(lane == offset + j, column, 0.0)
    return packed


def add_products(nvec, left_ref, right_ref, sums, number, places, symmetric):
    groups = vector_groups(nvec)
    for ours in groups:
        for other in groups:
            pairs = [(i, j) for i in ours for j in other if i <= j or not symmetric]
            if not pairs:
                continue
            totals = {pair: sums[number, pair[0] * nvec + pair[1]] for pair in pairs}
            for place in places:
                lefts = {i: left_ref[(i, *place)] for i in {p[0] for p in pairs}}
                rights = {j: right_ref[(j, *place)] for j in {p[1] for p in pairs}}
                for i, j in pairs:
                    totals[i, j] = totals[i, j] + lefts[i] * rights[j]
            for i, j in pairs:
                sums[number, i * nvec + j] = totals[i, j]


def resident_kernel(nvec, vec_ref, fn_ref, *refs):
    out_ref, copy_ref, fn_copy_ref, sums = refs[-4:]
    step = pl.program_id(0)

    @pl.when(step == 0)
    def _():
        sums[...] = jnp.zeros_like(sums)

    copy_ref[...] = vec_ref[...]
    fn_copy_ref[...] = fn_ref[...]
    add_products(nvec, vec_ref, vec_ref, sums, 0, tiles(*vec_ref.shape[1:]), True)

    @pl.when(step == pl.num_programs(0) - 1)
    def _():
        lane = lax.broadcasted_iota(jnp.int32, (nvec, LANES), 1)
        out_ref[...] = packed_columns(
            lambda i, j: sums[0, min(i, j) * nvec + max(i, j)], nvec, 2 * nvec, lane
        )


def resident(vec, skip_fn, after, block_rows):
    nvec, rows, width = vec.shape
    block = pl.BlockSpec((nvec, block_rows, width), lambda s: (0, s, 0))
    fn_block = pl.BlockSpec((block_rows, width), lambda s: (s, 0))
    return pl.pallas_call(
        functools.partial(resident_kernel, nvec),
        grid=(rows // block_rows,),
        in_specs=[block, fn_block] + [pl.BlockSpec(memory_space=pl.ANY)] * len(after),
        out_specs=[whole_spec((nvec, LANES)), block, fn_block],
        out_shape=[
            jax.ShapeDtypeStruct((nvec, LANES), jnp.float32),
            jax.ShapeDtypeStruct(vec.shape, jnp.float32),
            jax.ShapeDtypeStruct(skip_fn.shape, jnp.float32),
        ],
        scratch_shapes=[pltpu.VMEM((1, nvec * nvec, SUBLANES, LANES), jnp.float32)],
        compiler_params=pltpu.CompilerParams(vmem_limit_bytes=VMEM_BYTES),
        cost_estimate=pl.CostEstimate(
            flops=nvec * (nvec + 1) * rows * width, bytes_accessed=8 * vec.size, transcendentals=0
        ),
        name="resident",
    )(vec, skip_fn, *after)


def split_kernel(start, vec_ref, out_ref, held, sems):
    count, rows, _ = out_ref.shape
    loads = [
        pltpu.make_async_copy(vec_ref.at[i, pl.ds(start, rows)], held.at[i], sems.at[0, i])
        for i in range(count)
    ]
    stores = [
        pltpu.make_async_copy(held.at[i], out_ref.at[i], sems.at[1, i]) for i in range(count)
    ]
    for load in loads:
        load.start()
    for load, store in zip(loads, stores):
        load.wait()
        store.start()
    for store in stores:
        store.wait()


def split_rows(vec, start, stop):
    nvec, _, width = vec.shape
    shape = (nvec, stop - start, width)
    return pl.pallas_call(
        functools.partial(split_kernel, start),
        in_specs=[pl.BlockSpec(memory_space=pl.ANY)],
        out_specs=pl.BlockSpec(memory_space=pl.ANY),
        out_shape=jax.ShapeDtypeStruct(shape, jnp.float32),
        scratch_shapes=[
            pltpu.VMEM(shape, jnp.float32),
            pltpu.SemaphoreType.DMA((2, nvec)),
        ],
        compiler_params=pltpu.CompilerParams(vmem_limit_bytes=FULL_VMEM_BYTES),
        cost_estimate=pl.CostEstimate(
            flops=0, bytes_accessed=8 * nvec * (stop - start) * width, transcendentals=0
        ),
        name="split_rows",
    )(vec)


def handed_on(array, weight, after=()):
    return pl.pallas_call(
        lambda *_: None,
        in_specs=[pl.BlockSpec(memory_space=pl.ANY)] * (1 + len(after)),
        out_specs=pl.BlockSpec(memory_space=pl.ANY),
        out_shape=jax.ShapeDtypeStruct(array.shape, array.dtype),
        input_output_aliases={0: 0},
        cost_estimate=pl.CostEstimate(flops=weight, bytes_accessed=0, transcendentals=0),
        name="handed_on",
    )(array, *after)


def kron_term(matrix, size, stride, extent, row_offset=0, column_offset=0, sign=1.0):
    points = matrix.shape[0]

    def digits(shape, axis):
        index = lax.broadcasted_iota(jnp.int32, shape, axis)
        return index, lax.rem(lax.div(index, stride), size)

    def picks(offset):
        _, digit = digits((extent, points), 0)
        point = lax.broadcasted_iota(jnp.int32, (extent, points), 1)
        return jnp.where(digit + offset == point, 1.0, 0.0)

    def transposed_dot(one, two):
        return lax.dot_general(
            one, two, (((1,), (1,)), ((), ())), precision=precise_mode,
            preferred_element_type=jnp.float32,
        )

    picked = picks(row_offset)
    picked = 0.5 * (precise_dot(picked, matrix) + sign * transposed_dot(picked, matrix))
    spread = transposed_dot(picked, picks(column_offset))
    row, row_digit = digits((extent, extent), 0)
    column, column_digit = digits((extent, extent), 1)
    same = (row - row_digit * stride) == (column - column_digit * stride)
    return jnp.where(same, spread, 0.0)


def operators_kernel(
    points, group, at_ref, coupling_ref, one_ref, two_ref, three_ref, four_ref, five_ref, six_ref,
    der_ref, *refs,
):
    left_ref, mode_ref, tail_ref, near_ref = refs[-4:]
    points_one, points_two, points_three = points
    rows = points_one * points_two * points_three
    stride = points_two * points_three
    mine = at_ref[1] * points_two
    left_ref[0] = kron_term(two_ref[...], points_two, points_three, rows, mine, mine) + kron_term(
        three_ref[...], points_three, 1, rows
    )
    if group > 1:
        sibling = at_ref[2] * points_two
        left_ref[1] = kron_term(two_ref[...], points_two, points_three, rows, mine, sibling)
    mode_ref[...] = kron_term(one_ref[...], one_ref.shape[0], stride, mode_ref.shape[0])
    width = tail_ref.shape[0]
    fives, sixes = five_ref.shape[0], six_ref.shape[0]
    tail_ref[...] = (
        kron_term(four_ref[...], four_ref.shape[0], fives * sixes, width)
        + kron_term(five_ref[...], fives, sixes, width)
        + kron_term(six_ref[...], sixes, 1, width)
    )
    twist = kron_term(der_ref[...], sixes, 1, near_ref.shape[1], sign=-1.0)
    block = at_ref[0]
    even = lax.rem(block, 2) == 0
    from_above = -coupling_ref[0, block]
    from_below = coupling_ref[0, jnp.maximum(block - 1, 0)]
    near_ref[0] = jnp.where(even, from_above, from_below) * twist
    near_ref[1] = jnp.where(even, from_below, from_above) * twist


def operators(points, group, mode_extent, width, span, at, coupling, matrices, after):
    rows = points[0] * points[1] * points[2]
    shapes = [
        (group, rows, rows), (mode_extent, mode_extent), (width, width), (2, span, span)
    ]
    smem = pl.BlockSpec(memory_space=pltpu.SMEM)
    return pl.pallas_call(
        functools.partial(operators_kernel, points, group),
        in_specs=[smem, smem]
        + [pl.BlockSpec(memory_space=pltpu.VMEM)] * len(matrices)
        + [pl.BlockSpec(memory_space=pl.ANY)] * len(after),
        out_specs=[pl.BlockSpec(memory_space=pltpu.VMEM)] * len(shapes),
        out_shape=[jax.ShapeDtypeStruct(shape, jnp.float32) for shape in shapes],
        compiler_params=pltpu.CompilerParams(vmem_limit_bytes=VMEM_BYTES),
        cost_estimate=pl.CostEstimate(
            flops=500_000_000, bytes_accessed=4_000_000, transcendentals=0
        ),
        name="operators",
    )(at, coupling, *matrices, *after)


def crossing_kernel(points, group, at_ref, two_ref, *refs):
    points_one, points_two, points_three = points
    held_refs, out_refs = refs[:group], refs[group:]
    owners = [at_ref[1], at_ref[2]][:group]
    peers = two_ref.shape[0] // points_two
    stride = points_two * points_three
    for number, out_ref in enumerate(out_refs):
        target = lax.rem(at_ref[1] + group * (number + 1), peers) * points_two
        coefs = {
            (a, k, b): 0.5
            * (
                two_ref[target + a, owners[k] * points_two + b]
                + two_ref[owners[k] * points_two + b, target + a]
            )
            for a in range(points_two)
            for k in range(group)
            for b in range(points_two)
        }
        for start in range(0, points_one * stride, stride):
            for _, lanes in tiles(SUBLANES, out_ref.shape[2]):
                for inner in range(0, points_three, SUBLANES):
                    values = {
                        (k, b): held_refs[k][0, pl.ds(start + b * points_three + inner, SUBLANES), lanes]
                        for k in range(group)
                        for b in range(points_two)
                    }
                    for a in range(points_two):
                        total = None
                        for (k, b), value in values.items():
                            term = coefs[a, k, b] * value
                            total = term if total is None else total + term
                        out_ref[0, pl.ds(start + a * points_three + inner, SUBLANES), lanes] = total


def crossing(points, at, two, held, count):
    nvec, rows, width = held[0].shape
    one = pl.BlockSpec((1, rows, width), lambda i: (i, 0, 0))
    smem = pl.BlockSpec(memory_space=pltpu.SMEM)
    return pl.pallas_call(
        functools.partial(crossing_kernel, points, len(held)),
        grid=(nvec,),
        in_specs=[smem, smem] + [one] * len(held),
        out_specs=[one] * count,
        out_shape=[jax.ShapeDtypeStruct(held[0].shape, jnp.float32)] * count,
        compiler_params=pltpu.CompilerParams(vmem_limit_bytes=VMEM_BYTES),
        cost_estimate=pl.CostEstimate(
            flops=2 * held[0].size * points[1] * len(held) * count,
            bytes_accessed=4 * held[0].size * (len(held) + count),
            transcendentals=0,
        ),
        name="crossing",
    )(at, two, *held)


def local_kernel(nvec, nblocks, group, at_ref, rot_ref, beta_ref, *refs):
    held_refs = refs[:group]
    old_ref, pot_ref, left_ref, tail_ref, out_ref = refs[group:]
    me = pl.program_id(0)
    block = at_ref[0]
    level = (block - nblocks // 2).astype(jnp.float32)
    current = held_refs[0][0]
    total = (pot_ref[...] + rot_ref[block] * level * level) * current
    for j in range(nvec):
        total = total - beta_ref[me, j] * old_ref[j]
    total = total + precise_dot(current, tail_ref[...])
    for number, held_ref in enumerate(held_refs):
        total = total + precise_dot(left_ref[number], held_ref[0])
    out_ref[0] = total


def local_terms(nblocks, at, rot_const, beta, held, old, pot, left, tail):
    nvec, rows, width = old.shape
    one = pl.BlockSpec((1, rows, width), lambda i: (i, 0, 0))
    smem = pl.BlockSpec(memory_space=pltpu.SMEM)
    return pl.pallas_call(
        functools.partial(local_kernel, nvec, nblocks, len(held)),
        grid=(nvec,),
        in_specs=[smem, smem, smem]
        + [one] * len(held)
        + [
            whole_spec(old.shape),
            whole_spec(pot.shape),
            pl.BlockSpec((len(held), rows, rows), lambda i: (0, 0, 0)),
            whole_spec(tail.shape),
        ],
        out_specs=one,
        out_shape=jax.ShapeDtypeStruct(old.shape, jnp.float32),
        compiler_params=pltpu.CompilerParams(vmem_limit_bytes=VMEM_BYTES),
        cost_estimate=pl.CostEstimate(
            flops=12 * old.size * (rows * len(held) + width),
            bytes_accessed=4 * old.size * (2 + len(held)),
            transcendentals=0,
        ),
        name="local_terms",
    )(at, rot_const, beta, *held, old, pot, left, tail)


def mode_kinetic_kernel(peers, in_ref, mat_ref, out_ref):
    rows = in_ref.shape[2]
    field = jnp.concatenate([in_ref[peer, 0] for peer in range(peers)], axis=0)
    field = precise_dot(mat_ref[...], field)
    for peer in range(peers):
        out_ref[peer, 0] = field[peer * rows : (peer + 1) * rows]


def mode_kinetic(field, matrix, peers):
    nvec, rows, width = field.shape
    held = nvec // peers
    block = pl.BlockSpec((peers, 1, rows, width), lambda q: (0, q, 0, 0))
    out = pl.pallas_call(
        functools.partial(mode_kinetic_kernel, peers),
        grid=(held,),
        in_specs=[block, whole_spec(matrix.shape)],
        out_specs=block,
        out_shape=jax.ShapeDtypeStruct((peers, held, rows, width), jnp.float32),
        compiler_params=pltpu.CompilerParams(vmem_limit_bytes=VMEM_BYTES),
        cost_estimate=pl.CostEstimate(
            flops=12 * field.size * matrix.shape[0], bytes_accessed=8 * field.size, transcendentals=0
        ),
        name="mode_kinetic",
    )(field.reshape(peers, held, rows, width), matrix)
    return out.reshape(field.shape)


def join_kernel(starts, sum_count, at_ref, work_ref, cor_ref, near_ref, *refs):
    pieces = len(starts)
    first_refs, second_refs = refs[:pieces], refs[pieces : 2 * pieces]
    sum_refs = refs[2 * pieces : 2 * pieces + sum_count]
    out_ref = refs[-1]
    span = near_ref.shape[1]
    even = lax.rem(at_ref[0], 2) == 0
    for start, first_ref, second_ref in zip(starts, first_refs, second_refs):
        place = slice(start, start + first_ref.shape[1])
        for at in range(0, work_ref.shape[2], span):
            part = slice(at, at + span)
            total = work_ref[0, place, part]
            for sum_ref in sum_refs:
                total = total + sum_ref[0, place, part]
            twist_fn = cor_ref[place, part]
            if_even = jnp.where(even, twist_fn, 1.0)
            if_odd = jnp.where(even, 1.0, twist_fn)
            total = total + if_even * precise_dot(
                if_odd * first_ref[0, :, part], near_ref[0]
            )
            out_ref[0, place, part] = total + if_odd * precise_dot(
                if_even * second_ref[0, :, part], near_ref[1]
            )


def join_terms(at, work, cor, near, starts, first, second, sums):
    nvec, rows, width = work.shape
    one = pl.BlockSpec((1, rows, width), lambda i: (i, 0, 0))
    pieces = [pl.BlockSpec((1, b.shape[1], width), lambda i: (i, 0, 0)) for b in first]
    return pl.pallas_call(
        functools.partial(join_kernel, tuple(starts), len(sums)),
        grid=(nvec,),
        in_specs=[
            pl.BlockSpec(memory_space=pltpu.SMEM), one, whole_spec(cor.shape), whole_spec(near.shape)
        ]
        + pieces
        + pieces
        + [one] * len(sums),
        out_specs=one,
        out_shape=jax.ShapeDtypeStruct(work.shape, jnp.float32),
        compiler_params=pltpu.CompilerParams(vmem_limit_bytes=VMEM_BYTES),
        cost_estimate=pl.CostEstimate(
            flops=24 * work.size * near.shape[1], bytes_accessed=24 * work.size, transcendentals=0
        ),
        name="join_terms",
    )(at, work, cor, near, *first, *second, *sums)


def far_terms_kernel(
    nvec, start, coef_ref, work_ref, first_ref, second_ref, fn_ref, vec_ref, before_ref, out_ref,
    sum_ref, sums,
):
    del work_ref
    step = pl.program_id(0)
    _, block_rows, width = first_ref.shape

    @pl.when(step == 0)
    def _():
        sums[...] = jnp.zeros_like(sums)

    at = pl.multiple_of(start + step * block_rows, SUBLANES)
    places = []
    for rows_here, lanes in tiles(block_rows, width):
        place = (pl.ds(at + rows_here.start, SUBLANES), lanes)
        places.append(place)
        skip_fn = fn_ref[place]
        first_fn = coef_ref[0] * skip_fn
        second_fn = coef_ref[1] * skip_fn
        for i in range(nvec):
            out_ref[(i, *place)] = (
                out_ref[(i, *place)]
                + first_fn * first_ref[i, rows_here, lanes]
                + second_fn * second_ref[i, rows_here, lanes]
            )
    add_products(nvec, vec_ref, out_ref, sums, 0, places, False)
    add_products(nvec, out_ref, out_ref, sums, 1, places, True)

    @pl.when(step == pl.num_programs(0) - 1)
    def _():
        lane = lax.broadcasted_iota(jnp.int32, (nvec, LANES), 1)
        packed = before_ref[...]
        packed = packed + packed_columns(lambda i, j: sums[0, j * nvec + i], nvec, 0, lane)
        packed = packed + packed_columns(
            lambda i, j: sums[1, min(i, j) * nvec + max(i, j)], nvec, nvec, lane
        )
        sum_ref[...] = jnp.broadcast_to(packed[None], sum_ref.shape)


def far_terms(coef, work, first, second, skip_fn, vec, before, start, block_rows, copies):
    nvec, _, width = work.shape
    rows = first.shape[1]
    whole = pl.BlockSpec(memory_space=pltpu.VMEM)
    block = pl.BlockSpec((nvec, block_rows, width), lambda s: (0, s, 0))
    work, skip_fn, vec = (
        pltpu.with_memory_space_constraint(array, pltpu.VMEM) for array in (work, skip_fn, vec)
    )
    return pl.pallas_call(
        functools.partial(far_terms_kernel, nvec, start),
        grid=(rows // block_rows,),
        in_specs=[
            pl.BlockSpec(memory_space=pltpu.SMEM), whole, block, block, whole, whole, whole
        ],
        out_specs=[whole, whole],
        out_shape=[
            jax.ShapeDtypeStruct(work.shape, jnp.float32),
            jax.ShapeDtypeStruct((copies, nvec, LANES), jnp.float32),
        ],
        scratch_shapes=[pltpu.VMEM((2, nvec * nvec, SUBLANES, LANES), jnp.float32)],
        input_output_aliases={1: 0},
        compiler_params=pltpu.CompilerParams(vmem_limit_bytes=SMALL_VMEM_BYTES),
        cost_estimate=pl.CostEstimate(
            flops=3 * nvec * nvec * rows * width,
            bytes_accessed=20 * first.size,
            transcendentals=0,
        ),
        name="far_terms",
    )(coef, work, first, second, skip_fn, vec, before)


def across(column, row):
    return jnp.broadcast_to(column[row : row + 1, :], (SUBLANES, LANES))


def spread_columns(matrix, start, count):
    return [
        jnp.broadcast_to(matrix[:, k : k + 1], (count, LANES)) for k in range(start, start + count)
    ]


def spread_dot(left, right):
    count = len(left)
    columns = []
    for column in right:
        terms = [left[m] * jnp.broadcast_to(column[m : m + 1, :], left[m].shape) for m in range(count)]
        while len(terms) > 1:
            terms = [sum(terms[k + 1 : k + 2], terms[k]) for k in range(0, len(terms), 2)]
        columns.append(terms[0])
    return columns


def small_algebra(nvec, count, packed):
    packed = packed * (1.0 / count)
    cross = spread_columns(packed.T[0:nvec, :], 0, nvec)
    cross_turned = spread_columns(packed, 0, nvec)
    gram = spread_columns(packed, nvec, nvec)
    vec_gram = spread_columns(packed, 2 * nvec, nvec)
    total = [2.0 * c - d for c, d in zip(cross, spread_dot(vec_gram, cross))]
    total_turned = [2.0 * c - d for c, d in zip(cross_turned, spread_dot(cross_turned, vec_gram))]
    inner = [d - c for c, d in zip(cross, spread_dot(vec_gram, total))]
    gram = [
        g - one + other
        for g, one, other in zip(
            gram, spread_dot(cross_turned, total), spread_dot(total_turned, inner)
        )
    ]
    row = lax.broadcasted_iota(jnp.int32, (nvec, LANES), 0)
    inverse = [jnp.where(row == k, 1.0, 0.0) for k in range(nvec)]
    lower = []
    for at in range(nvec):
        pivot = jnp.broadcast_to(gram[at][at : at + 1, :], (nvec, LANES))
        scale = lax.rsqrt(pivot)
        scale = scale * (1.5 - 0.5 * pivot * scale * scale)
        scaled = gram[at] * scale
        lower.append(jnp.where(row >= at, scaled, 0.0))
        factor = jnp.where(row > at, scaled, 0.0)
        for k in range(at + 1, nvec):
            here = jnp.broadcast_to(gram[k][at : at + 1, :], (nvec, LANES)) * scale
            gram[k] = gram[k] - factor * here
        for k in range(at + 1):
            here = jnp.broadcast_to(inverse[k][at : at + 1, :], (nvec, LANES)) * scale
            inverse[k] = jnp.where(row == at, here, inverse[k] - factor * here)
    mixing = [-column for column in spread_dot(inverse, total_turned)]
    return total, lower, inverse, mixing


def gathered_columns(columns):
    lane = lax.broadcasted_iota(jnp.int32, columns[0].shape, 1)
    matrix = jnp.zeros_like(columns[0])
    for k, column in enumerate(columns):
        matrix = jnp.where(lane == k, column, matrix)
    return matrix[:, : len(columns)]


def basis_kernel(
    nvec, count, block_rows, sum_ref, work_ref, vec_ref, out_ref, alpha_ref, lower_ref, coefs, held, sems
):
    packed = sum_ref[0]
    for other in range(1, sum_ref.shape[0]):
        packed = packed + sum_ref[other]
    total, lower, inverse, mixing = small_algebra(nvec, count, packed)
    for number, columns in enumerate((inverse, mixing)):
        for j in range(nvec):
            for i in range(nvec):
                if number == 1 or j <= i:
                    coefs[number, i * nvec + j] = across(columns[j], i)
    alpha_ref[...] = gathered_columns(total)
    lower_ref[...] = gathered_columns(lower)
    rows, width = held.shape[1:]
    blocks = rows // block_rows

    def copy_out(step):
        place = pl.ds(pl.multiple_of(step * block_rows, block_rows), block_rows)
        return pltpu.make_async_copy(held.at[:, place], out_ref.at[:, place], sems.at[step])

    def some_rows(step, _):
        start = pl.multiple_of(step * block_rows, block_rows)
        places = [
            (pl.ds(start + place.start, SUBLANES), lanes)
            for place, lanes in tiles(block_rows, width)
        ]
        for at in range(0, len(places), 4):
            group = places[at : at + 4]
            totals = {}
            for number, ref in ((1, vec_ref), (0, work_ref)):
                for j in range(nvec):
                    values = [ref[(j, *place)] for place in group]
                    for i in range(nvec):
                        if number == 0 and j > i:
                            continue
                        coef = coefs[number, i * nvec + j]
                        for spot, value in enumerate(values):
                            term = coef * value
                            here = (i, spot)
                            totals[here] = totals[here] + term if here in totals else term
            for (i, spot), value in totals.items():
                held[(i, *group[spot])] = value
        copy_out(step).start()
        return 0

    lax.fori_loop(0, blocks, some_rows, 0)
    for step in range(blocks):
        copy_out(step).wait()


def basis_of(count, sums, work, vec, block_rows):
    nvec, rows, width = work.shape
    small = jax.ShapeDtypeStruct((nvec, nvec), jnp.float32)
    whole = pl.BlockSpec(memory_space=pltpu.VMEM)
    work, vec = (pltpu.with_memory_space_constraint(array, pltpu.VMEM) for array in (work, vec))
    return pl.pallas_call(
        functools.partial(basis_kernel, nvec, count, block_rows),
        in_specs=[whole, whole, whole],
        out_specs=[pl.BlockSpec(memory_space=pl.ANY), whole, whole],
        out_shape=[jax.ShapeDtypeStruct(work.shape, jnp.float32), small, small],
        scratch_shapes=[
            pltpu.VMEM((2, nvec * nvec, SUBLANES, LANES), jnp.float32),
            pltpu.VMEM(work.shape, jnp.float32),
            pltpu.SemaphoreType.DMA((rows // block_rows,)),
        ],
        compiler_params=pltpu.CompilerParams(vmem_limit_bytes=SMALL_VMEM_BYTES),
        cost_estimate=pl.CostEstimate(
            flops=4 * nvec * work.size, bytes_accessed=12 * work.size, transcendentals=0
        ),
        name="basis",
    )(sums, work, vec)


def shards(
    vectors,
    previous,
    beta,
    potential,
    coriolis_fn,
    second_fn,
    rot_const,
    coupling,
    kin_one,
    kin_two,
    kin_three,
    kin_four,
    kin_five,
    kin_six,
    coriolis_derivative,
):
    _, nvec, *points, width = vectors.shape
    rows = points[0] * points[1] * points[2]
    devices = lax.axis_size(ALL_AXES)
    block_index = lax.axis_index("ka")
    nblocks = lax.axis_size("ka")
    row_peers = lax.axis_size("row")
    mode_peers = lax.axis_size("mode")
    row_at = lax.axis_index("row")
    current = vectors.reshape(nvec, rows, width)
    older = previous.reshape(nvec, rows, width)
    block_rows = min(32, rows // 2)

    cut = rows * 3 // 4 // block_rows * block_rows or rows // 2
    starts, stops = [0, cut], [cut, rows]
    parts = [split_rows(current, start, stop) for start, stop in zip(starts, stops)]
    near_first = [pair_exchange(part, "ka", 0) for part in parts]
    near_second = [pair_exchange(part, "ka", 1) for part in parts]
    at = jnp.stack([block_index, row_at, row_at ^ 1]).astype(jnp.int32)
    group = 2 - row_peers % 2
    held = [current]
    if group == 2:
        held.append(lax.ppermute(current, "row", [(i, i ^ 1) for i in range(row_peers)]))
    away = row_peers // group - 1
    row_parts = crossing(tuple(points), at, kin_two, held, away) if away else []
    row_sums = [
        lax.ppermute(
            part, "row", [(i, (i + group * (number + 1)) % row_peers) for i in range(row_peers)]
        )
        for number, part in enumerate(row_parts)
    ]

    span = next((s for s in (256, 128) if width % s == 0 and s % kin_six.shape[0] == 0), width)
    left, mode_mat, tail, near = operators(
        tuple(points),
        group,
        mode_peers * rows,
        width,
        span,
        at,
        coupling,
        (kin_one, kin_two, kin_three, kin_four, kin_five, kin_six, coriolis_derivative),
        row_parts,
    )
    near_first[0] = handed_on(near_first[0], HOP_WEIGHT, [*row_parts, mode_mat])
    near_second[0] = handed_on(near_second[0], HOP_WEIGHT, [*row_parts, mode_mat])
    far_first = [pair_exchange(part, "ka", 0) for part in near_second]
    far_second = [pair_exchange(part, "ka", 1) for part in near_first]
    lower_two = jnp.maximum(block_index - 2, 0)
    far_above, far_below = coupling[1, block_index], coupling[1, lower_two]
    even = block_index % 2 == 0
    far_pair = jnp.stack(
        [jnp.where(even, far_above, far_below), jnp.where(even, far_below, far_above)]
    )
    sums, vec, skip_fn = resident(
        current, second_fn.reshape(rows, width), held[1:], block_rows
    )
    mode_shares = lax.all_to_all(vec, "mode", split_axis=0, concat_axis=0, tiled=True)
    mode_shares = mode_kinetic(mode_shares, mode_mat, mode_peers)
    mode_sum = lax.all_to_all(mode_shares, "mode", split_axis=0, concat_axis=0, tiled=True)
    work = local_terms(
        nblocks, at, rot_const, beta, held, older, potential.reshape(rows, width), left, tail
    )
    work = join_terms(
        at,
        work,
        coriolis_fn.reshape(rows, width),
        near,
        starts,
        near_first,
        near_second,
        [mode_sum, *row_sums],
    )
    for number, start in enumerate(starts):
        work, copied = far_terms(
            far_pair,
            work,
            far_first[number],
            far_second[number],
            skip_fn,
            vec,
            sums,
            start,
            block_rows,
            devices if number == len(starts) - 1 else 1,
        )
        sums = copied[0]
    every_sum = lax.all_to_all(copied, ALL_AXES, split_axis=0, concat_axis=0, tiled=True)
    count = float(devices * rows * width)
    basis, alpha, lower = basis_of(count, every_sum, work, vec, block_rows)
    return (basis.reshape(vectors.shape), alpha, lower)


def solution(mesh):
    return jax.shard_map(
        shards,
        mesh=mesh,
        in_specs=(
            P("ka", None, "mode", "row", None, None),
            P("ka", None, "mode", "row", None, None),
            P(),
            P("mode", "row", None, None),
            P("mode", "row", None, None),
            P("mode", "row", None, None),
            P(),
            P(),
            P(),
            P(),
            P(),
            P(),
            P(),
            P(),
            P(),
        ),
        out_specs=(P("ka", None, "mode", "row", None, None), P(), P()),
        check_vma=False,
    )
```

```python
import functools

import jax
import jax.numpy as jnp
from jax import lax
from jax.experimental import pallas as pl
from jax.experimental.pallas import tpu as pltpu
from jax.sharding import PartitionSpec as P

precise_mode = lax.Precision.HIGHEST
ALL_AXES = ("ka", "mode", "row")
VMEM_BYTES = 32 * 1024 * 1024
SMALL_VMEM_BYTES = 16 * 1024 * 1024
FULL_VMEM_BYTES = 56 * 1024 * 1024
LANES = 128
HOP_WEIGHT = 25_000_000_000
SUBLANES = 8


def precise_dot(left, right):
    return jnp.dot(left, right, precision=precise_mode, preferred_element_type=jnp.float32)


def whole_spec(shape):
    return pl.BlockSpec(shape, lambda *_: (0,) * len(shape))


def pairing(peers, first):
    return [(low, low + 1) for low in range(first, peers - 1, 2)]


def pair_exchange(value, axis, first):
    pairs = pairing(lax.axis_size(axis), first)
    return lax.ppermute(value, axis, pairs + [(high, low) for low, high in pairs])


def pair_forward(value, axis, first):
    peers = lax.axis_size(axis)
    holders = {member for pair in pairing(peers, 1 - first) for member in pair}
    pairs = pairing(peers, first)
    pairs = pairs + [(high, low) for low, high in pairs]
    return lax.ppermute(value, axis, [pair for pair in pairs if pair[0] in holders])


def vector_groups(nvec):
    return [tuple(range(at, min(at + 4, nvec))) for at in range(0, nvec, 4)]


def tiles(rows, width):
    return [
        (slice(r, r + SUBLANES), slice(c, c + LANES))
        for r in range(0, rows, SUBLANES)
        for c in range(0, width, LANES)
    ]


def packed_columns(sums, nvec, offset, lane):
    packed = jnp.zeros((nvec, LANES), jnp.float32)
    for j in range(nvec):
        stacked = jnp.stack([sums(i, j) for i in range(nvec)])
        column = jnp.sum(jnp.sum(stacked, axis=1), axis=1, keepdims=True)
        packed = packed + jnp.where(lane == offset + j, column, 0.0)
    return packed


def add_products(nvec, left_ref, right_ref, sums, number, places, symmetric):
    groups = vector_groups(nvec)
    for ours in groups:
        for other in groups:
            pairs = [(i, j) for i in ours for j in other if i <= j or not symmetric]
            if not pairs:
                continue
            totals = {pair: sums[number, pair[0] * nvec + pair[1]] for pair in pairs}
            for place in places:
                lefts = {i: left_ref[(i, *place)] for i in {p[0] for p in pairs}}
                rights = {j: right_ref[(j, *place)] for j in {p[1] for p in pairs}}
                for i, j in pairs:
                    totals[i, j] = totals[i, j] + lefts[i] * rights[j]
            for i, j in pairs:
                sums[number, i * nvec + j] = totals[i, j]


def resident_kernel(nvec, vec_ref, fn_ref, *refs):
    out_ref, copy_ref, fn_copy_ref, sums = refs[-4:]
    step = pl.program_id(0)

    @pl.when(step == 0)
    def _():
        sums[...] = jnp.zeros_like(sums)

    copy_ref[...] = vec_ref[...]
    fn_copy_ref[...] = fn_ref[...]
    add_products(nvec, vec_ref, vec_ref, sums, 0, tiles(*vec_ref.shape[1:]), True)

    @pl.when(step == pl.num_programs(0) - 1)
    def _():
        lane = lax.broadcasted_iota(jnp.int32, (nvec, LANES), 1)
        out_ref[...] = packed_columns(
            lambda i, j: sums[0, min(i, j) * nvec + max(i, j)], nvec, 2 * nvec, lane
        )


def resident(vec, skip_fn, after, block_rows):
    nvec, rows, width = vec.shape
    block = pl.BlockSpec((nvec, block_rows, width), lambda s: (0, s, 0))
    fn_block = pl.BlockSpec((block_rows, width), lambda s: (s, 0))
    return pl.pallas_call(
        functools.partial(resident_kernel, nvec),
        grid=(rows // block_rows,),
        in_specs=[block, fn_block] + [pl.BlockSpec(memory_space=pl.ANY)] * len(after),
        out_specs=[whole_spec((nvec, LANES)), block, fn_block],
        out_shape=[
            jax.ShapeDtypeStruct((nvec, LANES), jnp.float32),
            jax.ShapeDtypeStruct(vec.shape, jnp.float32),
            jax.ShapeDtypeStruct(skip_fn.shape, jnp.float32),
        ],
        scratch_shapes=[pltpu.VMEM((1, nvec * nvec, SUBLANES, LANES), jnp.float32)],
        compiler_params=pltpu.CompilerParams(vmem_limit_bytes=VMEM_BYTES),
        cost_estimate=pl.CostEstimate(
            flops=nvec * (nvec + 1) * rows * width, bytes_accessed=8 * vec.size, transcendentals=0
        ),
        name="resident",
    )(vec, skip_fn, *after)


def split_kernel(start, vec_ref, out_ref, held, sems):
    count, rows, _ = out_ref.shape
    loads = [
        pltpu.make_async_copy(vec_ref.at[i, pl.ds(start, rows)], held.at[i], sems.at[0, i])
        for i in range(count)
    ]
    stores = [
        pltpu.make_async_copy(held.at[i], out_ref.at[i], sems.at[1, i]) for i in range(count)
    ]
    for load in loads:
        load.start()
    for load, store in zip(loads, stores):
        load.wait()
        store.start()
    for store in stores:
        store.wait()


def split_rows(vec, start, stop):
    nvec, _, width = vec.shape
    shape = (nvec, stop - start, width)
    return pl.pallas_call(
        functools.partial(split_kernel, start),
        in_specs=[pl.BlockSpec(memory_space=pl.ANY)],
        out_specs=pl.BlockSpec(memory_space=pl.ANY),
        out_shape=jax.ShapeDtypeStruct(shape, jnp.float32),
        scratch_shapes=[
            pltpu.VMEM(shape, jnp.float32),
            pltpu.SemaphoreType.DMA((2, nvec)),
        ],
        compiler_params=pltpu.CompilerParams(vmem_limit_bytes=FULL_VMEM_BYTES),
        cost_estimate=pl.CostEstimate(
            flops=0, bytes_accessed=8 * nvec * (stop - start) * width, transcendentals=0
        ),
        name="split_rows",
    )(vec)


def handed_on(array, weight, after=()):
    return pl.pallas_call(
        lambda *_: None,
        in_specs=[pl.BlockSpec(memory_space=pl.ANY)] * (1 + len(after)),
        out_specs=pl.BlockSpec(memory_space=pl.ANY),
        out_shape=jax.ShapeDtypeStruct(array.shape, array.dtype),
        input_output_aliases={0: 0},
        cost_estimate=pl.CostEstimate(flops=weight, bytes_accessed=0, transcendentals=0),
        name="handed_on",
    )(array, *after)


def kron_term(matrix, size, stride, extent, row_offset=0, column_offset=0, sign=1.0):
    points = matrix.shape[0]

    def digits(shape, axis):
        index = lax.broadcasted_iota(jnp.int32, shape, axis)
        return index, lax.rem(lax.div(index, stride), size)

    def picks(offset):
        _, digit = digits((extent, points), 0)
        point = lax.broadcasted_iota(jnp.int32, (extent, points), 1)
        return jnp.where(digit + offset == point, 1.0, 0.0)

    def transposed_dot(one, two):
        return lax.dot_general(
            one, two, (((1,), (1,)), ((), ())), precision=precise_mode,
            preferred_element_type=jnp.float32,
        )

    picked = picks(row_offset)
    picked = 0.5 * (precise_dot(picked, matrix) + sign * transposed_dot(picked, matrix))
    spread = transposed_dot(picked, picks(column_offset))
    row, row_digit = digits((extent, extent), 0)
    column, column_digit = digits((extent, extent), 1)
    same = (row - row_digit * stride) == (column - column_digit * stride)
    return jnp.where(same, spread, 0.0)


def operators_kernel(
    points, group, at_ref, coupling_ref, one_ref, two_ref, three_ref, four_ref, five_ref, six_ref,
    der_ref, *refs,
):
    left_ref, mode_ref, tail_ref, near_ref = refs[-4:]
    points_one, points_two, points_three = points
    rows = points_one * points_two * points_three
    stride = points_two * points_three
    mine = at_ref[1] * points_two
    left_ref[0] = kron_term(two_ref[...], points_two, points_three, rows, mine, mine) + kron_term(
        three_ref[...], points_three, 1, rows
    )
    if group > 1:
        sibling = at_ref[2] * points_two
        left_ref[1] = kron_term(two_ref[...], points_two, points_three, rows, mine, sibling)
    mode_ref[...] = kron_term(one_ref[...], one_ref.shape[0], stride, mode_ref.shape[0])
    width = tail_ref.shape[0]
    fives, sixes = five_ref.shape[0], six_ref.shape[0]
    tail_ref[...] = (
        kron_term(four_ref[...], four_ref.shape[0], fives * sixes, width)
        + kron_term(five_ref[...], fives, sixes, width)
        + kron_term(six_ref[...], sixes, 1, width)
    )
    twist = kron_term(der_ref[...], sixes, 1, near_ref.shape[1], sign=-1.0)
    block = at_ref[0]
    even = lax.rem(block, 2) == 0
    from_above = -coupling_ref[0, block]
    from_below = coupling_ref[0, jnp.maximum(block - 1, 0)]
    near_ref[0] = jnp.where(even, from_above, from_below) * twist
    near_ref[1] = jnp.where(even, from_below, from_above) * twist


def operators(points, group, mode_extent, width, span, at, coupling, matrices, after):
    rows = points[0] * points[1] * points[2]
    shapes = [
        (group, rows, rows), (mode_extent, mode_extent), (width, width), (2, span, span)
    ]
    smem = pl.BlockSpec(memory_space=pltpu.SMEM)
    return pl.pallas_call(
        functools.partial(operators_kernel, points, group),
        in_specs=[smem, smem]
        + [pl.BlockSpec(memory_space=pltpu.VMEM)] * len(matrices)
        + [pl.BlockSpec(memory_space=pl.ANY)] * len(after),
        out_specs=[pl.BlockSpec(memory_space=pltpu.VMEM)] * len(shapes),
        out_shape=[jax.ShapeDtypeStruct(shape, jnp.float32) for shape in shapes],
        compiler_params=pltpu.CompilerParams(vmem_limit_bytes=VMEM_BYTES),
        cost_estimate=pl.CostEstimate(
            flops=500_000_000, bytes_accessed=4_000_000, transcendentals=0
        ),
        name="operators",
    )(at, coupling, *matrices, *after)


def crossing_kernel(points, group, at_ref, two_ref, *refs):
    points_one, points_two, points_three = points
    held_refs, out_refs = refs[:group], refs[group:]
    owners = [at_ref[1], at_ref[2]][:group]
    peers = two_ref.shape[0] // points_two
    stride = points_two * points_three
    for number, out_ref in enumerate(out_refs):
        target = lax.rem(at_ref[1] + group * (number + 1), peers) * points_two
        coefs = {
            (a, k, b): 0.5
            * (
                two_ref[target + a, owners[k] * points_two + b]
                + two_ref[owners[k] * points_two + b, target + a]
            )
            for a in range(points_two)
            for k in range(group)
            for b in range(points_two)
        }
        for start in range(0, points_one * stride, stride):
            for _, lanes in tiles(SUBLANES, out_ref.shape[2]):
                for inner in range(0, points_three, SUBLANES):
                    values = {
                        (k, b): held_refs[k][0, pl.ds(start + b * points_three + inner, SUBLANES), lanes]
                        for k in range(group)
                        for b in range(points_two)
                    }
                    for a in range(points_two):
                        total = None
                        for (k, b), value in values.items():
                            term = coefs[a, k, b] * value
                            total = term if total is None else total + term
                        out_ref[0, pl.ds(start + a * points_three + inner, SUBLANES), lanes] = total


def crossing(points, at, two, held, count):
    nvec, rows, width = held[0].shape
    one = pl.BlockSpec((1, rows, width), lambda i: (i, 0, 0))
    smem = pl.BlockSpec(memory_space=pltpu.SMEM)
    return pl.pallas_call(
        functools.partial(crossing_kernel, points, len(held)),
        grid=(nvec,),
        in_specs=[smem, smem] + [one] * len(held),
        out_specs=[one] * count,
        out_shape=[jax.ShapeDtypeStruct(held[0].shape, jnp.float32)] * count,
        compiler_params=pltpu.CompilerParams(vmem_limit_bytes=VMEM_BYTES),
        cost_estimate=pl.CostEstimate(
            flops=2 * held[0].size * points[1] * len(held) * count,
            bytes_accessed=4 * held[0].size * (len(held) + count),
            transcendentals=0,
        ),
        name="crossing",
    )(at, two, *held)


def local_kernel(nvec, nblocks, group, at_ref, rot_ref, beta_ref, *refs):
    held_refs = refs[:group]
    old_ref, pot_ref, left_ref, tail_ref, out_ref = refs[group:]
    me = pl.program_id(0)
    block = at_ref[0]
    level = (block - nblocks // 2).astype(jnp.float32)
    current = held_refs[0][0]
    total = (pot_ref[...] + rot_ref[block] * level * level) * current
    for j in range(nvec):
        total = total - beta_ref[me, j] * old_ref[j]
    total = total + precise_dot(current, tail_ref[...])
    for number, held_ref in enumerate(held_refs):
        total = total + precise_dot(left_ref[number], held_ref[0])
    out_ref[0] = total


def local_terms(nblocks, at, rot_const, beta, held, old, pot, left, tail):
    nvec, rows, width = old.shape
    one = pl.BlockSpec((1, rows, width), lambda i: (i, 0, 0))
    smem = pl.BlockSpec(memory_space=pltpu.SMEM)
    return pl.pallas_call(
        functools.partial(local_kernel, nvec, nblocks, len(held)),
        grid=(nvec,),
        in_specs=[smem, smem, smem]
        + [one] * len(held)
        + [
            whole_spec(old.shape),
            whole_spec(pot.shape),
            pl.BlockSpec((len(held), rows, rows), lambda i: (0, 0, 0)),
            whole_spec(tail.shape),
        ],
        out_specs=one,
        out_shape=jax.ShapeDtypeStruct(old.shape, jnp.float32),
        compiler_params=pltpu.CompilerParams(vmem_limit_bytes=VMEM_BYTES),
        cost_estimate=pl.CostEstimate(
            flops=12 * old.size * (rows * len(held) + width),
            bytes_accessed=4 * old.size * (2 + len(held)),
            transcendentals=0,
        ),
        name="local_terms",
    )(at, rot_const, beta, *held, old, pot, left, tail)


def mode_kinetic_kernel(peers, in_ref, mat_ref, out_ref):
    rows = in_ref.shape[2]
    field = jnp.concatenate([in_ref[peer, 0] for peer in range(peers)], axis=0)
    field = precise_dot(mat_ref[...], field)
    for peer in range(peers):
        out_ref[peer, 0] = field[peer * rows : (peer + 1) * rows]


def mode_kinetic(field, matrix, peers):
    nvec, rows, width = field.shape
    held = nvec // peers
    block = pl.BlockSpec((peers, 1, rows, width), lambda q: (0, q, 0, 0))
    out = pl.pallas_call(
        functools.partial(mode_kinetic_kernel, peers),
        grid=(held,),
        in_specs=[block, whole_spec(matrix.shape)],
        out_specs=block,
        out_shape=jax.ShapeDtypeStruct((peers, held, rows, width), jnp.float32),
        compiler_params=pltpu.CompilerParams(vmem_limit_bytes=VMEM_BYTES),
        cost_estimate=pl.CostEstimate(
            flops=12 * field.size * matrix.shape[0], bytes_accessed=8 * field.size, transcendentals=0
        ),
        name="mode_kinetic",
    )(field.reshape(peers, held, rows, width), matrix)
    return out.reshape(field.shape)


def join_kernel(starts, sum_count, at_ref, work_ref, cor_ref, near_ref, *refs):
    pieces = len(starts)
    first_refs, second_refs = refs[:pieces], refs[pieces : 2 * pieces]
    sum_refs = refs[2 * pieces : 2 * pieces + sum_count]
    out_ref = refs[-1]
    span = near_ref.shape[1]
    even = lax.rem(at_ref[0], 2) == 0
    for start, first_ref, second_ref in zip(starts, first_refs, second_refs):
        place = slice(start, start + first_ref.shape[1])
        for at in range(0, work_ref.shape[2], span):
            part = slice(at, at + span)
            total = work_ref[0, place, part]
            for sum_ref in sum_refs:
                total = total + sum_ref[0, place, part]
            twist_fn = cor_ref[place, part]
            if_even = jnp.where(even, twist_fn, 1.0)
            if_odd = jnp.where(even, 1.0, twist_fn)
            total = total + if_even * precise_dot(
                if_odd * first_ref[0, :, part], near_ref[0]
            )
            out_ref[0, place, part] = total + if_odd * precise_dot(
                if_even * second_ref[0, :, part], near_ref[1]
            )


def join_terms(at, work, cor, near, starts, first, second, sums):
    nvec, rows, width = work.shape
    one = pl.BlockSpec((1, rows, width), lambda i: (i, 0, 0))
    pieces = [pl.BlockSpec((1, b.shape[1], width), lambda i: (i, 0, 0)) for b in first]
    return pl.pallas_call(
        functools.partial(join_kernel, tuple(starts), len(sums)),
        grid=(nvec,),
        in_specs=[
            pl.BlockSpec(memory_space=pltpu.SMEM), one, whole_spec(cor.shape), whole_spec(near.shape)
        ]
        + pieces
        + pieces
        + [one] * len(sums),
        out_specs=one,
        out_shape=jax.ShapeDtypeStruct(work.shape, jnp.float32),
        compiler_params=pltpu.CompilerParams(vmem_limit_bytes=VMEM_BYTES),
        cost_estimate=pl.CostEstimate(
            flops=24 * work.size * near.shape[1], bytes_accessed=24 * work.size, transcendentals=0
        ),
        name="join_terms",
    )(at, work, cor, near, *first, *second, *sums)


def far_terms_kernel(
    nvec, start, coef_ref, work_ref, first_ref, second_ref, fn_ref, vec_ref, before_ref, out_ref,
    sum_ref, sums,
):
    del work_ref
    step = pl.program_id(0)
    _, block_rows, width = first_ref.shape

    @pl.when(step == 0)
    def _():
        sums[...] = jnp.zeros_like(sums)

    at = pl.multiple_of(start + step * block_rows, SUBLANES)
    places = []
    for rows_here, lanes in tiles(block_rows, width):
        place = (pl.ds(at + rows_here.start, SUBLANES), lanes)
        places.append(place)
        skip_fn = fn_ref[place]
        first_fn = coef_ref[0] * skip_fn
        second_fn = coef_ref[1] * skip_fn
        for i in range(nvec):
            out_ref[(i, *place)] = (
                out_ref[(i, *place)]
                + first_fn * first_ref[i, rows_here, lanes]
                + second_fn * second_ref[i, rows_here, lanes]
            )
    add_products(nvec, vec_ref, out_ref, sums, 0, places, False)
    add_products(nvec, out_ref, out_ref, sums, 1, places, True)

    @pl.when(step == pl.num_programs(0) - 1)
    def _():
        lane = lax.broadcasted_iota(jnp.int32, (nvec, LANES), 1)
        packed = before_ref[...]
        packed = packed + packed_columns(lambda i, j: sums[0, j * nvec + i], nvec, 0, lane)
        packed = packed + packed_columns(
            lambda i, j: sums[1, min(i, j) * nvec + max(i, j)], nvec, nvec, lane
        )
        sum_ref[...] = jnp.broadcast_to(packed[None], sum_ref.shape)


def far_terms(coef, work, first, second, skip_fn, vec, before, start, block_rows, copies):
    nvec, _, width = work.shape
    rows = first.shape[1]
    whole = pl.BlockSpec(memory_space=pltpu.VMEM)
    block = pl.BlockSpec((nvec, block_rows, width), lambda s: (0, s, 0))
    work, skip_fn, vec = (
        pltpu.with_memory_space_constraint(array, pltpu.VMEM) for array in (work, skip_fn, vec)
    )
    return pl.pallas_call(
        functools.partial(far_terms_kernel, nvec, start),
        grid=(rows // block_rows,),
        in_specs=[
            pl.BlockSpec(memory_space=pltpu.SMEM), whole, block, block, whole, whole, whole
        ],
        out_specs=[whole, whole],
        out_shape=[
            jax.ShapeDtypeStruct(work.shape, jnp.float32),
            jax.ShapeDtypeStruct((copies, nvec, LANES), jnp.float32),
        ],
        scratch_shapes=[pltpu.VMEM((2, nvec * nvec, SUBLANES, LANES), jnp.float32)],
        input_output_aliases={1: 0},
        compiler_params=pltpu.CompilerParams(vmem_limit_bytes=SMALL_VMEM_BYTES),
        cost_estimate=pl.CostEstimate(
            flops=3 * nvec * nvec * rows * width,
            bytes_accessed=20 * first.size,
            transcendentals=0,
        ),
        name="far_terms",
    )(coef, work, first, second, skip_fn, vec, before)


def across(column, row):
    return jnp.broadcast_to(column[row : row + 1, :], (SUBLANES, LANES))


def spread_columns(matrix, start, count):
    return [
        jnp.broadcast_to(matrix[:, k : k + 1], (count, LANES)) for k in range(start, start + count)
    ]


def spread_dot(left, right):
    count = len(left)
    columns = []
    for column in right:
        terms = [left[m] * jnp.broadcast_to(column[m : m + 1, :], left[m].shape) for m in range(count)]
        while len(terms) > 1:
            terms = [sum(terms[k + 1 : k + 2], terms[k]) for k in range(0, len(terms), 2)]
        columns.append(terms[0])
    return columns


def small_algebra(nvec, count, packed):
    packed = packed * (1.0 / count)
    cross = spread_columns(packed.T[0:nvec, :], 0, nvec)
    cross_turned = spread_columns(packed, 0, nvec)
    gram = spread_columns(packed, nvec, nvec)
    vec_gram = spread_columns(packed, 2 * nvec, nvec)
    total = [2.0 * c - d for c, d in zip(cross, spread_dot(vec_gram, cross))]
    total_turned = [2.0 * c - d for c, d in zip(cross_turned, spread_dot(cross_turned, vec_gram))]
    inner = [d - c for c, d in zip(cross, spread_dot(vec_gram, total))]
    gram = [
        g - one + other
        for g, one, other in zip(
            gram, spread_dot(cross_turned, total), spread_dot(total_turned, inner)
        )
    ]
    row = lax.broadcasted_iota(jnp.int32, (nvec, LANES), 0)
    inverse = [jnp.where(row == k, 1.0, 0.0) for k in range(nvec)]
    lower = []
    for at in range(nvec):
        pivot = jnp.broadcast_to(gram[at][at : at + 1, :], (nvec, LANES))
        scale = lax.rsqrt(pivot)
        scale = scale * (1.5 - 0.5 * pivot * scale * scale)
        scaled = gram[at] * scale
        lower.append(jnp.where(row >= at, scaled, 0.0))
        factor = jnp.where(row > at, scaled, 0.0)
        for k in range(at + 1, nvec):
            here = jnp.broadcast_to(gram[k][at : at + 1, :], (nvec, LANES)) * scale
            gram[k] = gram[k] - factor * here
        for k in range(at + 1):
            here = jnp.broadcast_to(inverse[k][at : at + 1, :], (nvec, LANES)) * scale
            inverse[k] = jnp.where(row == at, here, inverse[k] - factor * here)
    mixing = [-column for column in spread_dot(inverse, total_turned)]
    return total, lower, inverse, mixing


def gathered_columns(columns):
    lane = lax.broadcasted_iota(jnp.int32, columns[0].shape, 1)
    matrix = jnp.zeros_like(columns[0])
    for k, column in enumerate(columns):
        matrix = jnp.where(lane == k, column, matrix)
    return matrix[:, : len(columns)]


def basis_kernel(
    nvec, count, block_rows, sum_ref, work_ref, vec_ref, out_ref, alpha_ref, lower_ref, coefs, held, sems
):
    packed = sum_ref[0]
    for other in range(1, sum_ref.shape[0]):
        packed = packed + sum_ref[other]
    total, lower, inverse, mixing = small_algebra(nvec, count, packed)
    for number, columns in enumerate((inverse, mixing)):
        for j in range(nvec):
            for i in range(nvec):
                if number == 1 or j <= i:
                    coefs[number, i * nvec + j] = across(columns[j], i)
    alpha_ref[...] = gathered_columns(total)
    lower_ref[...] = gathered_columns(lower)
    rows, width = held.shape[1:]
    blocks = rows // block_rows

    def copy_out(step):
        place = pl.ds(pl.multiple_of(step * block_rows, block_rows), block_rows)
        return pltpu.make_async_copy(held.at[:, place], out_ref.at[:, place], sems.at[step])

    def some_rows(step, _):
        start = pl.multiple_of(step * block_rows, block_rows)
        places = [
            (pl.ds(start + place.start, SUBLANES), lanes)
            for place, lanes in tiles(block_rows, width)
        ]
        for at in range(0, len(places), 4):
            group = places[at : at + 4]
            totals = {}
            for number, ref in ((1, vec_ref), (0, work_ref)):
                for j in range(nvec):
                    values = [ref[(j, *place)] for place in group]
                    for i in range(nvec):
                        if number == 0 and j > i:
                            continue
                        coef = coefs[number, i * nvec + j]
                        for spot, value in enumerate(values):
                            term = coef * value
                            here = (i, spot)
                            totals[here] = totals[here] + term if here in totals else term
            for (i, spot), value in totals.items():
                held[(i, *group[spot])] = value
        copy_out(step).start()
        return 0

    lax.fori_loop(0, blocks, some_rows, 0)
    for step in range(blocks):
        copy_out(step).wait()


def basis_of(count, sums, work, vec, block_rows):
    nvec, rows, width = work.shape
    small = jax.ShapeDtypeStruct((nvec, nvec), jnp.float32)
    whole = pl.BlockSpec(memory_space=pltpu.VMEM)
    work, vec = (pltpu.with_memory_space_constraint(array, pltpu.VMEM) for array in (work, vec))
    return pl.pallas_call(
        functools.partial(basis_kernel, nvec, count, block_rows),
        in_specs=[whole, whole, whole],
        out_specs=[pl.BlockSpec(memory_space=pl.ANY), whole, whole],
        out_shape=[jax.ShapeDtypeStruct(work.shape, jnp.float32), small, small],
        scratch_shapes=[
            pltpu.VMEM((2, nvec * nvec, SUBLANES, LANES), jnp.float32),
            pltpu.VMEM(work.shape, jnp.float32),
            pltpu.SemaphoreType.DMA((rows // block_rows,)),
        ],
        compiler_params=pltpu.CompilerParams(vmem_limit_bytes=SMALL_VMEM_BYTES),
        cost_estimate=pl.CostEstimate(
            flops=4 * nvec * work.size, bytes_accessed=12 * work.size, transcendentals=0
        ),
        name="basis",
    )(sums, work, vec)


def shards(
    vectors,
    previous,
    beta,
    potential,
    coriolis_fn,
    second_fn,
    rot_const,
    coupling,
    kin_one,
    kin_two,
    kin_three,
    kin_four,
    kin_five,
    kin_six,
    coriolis_derivative,
):
    _, nvec, *points, width = vectors.shape
    rows = points[0] * points[1] * points[2]
    devices = lax.axis_size(ALL_AXES)
    block_index = lax.axis_index("ka")
    nblocks = lax.axis_size("ka")
    row_peers = lax.axis_size("row")
    mode_peers = lax.axis_size("mode")
    row_at = lax.axis_index("row")
    current = vectors.reshape(nvec, rows, width)
    older = previous.reshape(nvec, rows, width)
    block_rows = min(32, rows // 2)

    cut = rows * 3 // 4 // block_rows * block_rows or rows // 2
    starts, stops = [0, cut], [cut, rows]
    parts = [split_rows(current, start, stop) for start, stop in zip(starts, stops)]
    near_first = [pair_exchange(part, "ka", 0) for part in parts]
    near_second = [pair_exchange(part, "ka", 1) for part in parts]
    at = jnp.stack([block_index, row_at, row_at ^ 1]).astype(jnp.int32)
    group = 2 - row_peers % 2
    held = [current]
    if group == 2:
        held.append(lax.ppermute(current, "row", [(i, i ^ 1) for i in range(row_peers)]))
    away = row_peers // group - 1
    row_parts = crossing(tuple(points), at, kin_two, held, away) if away else []
    row_sums = [
        lax.ppermute(
            part, "row", [(i, (i + group * (number + 1)) % row_peers) for i in range(row_peers)]
        )
        for number, part in enumerate(row_parts)
    ]

    span = next((s for s in (256, 128) if width % s == 0 and s % kin_six.shape[0] == 0), width)
    left, mode_mat, tail, near = operators(
        tuple(points),
        group,
        mode_peers * rows,
        width,
        span,
        at,
        coupling,
        (kin_one, kin_two, kin_three, kin_four, kin_five, kin_six, coriolis_derivative),
        row_parts,
    )
    near_first[0] = handed_on(near_first[0], HOP_WEIGHT, [*row_parts, mode_mat])
    near_second[0] = handed_on(near_second[0], HOP_WEIGHT, [*row_parts, mode_mat])
    far_first = [pair_forward(part, "ka", 0) for part in near_second]
    far_second = [pair_forward(part, "ka", 1) for part in near_first]
    lower_two = jnp.maximum(block_index - 2, 0)
    far_above, far_below = coupling[1, block_index], coupling[1, lower_two]
    even = block_index % 2 == 0
    far_pair = jnp.stack(
        [jnp.where(even, far_above, far_below), jnp.where(even, far_below, far_above)]
    )
    sums, vec, skip_fn = resident(
        current, second_fn.reshape(rows, width), held[1:], block_rows
    )
    mode_shares = lax.all_to_all(vec, "mode", split_axis=0, concat_axis=0, tiled=True)
    mode_shares = mode_kinetic(mode_shares, mode_mat, mode_peers)
    mode_sum = lax.all_to_all(mode_shares, "mode", split_axis=0, concat_axis=0, tiled=True)
    work = local_terms(
        nblocks, at, rot_const, beta, held, older, potential.reshape(rows, width), left, tail
    )
    work = join_terms(
        at,
        work,
        coriolis_fn.reshape(rows, width),
        near,
        starts,
        near_first,
        near_second,
        [mode_sum, *row_sums],
    )
    for number, start in enumerate(starts):
        work, copied = far_terms(
            far_pair,
            work,
            far_first[number],
            far_second[number],
            skip_fn,
            vec,
            sums,
            start,
            block_rows,
            devices if number == len(starts) - 1 else 1,
        )
        sums = copied[0]
    every_sum = lax.all_to_all(copied, ALL_AXES, split_axis=0, concat_axis=0, tiled=True)
    count = float(devices * rows * width)
    basis, alpha, lower = basis_of(count, every_sum, work, vec, block_rows)
    return (basis.reshape(vectors.shape), alpha, lower)


def solution(mesh):
    return jax.shard_map(
        shards,
        mesh=mesh,
        in_specs=(
            P("ka", None, "mode", "row", None, None),
            P("ka", None, "mode", "row", None, None),
            P(),
            P("mode", "row", None, None),
            P("mode", "row", None, None),
            P("mode", "row", None, None),
            P(),
            P(),
            P(),
            P(),
            P(),
            P(),
            P(),
            P(),
            P(),
        ),
        out_specs=(P("ka", None, "mode", "row", None, None), P(), P()),
        check_vma=False,
    )
```

```python
import functools

import jax
import jax.numpy as jnp
from jax import lax
from jax.experimental import pallas as pl
from jax.experimental.pallas import tpu as pltpu
from jax.sharding import PartitionSpec as P

precise_mode = lax.Precision.HIGHEST
ALL_AXES = ("ka", "mode", "row")
VMEM_BYTES = 32 * 1024 * 1024
SMALL_VMEM_BYTES = 16 * 1024 * 1024
FULL_VMEM_BYTES = 56 * 1024 * 1024
LANES = 128
HOP_WEIGHT = 25_000_000_000
SUBLANES = 8


def precise_dot(left, right):
    return jnp.dot(left, right, precision=precise_mode, preferred_element_type=jnp.float32)


def whole_spec(shape):
    return pl.BlockSpec(shape, lambda *_: (0,) * len(shape))


def pair_exchange(value, axis, first):
    peers = lax.axis_size(axis)
    pairs = []
    for low in range(first, peers - 1, 2):
        pairs += [(low, low + 1), (low + 1, low)]
    return lax.ppermute(value, axis, pairs)


def vector_groups(nvec):
    return [tuple(range(at, min(at + 4, nvec))) for at in range(0, nvec, 4)]


def tiles(rows, width):
    return [
        (slice(r, r + SUBLANES), slice(c, c + LANES))
        for r in range(0, rows, SUBLANES)
        for c in range(0, width, LANES)
    ]


def packed_columns(sums, nvec, offset, lane):
    packed = jnp.zeros((nvec, LANES), jnp.float32)
    for j in range(nvec):
        stacked = jnp.stack([sums(i, j) for i in range(nvec)])
        column = jnp.sum(jnp.sum(stacked, axis=1), axis=1, keepdims=True)
        packed = packed + jnp.where(lane == offset + j, column, 0.0)
    return packed


def add_products(nvec, left_ref, right_ref, sums, number, places, symmetric):
    groups = vector_groups(nvec)
    for ours in groups:
        for other in groups:
            pairs = [(i, j) for i in ours for j in other if i <= j or not symmetric]
            if not pairs:
                continue
            totals = {pair: sums[number, pair[0] * nvec + pair[1]] for pair in pairs}
            for place in places:
                lefts = {i: left_ref[(i, *place)] for i in {p[0] for p in pairs}}
                rights = {j: right_ref[(j, *place)] for j in {p[1] for p in pairs}}
                for i, j in pairs:
                    totals[i, j] = totals[i, j] + lefts[i] * rights[j]
            for i, j in pairs:
                sums[number, i * nvec + j] = totals[i, j]


def resident_kernel(nvec, vec_ref, fn_ref, *refs):
    out_ref, copy_ref, fn_copy_ref, sums = refs[-4:]
    step = pl.program_id(0)

    @pl.when(step == 0)
    def _():
        sums[...] = jnp.zeros_like(sums)

    copy_ref[...] = vec_ref[...]
    fn_copy_ref[...] = fn_ref[...]
    add_products(nvec, vec_ref, vec_ref, sums, 0, tiles(*vec_ref.shape[1:]), True)

    @pl.when(step == pl.num_programs(0) - 1)
    def _():
        lane = lax.broadcasted_iota(jnp.int32, (nvec, LANES), 1)
        out_ref[...] = packed_columns(
            lambda i, j: sums[0, min(i, j) * nvec + max(i, j)], nvec, 2 * nvec, lane
        )


def resident(vec, skip_fn, after, block_rows):
    nvec, rows, width = vec.shape
    block = pl.BlockSpec((nvec, block_rows, width), lambda s: (0, s, 0))
    fn_block = pl.BlockSpec((block_rows, width), lambda s: (s, 0))
    return pl.pallas_call(
        functools.partial(resident_kernel, nvec),
        grid=(rows // block_rows,),
        in_specs=[block, fn_block] + [pl.BlockSpec(memory_space=pl.ANY)] * len(after),
        out_specs=[whole_spec((nvec, LANES)), block, fn_block],
        out_shape=[
            jax.ShapeDtypeStruct((nvec, LANES), jnp.float32),
            jax.ShapeDtypeStruct(vec.shape, jnp.float32),
            jax.ShapeDtypeStruct(skip_fn.shape, jnp.float32),
        ],
        scratch_shapes=[pltpu.VMEM((1, nvec * nvec, SUBLANES, LANES), jnp.float32)],
        compiler_params=pltpu.CompilerParams(vmem_limit_bytes=VMEM_BYTES),
        cost_estimate=pl.CostEstimate(
            flops=nvec * (nvec + 1) * rows * width, bytes_accessed=8 * vec.size, transcendentals=0
        ),
        name="resident",
    )(vec, skip_fn, *after)


def split_kernel(start, vec_ref, out_ref, held, sems):
    count, rows, _ = out_ref.shape
    size = 2 - count % 2
    spots = [(i // size, pl.ds(i, size)) for i in range(0, count, size)]
    loads = [
        pltpu.make_async_copy(vec_ref.at[some, pl.ds(start, rows)], held.at[some], sems.at[0, i])
        for i, some in spots
    ]
    stores = [
        pltpu.make_async_copy(held.at[some], out_ref.at[some], sems.at[1, i]) for i, some in spots
    ]
    for load in loads:
        load.start()
    for load, store in zip(loads, stores):
        load.wait()
        store.start()
    for store in stores:
        store.wait()


def split_rows(vec, start, stop):
    nvec, _, width = vec.shape
    shape = (nvec, stop - start, width)
    return pl.pallas_call(
        functools.partial(split_kernel, start),
        in_specs=[pl.BlockSpec(memory_space=pl.ANY)],
        out_specs=pl.BlockSpec(memory_space=pl.ANY),
        out_shape=jax.ShapeDtypeStruct(shape, jnp.float32),
        scratch_shapes=[
            pltpu.VMEM(shape, jnp.float32),
            pltpu.SemaphoreType.DMA((2, nvec)),
        ],
        compiler_params=pltpu.CompilerParams(vmem_limit_bytes=FULL_VMEM_BYTES),
        cost_estimate=pl.CostEstimate(
            flops=0, bytes_accessed=8 * nvec * (stop - start) * width, transcendentals=0
        ),
        name="split_rows",
    )(vec)


def handed_on(array, weight, after=()):
    return pl.pallas_call(
        lambda *_: None,
        in_specs=[pl.BlockSpec(memory_space=pl.ANY)] * (1 + len(after)),
        out_specs=pl.BlockSpec(memory_space=pl.ANY),
        out_shape=jax.ShapeDtypeStruct(array.shape, array.dtype),
        input_output_aliases={0: 0},
        cost_estimate=pl.CostEstimate(flops=weight, bytes_accessed=0, transcendentals=0),
        name="handed_on",
    )(array, *after)


def kron_term(matrix, size, stride, extent, row_offset=0, column_offset=0, sign=1.0):
    points = matrix.shape[0]

    def digits(shape, axis):
        index = lax.broadcasted_iota(jnp.int32, shape, axis)
        return index, lax.rem(lax.div(index, stride), size)

    def picks(offset):
        _, digit = digits((extent, points), 0)
        point = lax.broadcasted_iota(jnp.int32, (extent, points), 1)
        return jnp.where(digit + offset == point, 1.0, 0.0)

    def transposed_dot(one, two):
        return lax.dot_general(
            one, two, (((1,), (1,)), ((), ())), precision=precise_mode,
            preferred_element_type=jnp.float32,
        )

    picked = picks(row_offset)
    picked = 0.5 * (precise_dot(picked, matrix) + sign * transposed_dot(picked, matrix))
    spread = transposed_dot(picked, picks(column_offset))
    row, row_digit = digits((extent, extent), 0)
    column, column_digit = digits((extent, extent), 1)
    same = (row - row_digit * stride) == (column - column_digit * stride)
    return jnp.where(same, spread, 0.0)


def operators_kernel(
    points, group, at_ref, coupling_ref, one_ref, two_ref, three_ref, four_ref, five_ref, six_ref,
    der_ref, *refs,
):
    left_ref, mode_ref, tail_ref, near_ref = refs[-4:]
    points_one, points_two, points_three = points
    rows = points_one * points_two * points_three
    stride = points_two * points_three
    mine = at_ref[1] * points_two
    left_ref[0] = kron_term(two_ref[...], points_two, points_three, rows, mine, mine) + kron_term(
        three_ref[...], points_three, 1, rows
    )
    if group > 1:
        sibling = at_ref[2] * points_two
        left_ref[1] = kron_term(two_ref[...], points_two, points_three, rows, mine, sibling)
    mode_ref[...] = kron_term(one_ref[...], one_ref.shape[0], stride, mode_ref.shape[0])
    width = tail_ref.shape[0]
    fives, sixes = five_ref.shape[0], six_ref.shape[0]
    tail_ref[...] = (
        kron_term(four_ref[...], four_ref.shape[0], fives * sixes, width)
        + kron_term(five_ref[...], fives, sixes, width)
        + kron_term(six_ref[...], sixes, 1, width)
    )
    twist = kron_term(der_ref[...], sixes, 1, near_ref.shape[1], sign=-1.0)
    block = at_ref[0]
    even = lax.rem(block, 2) == 0
    from_above = -coupling_ref[0, block]
    from_below = coupling_ref[0, jnp.maximum(block - 1, 0)]
    near_ref[0] = jnp.where(even, from_above, from_below) * twist
    near_ref[1] = jnp.where(even, from_below, from_above) * twist


def operators(points, group, mode_extent, width, span, at, coupling, matrices, after):
    rows = points[0] * points[1] * points[2]
    shapes = [
        (group, rows, rows), (mode_extent, mode_extent), (width, width), (2, span, span)
    ]
    smem = pl.BlockSpec(memory_space=pltpu.SMEM)
    return pl.pallas_call(
        functools.partial(operators_kernel, points, group),
        in_specs=[smem, smem]
        + [pl.BlockSpec(memory_space=pltpu.VMEM)] * len(matrices)
        + [pl.BlockSpec(memory_space=pl.ANY)] * len(after),
        out_specs=[pl.BlockSpec(memory_space=pltpu.VMEM)] * len(shapes),
        out_shape=[jax.ShapeDtypeStruct(shape, jnp.float32) for shape in shapes],
        compiler_params=pltpu.CompilerParams(vmem_limit_bytes=VMEM_BYTES),
        cost_estimate=pl.CostEstimate(
            flops=500_000_000, bytes_accessed=4_000_000, transcendentals=0
        ),
        name="operators",
    )(at, coupling, *matrices, *after)


def crossing_kernel(points, group, at_ref, two_ref, *refs):
    points_one, points_two, points_three = points
    held_refs, out_refs = refs[:group], refs[group:]
    owners = [at_ref[1], at_ref[2]][:group]
    peers = two_ref.shape[0] // points_two
    stride = points_two * points_three
    for number, out_ref in enumerate(out_refs):
        target = lax.rem(at_ref[1] + group * (number + 1), peers) * points_two
        coefs = {
            (a, k, b): 0.5
            * (
                two_ref[target + a, owners[k] * points_two + b]
                + two_ref[owners[k] * points_two + b, target + a]
            )
            for a in range(points_two)
            for k in range(group)
            for b in range(points_two)
        }
        for start in range(0, points_one * stride, stride):
            for _, lanes in tiles(SUBLANES, out_ref.shape[2]):
                for inner in range(0, points_three, SUBLANES):
                    values = {
                        (k, b): held_refs[k][0, pl.ds(start + b * points_three + inner, SUBLANES), lanes]
                        for k in range(group)
                        for b in range(points_two)
                    }
                    for a in range(points_two):
                        total = None
                        for (k, b), value in values.items():
                            term = coefs[a, k, b] * value
                            total = term if total is None else total + term
                        out_ref[0, pl.ds(start + a * points_three + inner, SUBLANES), lanes] = total


def crossing(points, at, two, held, count):
    nvec, rows, width = held[0].shape
    one = pl.BlockSpec((1, rows, width), lambda i: (i, 0, 0))
    smem = pl.BlockSpec(memory_space=pltpu.SMEM)
    return pl.pallas_call(
        functools.partial(crossing_kernel, points, len(held)),
        grid=(nvec,),
        in_specs=[smem, smem] + [one] * len(held),
        out_specs=[one] * count,
        out_shape=[jax.ShapeDtypeStruct(held[0].shape, jnp.float32)] * count,
        compiler_params=pltpu.CompilerParams(vmem_limit_bytes=VMEM_BYTES),
        cost_estimate=pl.CostEstimate(
            flops=2 * held[0].size * points[1] * len(held) * count,
            bytes_accessed=4 * held[0].size * (len(held) + count),
            transcendentals=0,
        ),
        name="crossing",
    )(at, two, *held)


def local_kernel(nvec, nblocks, group, at_ref, rot_ref, beta_ref, *refs):
    held_refs = refs[:group]
    old_ref, pot_ref, left_ref, tail_ref, out_ref = refs[group:]
    me = pl.program_id(0)
    block = at_ref[0]
    level = (block - nblocks // 2).astype(jnp.float32)
    current = held_refs[0][0]
    total = (pot_ref[...] + rot_ref[block] * level * level) * current
    for j in range(nvec):
        total = total - beta_ref[me, j] * old_ref[j]
    total = total + precise_dot(current, tail_ref[...])
    for number, held_ref in enumerate(held_refs):
        total = total + precise_dot(left_ref[number], held_ref[0])
    out_ref[0] = total


def local_terms(nblocks, at, rot_const, beta, held, old, pot, left, tail):
    nvec, rows, width = old.shape
    one = pl.BlockSpec((1, rows, width), lambda i: (i, 0, 0))
    smem = pl.BlockSpec(memory_space=pltpu.SMEM)
    return pl.pallas_call(
        functools.partial(local_kernel, nvec, nblocks, len(held)),
        grid=(nvec,),
        in_specs=[smem, smem, smem]
        + [one] * len(held)
        + [
            whole_spec(old.shape),
            whole_spec(pot.shape),
            pl.BlockSpec((len(held), rows, rows), lambda i: (0, 0, 0)),
            whole_spec(tail.shape),
        ],
        out_specs=one,
        out_shape=jax.ShapeDtypeStruct(old.shape, jnp.float32),
        compiler_params=pltpu.CompilerParams(vmem_limit_bytes=VMEM_BYTES),
        cost_estimate=pl.CostEstimate(
            flops=12 * old.size * (rows * len(held) + width),
            bytes_accessed=4 * old.size * (2 + len(held)),
            transcendentals=0,
        ),
        name="local_terms",
    )(at, rot_const, beta, *held, old, pot, left, tail)


def mode_kinetic_kernel(peers, in_ref, mat_ref, out_ref):
    rows = in_ref.shape[2]
    field = jnp.concatenate([in_ref[peer, 0] for peer in range(peers)], axis=0)
    field = precise_dot(mat_ref[...], field)
    for peer in range(peers):
        out_ref[peer, 0] = field[peer * rows : (peer + 1) * rows]


def mode_kinetic(field, matrix, peers):
    nvec, rows, width = field.shape
    held = nvec // peers
    block = pl.BlockSpec((peers, 1, rows, width), lambda q: (0, q, 0, 0))
    out = pl.pallas_call(
        functools.partial(mode_kinetic_kernel, peers),
        grid=(held,),
        in_specs=[block, whole_spec(matrix.shape)],
        out_specs=block,
        out_shape=jax.ShapeDtypeStruct((peers, held, rows, width), jnp.float32),
        compiler_params=pltpu.CompilerParams(vmem_limit_bytes=VMEM_BYTES),
        cost_estimate=pl.CostEstimate(
            flops=12 * field.size * matrix.shape[0], bytes_accessed=8 * field.size, transcendentals=0
        ),
        name="mode_kinetic",
    )(field.reshape(peers, held, rows, width), matrix)
    return out.reshape(field.shape)


def join_kernel(starts, sum_count, at_ref, work_ref, cor_ref, near_ref, *refs):
    pieces = len(starts)
    first_refs, second_refs = refs[:pieces], refs[pieces : 2 * pieces]
    sum_refs = refs[2 * pieces : 2 * pieces + sum_count]
    out_ref = refs[-1]
    span = near_ref.shape[1]
    even = lax.rem(at_ref[0], 2) == 0
    for start, first_ref, second_ref in zip(starts, first_refs, second_refs):
        place = slice(start, start + first_ref.shape[1])
        for at in range(0, work_ref.shape[2], span):
            part = slice(at, at + span)
            total = work_ref[0, place, part]
            for sum_ref in sum_refs:
                total = total + sum_ref[0, place, part]
            twist_fn = cor_ref[place, part]
            if_even = jnp.where(even, twist_fn, 1.0)
            if_odd = jnp.where(even, 1.0, twist_fn)
            total = total + if_even * precise_dot(
                if_odd * first_ref[0, :, part], near_ref[0]
            )
            out_ref[0, place, part] = total + if_odd * precise_dot(
                if_even * second_ref[0, :, part], near_ref[1]
            )


def join_terms(at, work, cor, near, starts, first, second, sums):
    nvec, rows, width = work.shape
    one = pl.BlockSpec((1, rows, width), lambda i: (i, 0, 0))
    pieces = [pl.BlockSpec((1, b.shape[1], width), lambda i: (i, 0, 0)) for b in first]
    return pl.pallas_call(
        functools.partial(join_kernel, tuple(starts), len(sums)),
        grid=(nvec,),
        in_specs=[
            pl.BlockSpec(memory_space=pltpu.SMEM), one, whole_spec(cor.shape), whole_spec(near.shape)
        ]
        + pieces
        + pieces
        + [one] * len(sums),
        out_specs=one,
        out_shape=jax.ShapeDtypeStruct(work.shape, jnp.float32),
        compiler_params=pltpu.CompilerParams(vmem_limit_bytes=VMEM_BYTES),
        cost_estimate=pl.CostEstimate(
            flops=24 * work.size * near.shape[1], bytes_accessed=24 * work.size, transcendentals=0
        ),
        name="join_terms",
    )(at, work, cor, near, *first, *second, *sums)


def far_terms_kernel(
    nvec, start, coef_ref, work_ref, first_ref, second_ref, fn_ref, vec_ref, before_ref, out_ref,
    sum_ref, sums,
):
    del work_ref
    step = pl.program_id(0)
    _, block_rows, width = first_ref.shape

    @pl.when(step == 0)
    def _():
        sums[...] = jnp.zeros_like(sums)

    at = pl.multiple_of(start + step * block_rows, SUBLANES)
    places = []
    for rows_here, lanes in tiles(block_rows, width):
        place = (pl.ds(at + rows_here.start, SUBLANES), lanes)
        places.append(place)
        skip_fn = fn_ref[place]
        first_fn = coef_ref[0] * skip_fn
        second_fn = coef_ref[1] * skip_fn
        for i in range(nvec):
            out_ref[(i, *place)] = (
                out_ref[(i, *place)]
                + first_fn * first_ref[i, rows_here, lanes]
                + second_fn * second_ref[i, rows_here, lanes]
            )
    add_products(nvec, vec_ref, out_ref, sums, 0, places, False)
    add_products(nvec, out_ref, out_ref, sums, 1, places, True)

    @pl.when(step == pl.num_programs(0) - 1)
    def _():
        lane = lax.broadcasted_iota(jnp.int32, (nvec, LANES), 1)
        packed = before_ref[...]
        packed = packed + packed_columns(lambda i, j: sums[0, j * nvec + i], nvec, 0, lane)
        packed = packed + packed_columns(
            lambda i, j: sums[1, min(i, j) * nvec + max(i, j)], nvec, nvec, lane
        )
        sum_ref[...] = jnp.broadcast_to(packed[None], sum_ref.shape)


def far_terms(coef, work, first, second, skip_fn, vec, before, start, block_rows, copies):
    nvec, _, width = work.shape
    rows = first.shape[1]
    whole = pl.BlockSpec(memory_space=pltpu.VMEM)
    block = pl.BlockSpec((nvec, block_rows, width), lambda s: (0, s, 0))
    work, skip_fn, vec = (
        pltpu.with_memory_space_constraint(array, pltpu.VMEM) for array in (work, skip_fn, vec)
    )
    return pl.pallas_call(
        functools.partial(far_terms_kernel, nvec, start),
        grid=(rows // block_rows,),
        in_specs=[
            pl.BlockSpec(memory_space=pltpu.SMEM), whole, block, block, whole, whole, whole
        ],
        out_specs=[whole, whole],
        out_shape=[
            jax.ShapeDtypeStruct(work.shape, jnp.float32),
            jax.ShapeDtypeStruct((copies, nvec, LANES), jnp.float32),
        ],
        scratch_shapes=[pltpu.VMEM((2, nvec * nvec, SUBLANES, LANES), jnp.float32)],
        input_output_aliases={1: 0},
        compiler_params=pltpu.CompilerParams(vmem_limit_bytes=SMALL_VMEM_BYTES),
        cost_estimate=pl.CostEstimate(
            flops=3 * nvec * nvec * rows * width,
            bytes_accessed=20 * first.size,
            transcendentals=0,
        ),
        name="far_terms",
    )(coef, work, first, second, skip_fn, vec, before)


def across(column, row):
    return jnp.broadcast_to(column[row : row + 1, :], (SUBLANES, LANES))


def spread_columns(matrix, start, count):
    return [
        jnp.broadcast_to(matrix[:, k : k + 1], (count, LANES)) for k in range(start, start + count)
    ]


def spread_dot(left, right):
    count = len(left)
    columns = []
    for column in right:
        terms = [left[m] * jnp.broadcast_to(column[m : m + 1, :], left[m].shape) for m in range(count)]
        while len(terms) > 1:
            terms = [sum(terms[k + 1 : k + 2], terms[k]) for k in range(0, len(terms), 2)]
        columns.append(terms[0])
    return columns


def small_algebra(nvec, count, packed):
    packed = packed * (1.0 / count)
    cross = spread_columns(packed.T[0:nvec, :], 0, nvec)
    cross_turned = spread_columns(packed, 0, nvec)
    gram = spread_columns(packed, nvec, nvec)
    vec_gram = spread_columns(packed, 2 * nvec, nvec)
    total = [2.0 * c - d for c, d in zip(cross, spread_dot(vec_gram, cross))]
    total_turned = [2.0 * c - d for c, d in zip(cross_turned, spread_dot(cross_turned, vec_gram))]
    inner = [d - c for c, d in zip(cross, spread_dot(vec_gram, total))]
    gram = [
        g - one + other
        for g, one, other in zip(
            gram, spread_dot(cross_turned, total), spread_dot(total_turned, inner)
        )
    ]
    row = lax.broadcasted_iota(jnp.int32, (nvec, LANES), 0)
    inverse = [jnp.where(row == k, 1.0, 0.0) for k in range(nvec)]
    lower = []
    for at in range(nvec):
        pivot = jnp.broadcast_to(gram[at][at : at + 1, :], (nvec, LANES))
        scale = lax.rsqrt(pivot)
        scale = scale * (1.5 - 0.5 * pivot * scale * scale)
        scaled = gram[at] * scale
        lower.append(jnp.where(row >= at, scaled, 0.0))
        factor = jnp.where(row > at, scaled, 0.0)
        for k in range(at + 1, nvec):
            here = jnp.broadcast_to(gram[k][at : at + 1, :], (nvec, LANES)) * scale
            gram[k] = gram[k] - factor * here
        for k in range(at + 1):
            here = jnp.broadcast_to(inverse[k][at : at + 1, :], (nvec, LANES)) * scale
            inverse[k] = jnp.where(row == at, here, inverse[k] - factor * here)
    mixing = [-column for column in spread_dot(inverse, total_turned)]
    return total, lower, inverse, mixing


def gathered_columns(columns):
    lane = lax.broadcasted_iota(jnp.int32, columns[0].shape, 1)
    matrix = jnp.zeros_like(columns[0])
    for k, column in enumerate(columns):
        matrix = jnp.where(lane == k, column, matrix)
    return matrix[:, : len(columns)]


def basis_kernel(
    nvec, count, block_rows, sum_ref, work_ref, vec_ref, out_ref, alpha_ref, lower_ref, coefs, held, sems
):
    packed = sum_ref[0]
    for other in range(1, sum_ref.shape[0]):
        packed = packed + sum_ref[other]
    total, lower, inverse, mixing = small_algebra(nvec, count, packed)
    for number, columns in enumerate((inverse, mixing)):
        for j in range(nvec):
            for i in range(nvec):
                if number == 1 or j <= i:
                    coefs[number, i * nvec + j] = across(columns[j], i)
    alpha_ref[...] = gathered_columns(total)
    lower_ref[...] = gathered_columns(lower)
    rows, width = held.shape[1:]
    blocks = rows // block_rows

    def copy_out(step):
        place = pl.ds(pl.multiple_of(step * block_rows, block_rows), block_rows)
        return pltpu.make_async_copy(held.at[:, place], out_ref.at[:, place], sems.at[step])

    def some_rows(step, _):
        start = pl.multiple_of(step * block_rows, block_rows)
        places = [
            (pl.ds(start + place.start, SUBLANES), lanes)
            for place, lanes in tiles(block_rows, width)
        ]
        for at in range(0, len(places), 4):
            group = places[at : at + 4]
            totals = {}
            for number, ref in ((1, vec_ref), (0, work_ref)):
                for j in range(nvec):
                    values = [ref[(j, *place)] for place in group]
                    for i in range(nvec):
                        if number == 0 and j > i:
                            continue
                        coef = coefs[number, i * nvec + j]
                        for spot, value in enumerate(values):
                            term = coef * value
                            here = (i, spot)
                            totals[here] = totals[here] + term if here in totals else term
            for (i, spot), value in totals.items():
                held[(i, *group[spot])] = value
        copy_out(step).start()
        return 0

    lax.fori_loop(0, blocks, some_rows, 0)
    for step in range(blocks):
        copy_out(step).wait()


def basis_of(count, sums, work, vec, block_rows):
    nvec, rows, width = work.shape
    small = jax.ShapeDtypeStruct((nvec, nvec), jnp.float32)
    whole = pl.BlockSpec(memory_space=pltpu.VMEM)
    work, vec = (pltpu.with_memory_space_constraint(array, pltpu.VMEM) for array in (work, vec))
    return pl.pallas_call(
        functools.partial(basis_kernel, nvec, count, block_rows),
        in_specs=[whole, whole, whole],
        out_specs=[pl.BlockSpec(memory_space=pl.ANY), whole, whole],
        out_shape=[jax.ShapeDtypeStruct(work.shape, jnp.float32), small, small],
        scratch_shapes=[
            pltpu.VMEM((2, nvec * nvec, SUBLANES, LANES), jnp.float32),
            pltpu.VMEM(work.shape, jnp.float32),
            pltpu.SemaphoreType.DMA((rows // block_rows,)),
        ],
        compiler_params=pltpu.CompilerParams(vmem_limit_bytes=SMALL_VMEM_BYTES),
        cost_estimate=pl.CostEstimate(
            flops=4 * nvec * work.size, bytes_accessed=12 * work.size, transcendentals=0
        ),
        name="basis",
    )(sums, work, vec)


def shards(
    vectors,
    previous,
    beta,
    potential,
    coriolis_fn,
    second_fn,
    rot_const,
    coupling,
    kin_one,
    kin_two,
    kin_three,
    kin_four,
    kin_five,
    kin_six,
    coriolis_derivative,
):
    _, nvec, *points, width = vectors.shape
    rows = points[0] * points[1] * points[2]
    devices = lax.axis_size(ALL_AXES)
    block_index = lax.axis_index("ka")
    nblocks = lax.axis_size("ka")
    row_peers = lax.axis_size("row")
    mode_peers = lax.axis_size("mode")
    row_at = lax.axis_index("row")
    current = vectors.reshape(nvec, rows, width)
    older = previous.reshape(nvec, rows, width)
    block_rows = min(32, rows // 2)

    cut = rows * 3 // 4 // block_rows * block_rows or rows // 2
    starts, stops = [0, cut], [cut, rows]
    parts = [split_rows(current, start, stop) for start, stop in zip(starts, stops)]
    near_first = [pair_exchange(part, "ka", 0) for part in parts]
    near_second = [pair_exchange(part, "ka", 1) for part in parts]
    at = jnp.stack([block_index, row_at, row_at ^ 1]).astype(jnp.int32)
    group = 2 - row_peers % 2
    held = [current]
    if group == 2:
        held.append(lax.ppermute(current, "row", [(i, i ^ 1) for i in range(row_peers)]))
    away = row_peers // group - 1
    row_parts = crossing(tuple(points), at, kin_two, held, away) if away else []
    row_sums = [
        lax.ppermute(
            part, "row", [(i, (i + group * (number + 1)) % row_peers) for i in range(row_peers)]
        )
        for number, part in enumerate(row_parts)
    ]

    span = next((s for s in (256, 128) if width % s == 0 and s % kin_six.shape[0] == 0), width)
    left, mode_mat, tail, near = operators(
        tuple(points),
        group,
        mode_peers * rows,
        width,
        span,
        at,
        coupling,
        (kin_one, kin_two, kin_three, kin_four, kin_five, kin_six, coriolis_derivative),
        row_parts,
    )
    near_first[0] = handed_on(near_first[0], HOP_WEIGHT, [*row_parts, mode_mat])
    near_second[0] = handed_on(near_second[0], HOP_WEIGHT, [*row_parts, mode_mat])
    far_first = [pair_exchange(part, "ka", 0) for part in near_second]
    far_second = [pair_exchange(part, "ka", 1) for part in near_first]
    lower_two = jnp.maximum(block_index - 2, 0)
    far_above, far_below = coupling[1, block_index], coupling[1, lower_two]
    even = block_index % 2 == 0
    far_pair = jnp.stack(
        [jnp.where(even, far_above, far_below), jnp.where(even, far_below, far_above)]
    )
    sums, vec, skip_fn = resident(
        current, second_fn.reshape(rows, width), held[1:], block_rows
    )
    mode_shares = lax.all_to_all(vec, "mode", split_axis=0, concat_axis=0, tiled=True)
    mode_shares = mode_kinetic(mode_shares, mode_mat, mode_peers)
    mode_sum = lax.all_to_all(mode_shares, "mode", split_axis=0, concat_axis=0, tiled=True)
    work = local_terms(
        nblocks, at, rot_const, beta, held, older, potential.reshape(rows, width), left, tail
    )
    work = join_terms(
        at,
        work,
        coriolis_fn.reshape(rows, width),
        near,
        starts,
        near_first,
        near_second,
        [mode_sum, *row_sums],
    )
    for number, start in enumerate(starts):
        work, copied = far_terms(
            far_pair,
            work,
            far_first[number],
            far_second[number],
            skip_fn,
            vec,
            sums,
            start,
            block_rows if number < len(starts) - 1 else stops[number] - start,
            devices if number == len(starts) - 1 else 1,
        )
        sums = copied[0]
    every_sum = lax.all_to_all(copied, ALL_AXES, split_axis=0, concat_axis=0, tiled=True)
    count = float(devices * rows * width)
    basis, alpha, lower = basis_of(count, every_sum, work, vec, block_rows)
    return (basis.reshape(vectors.shape), alpha, lower)


def solution(mesh):
    return jax.shard_map(
        shards,
        mesh=mesh,
        in_specs=(
            P("ka", None, "mode", "row", None, None),
            P("ka", None, "mode", "row", None, None),
            P(),
            P("mode", "row", None, None),
            P("mode", "row", None, None),
            P("mode", "row", None, None),
            P(),
            P(),
            P(),
            P(),
            P(),
            P(),
            P(),
            P(),
            P(),
        ),
        out_specs=(P("ka", None, "mode", "row", None, None), P(), P()),
        check_vma=False,
    )
```
